32 devices in a mesh: lat: 8 (over z, x), lon: 4 (over y, core).
Axes of the slice: x: 2, y: 2, z: 4, core: 2. Of those that a mesh axis runs over, the one named last changes fastest.
Arguments:
- fields: float32 [4, 12, 16, 256, 128], P(None, None, 'lat', 'lon'), may hold values from -36 to 36
- weight_one: float32 [3, 3, 128, 128], replicated, may hold values from -0.1875 to 0.1875
- bias_one: float32 [128], replicated, may hold values from -3 to 3
- gain_one: float32 [128], replicated, may hold values from 0.25 to 1.75
- shift_one: float32 [128], replicated, may hold values from -3 to 3
- weight_two: float32 [3, 3, 128, 128], replicated, may hold values from -0.1875 to 0.1875
- bias_two: float32 [128], replicated, may hold values from -3 to 3
- gain_two: float32 [128], replicated, may hold values from 0.25 to 1.75
- shift_two: float32 [128], replicated, may hold values from -3 to 3
- cotangent: float32 [4, 12, 16, 256, 128], P(None, None, 'lat', 'lon'), may hold values from -6 to 6
Outputs:
- output: float32 [4, 12, 16, 256, 128], P(None, None, 'lat', 'lon')
- grad_fields: float32 [4, 12, 16, 256, 128], P(None, None, 'lat', 'lon')
- grad_weight_one: float32 [3, 3, 128, 128], replicated
- grad_bias_one: float32 [128], replicated
- grad_gain_one: float32 [128], replicated
- grad_shift_one: float32 [128], replicated
- grad_weight_two: float32 [3, 3, 128, 128], replicated
- grad_bias_two: float32 [128], replicated
- grad_gain_two: float32 [128], replicated
- grad_shift_two: float32 [128], replicated
The draws below stay inside these ranges and needn't reach their ends.
All inputs are finite; a program needn't handle non-finite values.
Results may differ from the reference program's by a relative error of at most 0.0003.
Values sent between devices are 32-bit elements; how exact they have to be, the bound alone decides.
No kernel may reach another device: no remote copies, remote signals or barrier semaphores. Data moves between devices by JAX's collectives and lax.ppermute only.
A program may use at most 192 MiB of HBM per device.

```python
import math
import jax
import jax.numpy as jnp
from jax import lax

C = 128
BATCH = 12
MB = 4
NLAT = 16
NLON = 256


def draw_fields(key, part):
    key = jax.random.fold_in(key, 11)
    noise_key, chan_key = jax.random.split(key)
    shape = (MB, BATCH, NLAT, NLON, C)
    base = jax.random.truncated_normal(noise_key, -4.0, 4.0, shape, jnp.float32)
    lat_pos = jnp.arange(NLAT, dtype=jnp.float32) / max(NLAT - 1, 1)
    lat_scale = 1.0 + 2.0 * lat_pos
    chan_scale = jnp.exp(jax.random.uniform(chan_key, (C,), jnp.float32, math.log(0.3), math.log(3.0)))
    return base * lat_scale[:, None, None] * chan_scale


def draw_cotangent(key, part):
    key = jax.random.fold_in(key, 23)
    noise_key, offset_key, offset_sign_key, slope_key, slope_sign_key = jax.random.split(key, 5)
    shape = (MB, BATCH, NLAT, NLON, C)
    base = jax.random.truncated_normal(noise_key, -4.0, 4.0, shape, jnp.float32)
    offset_sign = 2.0 * jax.random.randint(offset_sign_key, (MB, C), 0, 2).astype(jnp.float32) - 1.0
    slope_sign = 2.0 * jax.random.randint(slope_sign_key, (MB, C), 0, 2).astype(jnp.float32) - 1.0
    offset = jax.random.uniform(offset_key, (MB, C), jnp.float32, 0.5, 1.0) * offset_sign
    slope = jax.random.uniform(slope_key, (MB, C), jnp.float32, 1.0, 2.0) * slope_sign
    lat_pos = jnp.arange(NLAT, dtype=jnp.float32) / max(NLAT - 1, 1) - 0.5
    trend = offset[:, None, None, None, :] + slope[:, None, None, None, :] * lat_pos[None, None, :, None, None]
    return base + trend


def noise(stream_key, dims, deviation, bound, held_as=jnp.bfloat16):
    array = deviation * jax.random.normal(stream_key, dims, jnp.float32)
    return jnp.clip(array, min=-bound, max=bound).astype(held_as)


def setup_inputs(seed: int = 0) -> dict:
    key_list = jax.random.split(jax.random.key(seed), 11)
    fields = draw_fields(jax.random.fold_in(key_list[10], 71), 0)
    weight_one = noise(key_list[1], (3, 3, C, C), (9 * C) ** -0.5, 0.1875, jnp.float32)
    bias_one = noise(key_list[2], (C,), 0.5, 3.0, jnp.float32)
    gain_one = jnp.clip(1.0 + 0.15 * jax.random.normal(key_list[3], (C,), jnp.float32), 0.25, 1.75)
    shift_one = noise(key_list[4], (C,), 0.5, 3.0, jnp.float32)
    weight_two = noise(key_list[5], (3, 3, C, C), (9 * C) ** -0.5, 0.1875, jnp.float32)
    bias_two = noise(key_list[6], (C,), 0.5, 3.0, jnp.float32)
    gain_two = jnp.clip(1.0 + 0.15 * jax.random.normal(key_list[7], (C,), jnp.float32), 0.25, 1.75)
    shift_two = noise(key_list[8], (C,), 0.5, 3.0, jnp.float32)
    cotangent = draw_cotangent(jax.random.fold_in(key_list[10], 71), 0)
    return dict(fields=fields, weight_one=weight_one, bias_one=bias_one, gain_one=gain_one, shift_one=shift_one, weight_two=weight_two, bias_two=bias_two, gain_two=gain_two, shift_two=shift_two, cotangent=cotangent)


@jax.custom_vjp
def low(v):
    return lax.optimization_barrier(v.astype(jnp.bfloat16)).astype(jnp.float32)

@jax.custom_vjp
def low_back(v):
    return v

def low_keep(v):
    return (low(v), None)

def low_pass(kept, grad):
    return (grad,)

def back_keep(v):
    return (v, None)

def back_low(kept, grad):
    return (low(grad),)
low.defvjp(low_keep, low_pass)
low_back.defvjp(back_keep, back_low)

def padded(values):
    wrapped = jnp.concatenate([values[:, :, -1:], values, values[:, :, :1]], axis=2)
    return jnp.pad(wrapped, ((0, 0), (1, 1), (0, 0), (0, 0)))

def convolve(values, kernel):
    return lax.conv_general_dilated(padded(values), kernel, (1, 1), 'VALID', dimension_numbers=('NHWC', 'HWIO', 'NHWC'), precision=lax.Precision.HIGHEST)

def normalize(active, gain, shift):
    center = lax.optimization_barrier(jnp.mean(active, axis=(0, 1, 2)))
    spread = lax.optimization_barrier(jnp.mean((active - center) ** 2, axis=(0, 1, 2)))
    return gain * (active - center) * lax.rsqrt(spread + 1e-05) + shift

def forward(fields, weight_one, bias_one, gain_one, shift_one, weight_two, bias_two, gain_two, shift_two):
    results = []
    for batch_index in range(MB):
        inputs = fields[batch_index]
        hidden = normalize(jax.nn.silu(convolve(inputs, weight_one) + bias_one), gain_one, shift_one)
        branch = normalize(jax.nn.silu(convolve(hidden, weight_two) + bias_two), gain_two, shift_two)
        results.append(inputs + branch)
    return jnp.stack(results)

def reference(fields, weight_one, bias_one, gain_one, shift_one, weight_two, bias_two, gain_two, shift_two, cotangent):
    output, backward = jax.vjp(forward, fields, weight_one, bias_one, gain_one, shift_one, weight_two, bias_two, gain_two, shift_two)
    grads = backward(cotangent)
    return (output, grads[0], grads[1], grads[2], grads[3], grads[4], grads[5], grads[6], grads[7], grads[8])
```

```python
import functools

import jax
import jax.numpy as jnp
from jax import lax
from jax.experimental import pallas as pl
from jax.experimental.pallas import tpu as pltpu
from jax.sharding import PartitionSpec as P


EPSILON = 1e-05
F32 = jnp.float32
BF16 = jnp.bfloat16
AXES = ("lat", "lon")
STEP = 2
VMEM_LIMIT = 48 << 20


def permute(value, target):
    rows, cols = lax.axis_size("lat"), lax.axis_size("lon")
    pairs = []
    for row in range(rows):
        for col in range(cols):
            to = target(row, col)
            if 0 <= to[0] < rows and 0 <= to[1] < cols:
                pairs.append((row * cols + col, to[0] * cols + to[1]))
    return lax.ppermute(value, AXES, pairs)


def to_core(row, col):
    return row, col ^ 1


def to_side(row, col):
    return row ^ 1, col


def to_cross(row, col):
    return row ^ 1, col ^ 1


def to_east(row, col):
    return row, col ^ 2


def to_pair(row, col):
    return row ^ 2, col


def to_next(row, col):
    return (row + 2 if (row // 2) % 2 else row - 2), col


def group_steps():
    steps = []
    bit = 2
    while bit < lax.axis_size("lon"):
        steps.append(functools.partial(lambda bit, row, col: (row, col ^ bit), bit))
        bit *= 2
    bit = 2
    while bit < lax.axis_size("lat"):
        steps.append(functools.partial(lambda bit, row, col: (row ^ bit, col), bit))
        bit *= 2
    return steps


def exchange_rows(pair_row, next_row):
    return permute(pair_row, to_pair), permute(next_row, to_next)


def split(value):
    high = value.astype(BF16)
    return high, (value - high.astype(F32)).astype(BF16)


def sigmoid(value):
    return 1.0 / (1.0 + jnp.exp(-value))


def cost(flops, moved):
    return pl.CostEstimate(flops=int(flops), bytes_accessed=int(moved), transcendentals=0)


def call(body, grid, scalars, inputs, outputs, scratch, name, flops=0.0):
    moved = sum(a.size * a.dtype.itemsize for a, _, _ in inputs)
    moved += sum(4 * functools.reduce(lambda x, y: x * y, o[0], 1) for o in outputs)
    return pl.pallas_call(
        body,
        grid_spec=pltpu.PrefetchScalarGridSpec(
            num_scalar_prefetch=1,
            grid=(grid,),
            in_specs=[pl.BlockSpec(block, index) for _, block, index in inputs],
            out_specs=[pl.BlockSpec(o[2], o[3]) for o in outputs],
            scratch_shapes=scratch,
        ),
        out_shape=[jax.ShapeDtypeStruct(o[0], o[1]) for o in outputs],
        compiler_params=pltpu.CompilerParams(vmem_limit_bytes=VMEM_LIMIT),
        cost_estimate=cost(flops, moved),
        name=name,
    )(scalars, *[a for a, _, _ in inputs])


def by_sample(array, step=STEP):
    rest = (0,) * (array.ndim - 1)
    return array, (step,) + array.shape[1:], lambda i, s: (i,) + rest


def whole(array):
    rest = (0,) * array.ndim
    return array, array.shape, lambda i, s: rest


def out_by_sample(shape, step=STEP):
    rest = (0,) * (len(shape) - 1)
    return shape, F32, (step,) + shape[1:], lambda i, s: (i,) + rest


def out_whole(shape):
    rest = (0,) * len(shape)
    return shape, F32, shape, lambda i, s: rest


def pack_kernel(s_ref, to_side, to_cross, to_core, side_edge, cross_edge, core, side_inner, cross_inner):
    lx = s_ref[0]
    side_edge[...] = to_side[0, :, lx]
    cross_edge[...] = to_cross[0, :, lx]
    core[...] = to_core[0]
    side_inner[...] = to_side[0, :, 1 - lx]
    cross_inner[...] = to_cross[0, :, 1 - lx]


def pack(scalars, field, name):
    _, _, batch, rows, cols, chans = field.shape
    flat = field.reshape((-1,) + field.shape[2:])
    step = batch // 2
    block = (1, step, rows, cols, chans)
    one = (batch, cols, chans)
    return call(
        pack_kernel,
        batch // step,
        scalars,
        [
            (flat, block, lambda i, s: (2 * (1 - s[0]) + s[1], i, 0, 0, 0)),
            (flat, block, lambda i, s: (2 * (1 - s[0]) + 1 - s[1], i, 0, 0, 0)),
            (flat, block, lambda i, s: (2 * s[0] + 1 - s[1], i, 0, 0, 0)),
        ],
        [out_by_sample(shape, step) for shape in (one, one, (batch, rows, cols, chans), one, one)],
        [],
        name,
    )


def join_kernel(edge, s_ref, home, core, side, cross, rows_ref, tile_ref):
    lx, nc = s_ref[0], s_ref[1]
    half = home.shape[3]
    here = pl.ds(pl.multiple_of(nc * half, half), half)
    there = pl.ds(pl.multiple_of((1 - nc) * half, half), half)
    rows_ref[:, lx, here, :] = home[0, :, 0]
    rows_ref[:, lx, there, :] = core[:, 0]
    rows_ref[:, 1 - lx, here, :] = side[...]
    rows_ref[:, 1 - lx, there, :] = cross[...]
    wide = 2 * half
    tile_ref[...] = jnp.concatenate([rows_ref[:, :, 0:4, :], rows_ref[:, :, wide - 4 : wide, :]], axis=2)


def join(scalars, field, core, side, cross, edge, name):
    _, _, batch, rows, cols, chans = field.shape
    flat = field.reshape((-1,) + field.shape[2:])

    def row_of(s):
        return s[0] if edge else 1 - s[0]

    step = batch // 2
    return call(
        functools.partial(join_kernel, edge),
        batch // step,
        scalars,
        [
            (flat, (1, step, 1, cols, chans), lambda i, s: (2 * s[0] + s[1], i, row_of(s), 0, 0)),
            (core, (step, 1, cols, chans), lambda i, s: (i, row_of(s), 0, 0)),
            by_sample(side, step),
            by_sample(cross, step),
        ],
        [out_by_sample((batch, 2, 2 * cols, chans), step), out_by_sample((batch, 2, 8, chans), step)],
        [],
        name,
    )


def edges_kernel(s_ref, pair, pair_tile, following, following_tile, pair_out, next_out):
    wide = pair.shape[2]
    pair_out[:, 0:wide, :] = pair[:, 0]
    pair_out[:, wide : wide + 8, :] = pair_tile[:, 0]
    next_out[:, 0:wide, :] = following[:, 0]
    next_out[:, wide : wide + 8, :] = following_tile[:, 0]


def edges(scalars, rows, tile, name):
    batch, _, wide, chans = rows.shape
    step = batch // 2
    shape = (batch, wide + 8, chans)
    return call(
        edges_kernel,
        batch // step,
        scalars,
        [
            (rows, (step, 1, wide, chans), lambda i, s: (i, 1 - s[2], 0, 0)),
            (tile, (step, 1, 8, chans), lambda i, s: (i, 1 - s[2], 0, 0)),
            (rows, (step, 1, wide, chans), lambda i, s: (i, s[2], 0, 0)),
            (tile, (step, 1, 8, chans), lambda i, s: (i, s[2], 0, 0)),
        ],
        [out_by_sample(shape, step), out_by_sample(shape, step)],
        [],
        name,
    )


def gather(scalars, field, name):
    side_edge, cross_edge, core, side_inner, cross_inner = pack(scalars, field, name + "_pack")
    side_edge = permute(side_edge, to_side)
    cross_edge = permute(cross_edge, to_cross)
    core = permute(core, to_core)
    side_inner = permute(side_inner, to_side)
    cross_inner = permute(cross_inner, to_cross)
    edge, tile = join(scalars, field, core, side_edge, cross_edge, True, name + "_edge")
    edge_tile = permute(tile, to_east)
    halos = exchange_rows(*edges(scalars, edge, edge_tile, name + "_halo"))
    inner, tile = join(scalars, field, core, side_inner, cross_inner, False, name + "_inner")
    inner_tile = permute(tile, to_east)
    return (edge, edge_tile, inner, inner_tile), halos


def row_of_parts(parts, row):
    edge, edge_tile, inner, inner_tile = parts
    rows, tiles = (edge, edge_tile) if row in (0, 3) else (inner, inner_tile)
    slot = 0 if row < 2 else 1
    return rows[:, slot], tiles[:, slot]


def ring_row(values, pad, row, high, low):
    step, wide, chans = values.shape
    pad[row, :, 8 : 8 + wide, :] = values
    pad[row, :, 0:8, :] = values[:, wide - 8 : wide]
    pad[row, :, 8 + wide : 16 + wide, :] = values[:, 0:8]
    for tap in range(3):
        shifted = values if tap == 1 else pad[row, :, 7 + tap : 7 + tap + wide, :]
        at = (row * 3 + tap) * chans
        high[:, at : at + chans], low[:, at : at + chans] = split(shifted.reshape(step * wide, chans))


def pair_of_rows(pair, high, low, weight_high, weight_low):
    chans = weight_high.shape[1] // 2
    at = slice(pair * 6 * chans, (pair * 6 + 12) * chans)
    total = jnp.dot(high[:, at], weight_high[...], preferred_element_type=F32)
    total += jnp.dot(low[:, at], weight_high[...], preferred_element_type=F32)
    total += jnp.dot(high[:, at], weight_low[...], preferred_element_type=F32)
    return total[:, :chans], total[:, chans:]


def north_south(s_ref, pair, following):
    odd = s_ref[2] == 1
    first, second = pair[...], following[...]
    return jnp.where(odd, first, second), jnp.where(odd, second, first)


def put_edges(s_ref, top, bottom, pair_out, next_out):
    odd = s_ref[2] == 1
    pair_out[...] = jnp.where(odd, top, bottom)
    next_out[...] = jnp.where(odd, bottom, top)


def lanes(values):
    return jnp.sum(values.reshape(-1, 8, values.shape[-1]), axis=0)


def fold(total):
    return jnp.sum(total, axis=0, keepdims=True)


def add_moments(active, first, shift, sums, others):
    @pl.when(first)
    def _():
        mean = jnp.mean(active[0].reshape(-1, active[0].shape[-1]), axis=0, keepdims=True)
        shift[...] = jnp.broadcast_to(mean, shift.shape)
        sums[...] = jnp.zeros_like(sums)

    base = shift[0:1, :]
    for at, values in enumerate(active):
        distance = values - base
        sums[0] += lanes(distance)
        sums[1] += lanes(distance * distance)
        if others is not None:
            sums[2] += lanes(others[at])
            sums[3] += lanes(others[at] * distance)


def put_moments(out_ref, shift, sums, count, others):
    total, squares = fold(sums[0]), fold(sums[1])
    offset = total / count
    out_ref[...] = jnp.zeros_like(out_ref)
    out_ref[0:1, :] = shift[0:1, :] + offset
    out_ref[1:2, :] = squares - total * offset
    if others:
        weight = fold(sums[2])
        out_ref[2:3, :] = weight
        out_ref[3:4, :] = fold(sums[3]) - weight * offset


def conv_scratch(wide, chans):
    return [
        pltpu.VMEM((6, STEP, wide + 16, chans), F32),
        pltpu.VMEM((STEP * wide, 18 * chans), BF16),
        pltpu.VMEM((STEP * wide, 18 * chans), BF16),
    ]


def first_kernel(
    count, s_ref, edge, edge_tile, inner, inner_tile, pair, following, weight_high, weight_low, bias,
    z_ref, pair_out, next_out, six_ref, stat_ref, pad, high, low, shift, sums,
):
    step = pl.program_id(0)
    own = edge.shape[2]
    wide = own + 8
    north, south = north_south(s_ref, pair, following)
    parts = (edge, edge_tile, inner, inner_tile)
    for row in range(6):
        if row in (0, 5):
            values = north if row == 0 else south
        else:
            values = jnp.concatenate(row_of_parts(parts, row - 1), axis=1)
        six_ref[:, row] = values
        ring_row(values, pad, row, high, low)
    active = []
    rows = []
    for two in range(2):
        for total in pair_of_rows(two, high, low, weight_high, weight_low):
            z = (total + bias[0:1, :]).reshape(-1, wide, total.shape[-1])
            z_ref[:, len(rows)] = z
            rows.append(z)
            active.append(z[:, :own] * sigmoid(z[:, :own]))
    put_edges(s_ref, rows[0], rows[3], pair_out, next_out)
    add_moments(active, step == 0, shift, sums, None)

    @pl.when(step == pl.num_programs(0) - 1)
    def _():
        put_moments(stat_ref, shift, sums, count, False)


def first_conv(scalars, parts, halos, weight, bias):
    batch, _, own, chans = parts[0].shape
    wide = own + 8
    return call(
        functools.partial(first_kernel, float(batch * 4 * own)),
        batch // STEP,
        scalars,
        [by_sample(a) for a in parts + halos] + [whole(a) for a in weight + (bias,)],
        [
            out_by_sample((batch, 4, wide, chans)),
            out_by_sample((batch, wide, chans)),
            out_by_sample((batch, wide, chans)),
            out_by_sample((batch, 6, wide, chans)),
            out_whole((8, chans)),
        ],
        conv_scratch(wide, chans) + [pltpu.VMEM((8, chans), F32), pltpu.VMEM((4, 8, chans), F32)],
        "conv_one",
        1.2e10,
    )


def second_kernel(
    count, s_ref, z1, pair, following, g_edge, g_inner, coef, weight_high, weight_low, bias,
    z_ref, pair_out, next_out, six_ref, stat_ref, pad, high, low, shift, sums,
):
    step = pl.program_id(0)
    own = g_edge.shape[2]
    wide = own + 8
    center, scale, offset = coef[0:1, :], coef[1:2, :], coef[2:3, :]
    north, south = north_south(s_ref, pair, following)
    for row in range(6):
        values = north if row == 0 else south if row == 5 else z1[:, row - 1]
        hidden = (values * sigmoid(values) - center) * scale + offset
        if row in (0, 5):
            hidden = jnp.where(s_ref[3 if row == 0 else 4] == 1, 0.0, hidden)
        six_ref[:, row] = hidden
        ring_row(hidden, pad, row, high, low)
    active = []
    rows = []
    for two in range(2):
        for total in pair_of_rows(two, high, low, weight_high, weight_low):
            z = (total + bias[0:1, :]).reshape(-1, wide, total.shape[-1])
            z_ref[:, len(rows)] = z
            rows.append(z)
            active.append(z[:, :own] * sigmoid(z[:, :own]))
    put_edges(s_ref, rows[0], rows[3], pair_out, next_out)
    others = [g_edge[:, 0], g_inner[:, 0], g_inner[:, 1], g_edge[:, 1]]
    add_moments(active, step == 0, shift, sums, others)

    @pl.when(step == pl.num_programs(0) - 1)
    def _():
        put_moments(stat_ref, shift, sums, count, True)


def second_conv(scalars, z1, halos, g_parts, coef, weight, bias):
    batch, _, wide, chans = z1.shape
    own = wide - 8
    return call(
        functools.partial(second_kernel, float(batch * 4 * own)),
        batch // STEP,
        scalars,
        [by_sample(a) for a in (z1,) + halos + (g_parts[0], g_parts[2])]
        + [whole(a) for a in (coef,) + weight + (bias,)],
        [
            out_by_sample((batch, 4, wide, chans)),
            out_by_sample((batch, wide, chans)),
            out_by_sample((batch, wide, chans)),
            out_by_sample((batch, 6, wide, chans)),
            out_whole((8, chans)),
        ],
        conv_scratch(wide, chans) + [pltpu.VMEM((8, chans), F32), pltpu.VMEM((4, 8, chans), F32)],
        "conv_two",
        1.2e10,
    )


def put_pieces(s_ref, rows, pieces):
    lx, nc = s_ref[0], s_ref[1]
    half = rows.shape[2] // 2
    here = pl.ds(pl.multiple_of(nc * half, half), half)
    there = pl.ds(pl.multiple_of((1 - nc) * half, half), half)
    for row in range(2):
        pieces[0][:, row] = rows[2 * lx + row, :, here, :]
        pieces[1][:, row] = rows[2 * lx + row, :, there, :]
        pieces[2][:, row] = rows[2 - 2 * lx + row, :, here, :]
        pieces[3][:, row] = rows[2 - 2 * lx + row, :, there, :]


def output_kernel(s_ref, z2, six, coef, home, core, side, cross, rows):
    own = rows.shape[2]
    center, scale, offset = coef[0:1, :], coef[1:2, :], coef[2:3, :]
    for row in range(4):
        z = z2[:, row, :own]
        rows[row] = six[:, row + 1, :own] + ((z * sigmoid(z) - center) * scale + offset)
    put_pieces(s_ref, rows, (home, core, side, cross))


def output_pieces(scalars, z2, six, coef):
    batch, _, wide, chans = z2.shape
    own = wide - 8
    piece = (batch, 2, own // 2, chans)
    return call(
        output_kernel,
        batch // STEP,
        scalars,
        [by_sample(z2), by_sample(six), whole(coef)],
        [out_by_sample(piece)] * 4,
        [pltpu.VMEM((4, STEP, own, chans), F32)],
        "output",
    )


def send_home(pieces):
    home, core, side, cross = pieces
    side, cross = permute(side, to_side), permute(cross, to_cross)
    return home, permute(core, to_core), side, cross


def place_kernel(s_ref, home, core, side, cross, out):
    part = pl.program_id(0)
    for at, piece in enumerate((home, core, side, cross)):

        @pl.when(part == at)
        def _(piece=piece):
            out[0] = piece[...]


def place(scalars, pieces, name):
    shape = pieces[0].shape

    def to(i, s):
        return 2 * (s[0] ^ (i // 2)) + (s[1] ^ (i % 2)), 0, 0, 0, 0

    return call(
        place_kernel,
        4,
        scalars,
        [whole(a) for a in pieces],
        [((4,) + shape, F32, (1,) + shape, to)],
        [],
        name,
    )[0]


def silu_and_slope(z):
    sigma = sigmoid(z)
    return z * sigma, sigma * (1.0 + z * (1.0 - sigma))


def third_kernel(
    s_ref, z2, pair, following, g_edge, g_edge_tile, g_inner, g_inner_tile, g_pair, g_following, z1, coef,
    weight_high, weight_low, dh_ref, pair_out, next_out, dz_ref, stat_ref, pad, high, low, sums,
):
    step = pl.program_id(0)
    own = g_edge.shape[2]
    wide = own + 8
    center, inverse, scale = coef[0:1, :], coef[1:2, :], coef[2:3, :]
    mean_shift, mean_gain = coef[3:4, :], coef[4:5, :]
    center_one, inverse_one = coef[5:6, :], coef[6:7, :]

    @pl.when(step == 0)
    def _():
        sums[...] = jnp.zeros_like(sums)

    north, south = north_south(s_ref, pair, following)
    g_north, g_south = north_south(s_ref, g_pair, g_following)
    parts = (g_edge, g_edge_tile, g_inner, g_inner_tile)
    for row in range(6):
        if row in (0, 5):
            z, g = (north, g_north) if row == 0 else (south, g_south)
        else:
            z, g = z2[:, row - 1], jnp.concatenate(row_of_parts(parts, row - 1), axis=1)
        active, slope = silu_and_slope(z)
        normed = (active - center) * inverse
        dz = scale * (g - mean_shift - normed * mean_gain) * slope
        if row in (0, 5):
            dz = jnp.where(s_ref[3 if row == 0 else 4] == 1, 0.0, dz)
        else:
            dz_ref[:, row - 1] = dz[:, :own]
            sums[2] += lanes(dz[:, :own])
        ring_row(dz, pad, row, high, low)
    rows = []
    for two in range(2):
        for total in pair_of_rows(two, high, low, weight_high, weight_low):
            dh = total.reshape(-1, wide, total.shape[-1])
            row = len(rows)
            dh_ref[:, row] = dh
            rows.append(dh)
            z = z1[:, row, :own]
            sums[0] += lanes(dh[:, :own])
            sums[1] += lanes(dh[:, :own] * ((z * sigmoid(z) - center_one) * inverse_one))
    put_edges(s_ref, rows[0], rows[3], pair_out, next_out)

    @pl.when(step == pl.num_programs(0) - 1)
    def _():
        stat_ref[...] = jnp.zeros_like(stat_ref)
        for at in range(3):
            stat_ref[at : at + 1, :] = fold(sums[at])


def third_conv(scalars, z2, halos, g_parts, g_halos, z1, coef, weight):
    batch, _, wide, chans = z2.shape
    own = wide - 8
    return call(
        third_kernel,
        batch // STEP,
        scalars,
        [by_sample(a) for a in (z2,) + halos + g_parts + g_halos + (z1,)]
        + [whole(a) for a in (coef,) + weight],
        [
            out_by_sample((batch, 4, wide, chans)),
            out_by_sample((batch, wide, chans)),
            out_by_sample((batch, wide, chans)),
            out_by_sample((batch, 4, own, chans)),
            out_whole((8, chans)),
        ],
        conv_scratch(wide, chans) + [pltpu.VMEM((3, 8, chans), F32)],
        "conv_three",
        1.2e10,
    )


def fourth_kernel(
    s_ref, dh, pair, following, z1, z_pair, z_following, g_edge, g_inner, coef, weight_high, weight_low,
    home, core, side, cross, dz_ref, stat_ref, pad, high, low, sums, grads,
):
    step = pl.program_id(0)
    own = g_edge.shape[2]
    wide = own + 8
    center, inverse, scale = coef[0:1, :], coef[1:2, :], coef[2:3, :]
    mean_shift, mean_gain = coef[3:4, :], coef[4:5, :]

    @pl.when(step == 0)
    def _():
        sums[...] = jnp.zeros_like(sums)

    north, south = north_south(s_ref, pair, following)
    z_north, z_south = north_south(s_ref, z_pair, z_following)
    for row in range(6):
        if row in (0, 5):
            z, q = (z_north, north) if row == 0 else (z_south, south)
        else:
            z, q = z1[:, row - 1], dh[:, row - 1]
        active, slope = silu_and_slope(z)
        normed = (active - center) * inverse
        dz = scale * (q - mean_shift - normed * mean_gain) * slope
        if row in (0, 5):
            dz = jnp.where(s_ref[3 if row == 0 else 4] == 1, 0.0, dz)
        else:
            dz_ref[:, row - 1] = dz[:, :own]
            sums[0] += lanes(dz[:, :own])
        ring_row(dz, pad, row, high, low)
    others = [g_edge[:, 0], g_inner[:, 0], g_inner[:, 1], g_edge[:, 1]]
    row = 0
    for two in range(2):
        for total in pair_of_rows(two, high, low, weight_high, weight_low):
            grads[row] = others[row] + total.reshape(-1, wide, total.shape[-1])[:, :own]
            row += 1
    put_pieces(s_ref, grads, (home, core, side, cross))

    @pl.when(step == pl.num_programs(0) - 1)
    def _():
        stat_ref[...] = jnp.zeros_like(stat_ref)
        stat_ref[0:1, :] = fold(sums[0])


def fourth_conv(scalars, dh, halos, z1, z_halos, g_parts, coef, weight):
    batch, _, wide, chans = dh.shape
    own = wide - 8
    piece = (batch, 2, own // 2, chans)
    return call(
        fourth_kernel,
        batch // STEP,
        scalars,
        [by_sample(a) for a in (dh,) + halos + (z1,) + z_halos + (g_parts[0], g_parts[2])]
        + [whole(a) for a in (coef,) + weight],
        [out_by_sample(piece)] * 4 + [out_by_sample((batch, 4, own, chans)), out_whole((8, chans))],
        conv_scratch(wide, chans) + [pltpu.VMEM((1, 8, chans), F32), pltpu.VMEM((4, STEP, own, chans), F32)],
        "conv_four",
        1.2e10,
    )


def weight_kernel(s_ref, six, dz, out_ref, pad, high, low, total):
    step = pl.program_id(0)
    own, chans = dz.shape[2], dz.shape[3]
    wide = own + 8
    for row in range(6):
        values = six[:, row]
        pad[row, :, 8 : 8 + wide, :] = values
        pad[row, :, 0:8, :] = values[:, own:wide]
        for tap in range(3):
            shifted = values[:, :own] if tap == 1 else pad[row, :, 7 + tap : 7 + tap + own, :]
            at = (row * 3 + tap) * chans
            high[:, at : at + chans], low[:, at : at + chans] = split(shifted.reshape(-1, chans))

    @pl.when(step == 0)
    def _():
        total[...] = jnp.zeros_like(total)

    def product(left, right):
        return lax.dot_general(left, right, (((0,), (0,)), ((), ())), preferred_element_type=F32)

    sums = None
    for two in range(2):
        at = slice(two * 6 * chans, (two * 6 + 12) * chans)
        slope = jnp.concatenate(
            [dz[:, 2 * two].reshape(-1, chans), dz[:, 2 * two + 1].reshape(-1, chans)], axis=1
        )
        slope_high, slope_low = split(slope)
        part = product(high[:, at], slope_high)
        part += product(low[:, at], slope_high)
        part += product(high[:, at], slope_low)
        sums = part if sums is None else sums + part
    total[...] += sums

    @pl.when(step == pl.num_programs(0) - 1)
    def _():
        line = 3 * chans
        for row in range(3):
            out_ref[row * line : (row + 1) * line, :] = (
                total[row * line : (row + 1) * line, :chans] + total[(row + 1) * line : (row + 2) * line, chans:]
            )


def weight_grad(scalars, six, dz, name):
    batch, _, own, chans = dz.shape
    return call(
        weight_kernel,
        batch // STEP,
        scalars,
        [by_sample(six), by_sample(dz)],
        [out_whole((9 * chans, chans))],
        [
            pltpu.VMEM((6, STEP, own + 16, chans), F32),
            pltpu.VMEM((STEP * own, 18 * chans), BF16),
            pltpu.VMEM((STEP * own, 18 * chans), BF16),
            pltpu.VMEM((12 * chans, 2 * chans), F32),
        ],
        name,
        1.5e10,
    )[0]


def pack_weight(kernel):
    nothing = jnp.zeros_like(kernel[:1])
    both = jnp.stack(
        [jnp.concatenate([kernel, nothing], axis=0), jnp.concatenate([nothing, kernel], axis=0)], axis=3
    )
    both = both.reshape(4 * 3 * kernel.shape[2], 2 * kernel.shape[3])
    high = lax.reduce_precision(both, exponent_bits=8, mantissa_bits=7)
    return high.astype(BF16), (both - high).astype(BF16)


def flipped(kernel):
    return jnp.transpose(kernel[::-1, ::-1], (0, 1, 3, 2))


def rows_of(*vectors):
    filled = [jnp.reshape(v, (1, -1)) for v in vectors]
    nothing = jnp.zeros((8 - len(filled), filled[0].shape[1]), F32)
    return jnp.concatenate(filled + [nothing], axis=0)


def all_moments(stats, here):
    count = here
    for target in group_steps():
        other = permute(stats, target)
        mean = 0.5 * (stats[0] + other[0])
        gap = stats[0] - other[0]
        squares = stats[1] + other[1] + gap * gap * (0.5 * count)
        weight = stats[2] + other[2]
        product = (stats[3] + (stats[0] - mean) * stats[2]) + (other[3] + (other[0] - mean) * other[2])
        stats = rows_of(mean, squares, weight, product)
        count = 2.0 * count
    return stats


def all_sums(stats):
    for target in group_steps():
        stats = stats + permute(stats, target)
    return stats


def shards(
    fields, weight_one, bias_one, gain_one, shift_one, weight_two, bias_two, gain_two, shift_two, cotangent
):
    parts_here, batch, rows_here, cols_here, chans = fields.shape
    lat, lon = lax.axis_index("lat"), lax.axis_index("lon")
    lats, lons = lax.axis_size("lat"), lax.axis_size("lon")
    assert (parts_here, rows_here, lons) == (4, 2, 4)
    here = float(batch * 4 * 2 * cols_here)
    members = float(lats * lons // 4)
    count = here * members
    pair = lat // 2
    scalars = jnp.stack([lat % 2, lon % 2, pair % 2, pair == 0, pair == lats // 2 - 1]).astype(jnp.int32)
    cells = fields.reshape((2, 2) + fields.shape[1:])
    slopes = cotangent.reshape((2, 2) + cotangent.shape[1:])

    x_parts, x_halos = gather(scalars, cells, "x")
    tied = lax.optimization_barrier((slopes, x_parts[3]))
    g_parts, g_halos = gather(scalars, tied[0], "g")

    z1, pair_row, next_row, x_six, stats = first_conv(
        scalars, x_parts, x_halos, pack_weight(weight_one), rows_of(bias_one)
    )
    z1_halos = exchange_rows(pair_row, next_row)
    stats = all_moments(stats, here)
    center_one, spread_one = stats[0], stats[1] / count
    inv_one = lax.rsqrt(spread_one + EPSILON)

    z2, pair_row, next_row, h_six, stats = second_conv(
        scalars, z1, z1_halos, g_parts, rows_of(center_one, gain_one * inv_one, shift_one),
        pack_weight(weight_two), rows_of(bias_two),
    )
    z2_halos = exchange_rows(pair_row, next_row)
    stats = all_moments(stats, here)
    center_two, spread_two, dshift_two = stats[0], stats[1] / count, stats[2]
    inv_two = lax.rsqrt(spread_two + EPSILON)
    dgain_two = stats[3] * inv_two

    pieces = output_pieces(scalars, z2, x_six, rows_of(center_two, gain_two * inv_two, shift_two))
    output = place(scalars, send_home(pieces), "output_place")

    dh1, pair_row, next_row, dz2, stats = third_conv(
        scalars, z2, z2_halos, g_parts, g_halos, z1,
        rows_of(
            center_two, inv_two, gain_two * inv_two, dshift_two / count, dgain_two / count, center_one, inv_one
        ),
        pack_weight(flipped(weight_two)),
    )
    dh1_halos = exchange_rows(pair_row, next_row)
    dbias_two = stats[2]
    grad_w2 = weight_grad(scalars, h_six, dz2, "weight_two")
    stats = all_sums(stats)
    dshift_one, dgain_one = stats[0], stats[1]

    *pieces, dz1, stats = fourth_conv(
        scalars, dh1, dh1_halos, z1, z1_halos, g_parts,
        rows_of(center_one, inv_one, gain_one * inv_one, dshift_one / count, dgain_one / count),
        pack_weight(flipped(weight_one)),
    )
    input_grad = place(scalars, send_home(pieces), "grad_place")
    dbias_one = stats[0]
    grad_w1 = weight_grad(scalars, x_six, dz1, "weight_one")

    small = jnp.stack([
        dbias_one, dgain_one / members, dshift_one / members,
        dbias_two, dgain_two / members, dshift_two / members,
    ])
    grad_w1, grad_w2, small = lax.psum((grad_w1, grad_w2, small), AXES)
    return (
        output.reshape(fields.shape),
        input_grad.reshape(fields.shape),
        grad_w1.reshape(weight_one.shape),
        small[0],
        small[1],
        small[2],
        grad_w2.reshape(weight_two.shape),
        small[3],
        small[4],
        small[5],
    )


def solution(mesh):
    field = P(None, None, "lat", "lon", None)
    return jax.shard_map(
        shards,
        mesh=mesh,
        in_specs=(field,) + (P(),) * 8 + (field,),
        out_specs=(field, field) + (P(),) * 8,
        check_vma=False,
    )
```

```python
import functools

import jax
import jax.numpy as jnp
from jax import lax
from jax.experimental import pallas as pl
from jax.experimental.pallas import tpu as pltpu
from jax.sharding import PartitionSpec as P


EPSILON = 1e-05
F32 = jnp.float32
BF16 = jnp.bfloat16
AXES = ("lat", "lon")
STEP = 2
VMEM_LIMIT = 32 << 20
CHUNKS = 2


def permute(value, target):
    rows, cols = lax.axis_size("lat"), lax.axis_size("lon")
    pairs = []
    for row in range(rows):
        for col in range(cols):
            to = target(row, col)
            if 0 <= to[0] < rows and 0 <= to[1] < cols:
                pairs.append((row * cols + col, to[0] * cols + to[1]))
    return lax.ppermute(value, AXES, pairs)


def to_core(row, col):
    return row, col ^ 1


def to_side(row, col):
    return row ^ 1, col


def to_east(row, col):
    return row, col ^ 2


def to_east_side(row, col):
    return row ^ 1, col ^ 2


def to_pair(row, col):
    return row ^ 2, col


def to_next(row, col):
    return (row + 2 if (row // 2) % 2 else row - 2), col


def group_steps():
    steps = []
    bit = 2
    while bit < lax.axis_size("lon"):
        steps.append(functools.partial(lambda bit, row, col: (row, col ^ bit), bit))
        bit *= 2
    bit = 2
    while bit < lax.axis_size("lat"):
        steps.append(functools.partial(lambda bit, row, col: (row ^ bit, col), bit))
        bit *= 2
    return steps


def exchange_rows(pair_row, next_row):
    return permute(pair_row, to_pair), permute(next_row, to_next)


def after(value, *others):
    return lax.optimization_barrier((value,) + others)[0]


def split(value):
    high = value.astype(BF16)
    return high, (value - high.astype(F32)).astype(BF16)


def sigmoid(value):
    return 1.0 / (1.0 + jnp.exp(-value))


VMEM = pl.BlockSpec(memory_space=pltpu.VMEM)
SMEM = pl.BlockSpec(memory_space=pltpu.SMEM)
HBM = pl.BlockSpec(memory_space=pltpu.HBM)


def in_hbm(array):
    return pltpu.with_memory_space_constraint(array, pltpu.HBM)


class Stream:
    def __init__(self, array, first=0, count=None, group=0):
        self.array = array
        self.first = first
        self.count = array.shape[0] if count is None else count
        self.group = group


class Result:
    def __init__(self, *shape):
        self.shape = shape


class Flow:
    def __init__(self, ins, outs, sems):
        self.ins, self.outs, self.sems = ins, outs, sems

    def copy_in(self, k, i):
        _, far, near, first = self.ins[k]
        source = far.at[pl.ds(first + i * STEP, STEP)]
        return pltpu.make_async_copy(source, near.at[pl.ds(i * STEP, STEP)], self.sems.at[k, i])

    def copy_out(self, k, i):
        far, near = self.outs[k]
        at = pl.ds(i * STEP, STEP)
        return pltpu.make_async_copy(near.at[at], far.at[at], self.sems.at[len(self.ins) + k, i])

    def start(self):
        for group in sorted({stream[0] for stream in self.ins}):
            members = [k for k, stream in enumerate(self.ins) if stream[0] == group]
            for i in range(max(self.ins[k][2].shape[0] for k in members) // STEP):
                for k in members:
                    self.copy_in(k, i).start()

    def steps(self, samples, body, group=0):
        def one(i, carry):
            for k, stream in enumerate(self.ins):
                if stream[0] == group:
                    self.copy_in(k, i).wait()
            body(pl.ds(pl.multiple_of(i * STEP, STEP), STEP), i)
            for k in range(len(self.outs)):
                self.copy_out(k, i).start()
            return carry

        lax.fori_loop(0, samples // STEP, one, 0)

    def finish(self):
        for k, (_, near) in enumerate(self.outs):
            for i in range(near.shape[0] // STEP):
                self.copy_out(k, i).wait()


def call(body, scalars, inputs, outputs, scratch, name):
    streams = [a for a in inputs if isinstance(a, Stream)]
    results = [o for o in outputs if isinstance(o, Result)]
    buffers = [pltpu.VMEM((a.count,) + a.array.shape[1:], F32) for a in streams]
    buffers += [pltpu.VMEM(o.shape, F32) for o in results]
    most = max([a.count // STEP for a in streams] + [o.shape[0] // STEP for o in results] + [1])

    def kernel(s_ref, *refs):
        refs = list(refs)
        in_refs, out_refs = refs[: len(inputs)], refs[len(inputs) : len(inputs) + len(outputs)]
        rest = refs[len(inputs) + len(outputs) :]
        near, rest = rest[: len(buffers)], rest[len(buffers) :]
        sems, rest = rest[0], rest[1:]
        ins, outs = [], []
        for at, a in enumerate(inputs):
            if isinstance(a, Stream):
                ins.append((a.group, in_refs[at], near[len(ins)], a.first))
                in_refs[at] = ins[-1][2]
        for at, o in enumerate(outputs):
            if isinstance(o, Result):
                outs.append((out_refs[at], near[len(ins) + len(outs)]))
                out_refs[at] = outs[-1][1]
        flow = Flow(ins, outs, sems)
        flow.start()
        body(flow, s_ref, *in_refs, *out_refs, *rest)
        flow.finish()

    return pl.pallas_call(
        kernel,
        in_specs=[SMEM] + [HBM if isinstance(a, Stream) else VMEM for a in inputs],
        out_specs=[HBM if isinstance(o, Result) else VMEM for o in outputs],
        out_shape=[pltpu.HBM(o.shape, F32) if isinstance(o, Result) else jax.ShapeDtypeStruct(o, F32) for o in outputs],
        scratch_shapes=buffers + [pltpu.SemaphoreType.DMA((max(len(buffers), 1), most))] + list(scratch),
        compiler_params=pltpu.CompilerParams(vmem_limit_bytes=VMEM_LIMIT),
        cost_estimate=pl.CostEstimate(flops=0, bytes_accessed=0, transcendentals=0),
        name=name,
    )(scalars, *[in_hbm(a.array) if isinstance(a, Stream) else a for a in inputs])


def pack_kernel(other_core, s_ref, field, out, sem):
    core = 1 - s_ref[1] if other_core else s_ref[1]
    copy = pltpu.make_async_copy(field.at[:, core], out, sem)
    copy.start()
    copy.wait()


def pack(scalars, field, other_core, name):
    return pl.pallas_call(
        functools.partial(pack_kernel, other_core),
        in_specs=[SMEM, HBM],
        out_specs=VMEM,
        out_shape=jax.ShapeDtypeStruct((2,) + field.shape[2:], F32),
        scratch_shapes=[pltpu.SemaphoreType.DMA],
        compiler_params=pltpu.CompilerParams(vmem_limit_bytes=VMEM_LIMIT),
        name=name,
    )(scalars, in_hbm(field))


def wide_rows(nc, own, other, out):
    half = own.shape[1]
    out[:, pl.ds(pl.multiple_of(nc * half, half), half), :] = own
    out[:, pl.ds(pl.multiple_of((1 - nc) * half, half), half), :] = other


def ends(nc, own, other):
    cols = own.shape[1]
    west, east = jnp.where(nc == 0, own[:, 0:8], other[:, 0:8]), jnp.where(nc == 0, other[:, -8:], own[:, -8:])
    del cols
    return jnp.concatenate([west[:, 0:4], east[:, 4:8]], axis=1)


def rows_kernel(flow, s_ref, own, other, home, edge, inner, *tiles):
    lx, nc = s_ref[0], s_ref[1]
    for row in range(2):
        wide_rows(nc, own[lx, :, row], other[lx, :, row], home.at[:, row])
    wide_rows(nc, own[1 - lx, :, lx], other[1 - lx, :, lx], edge)
    wide_rows(nc, own[1 - lx, :, 1 - lx], other[1 - lx, :, 1 - lx], inner)
    for part, tile in zip((lx, 1 - lx), tiles):
        for row in range(2):
            tile[:, row] = ends(nc, own[part, :, row], other[part, :, row])


def rows(scalars, own, other, name):
    _, batch, _, cols, chans = own.shape
    row = (batch, 2 * cols, chans)
    tile = (batch, 2, 8, chans)
    return call(rows_kernel, scalars, [own, other], [(batch, 2) + row[1:], row, row, tile, tile], [], name)


def join_kernel(edge, flow, s_ref, home, foreign, tiles, foreign_tiles, rows_ref, pair_ref, next_ref):
    lx, odd = s_ref[0], s_ref[2]
    wide = home.shape[2]
    row = lx if edge else 1 - lx
    rows_ref[:, lx, 0:wide, :] = home[:, row]
    rows_ref[:, lx, wide : wide + 8, :] = tiles[:, row]
    rows_ref[:, 1 - lx, 0:wide, :] = foreign[...]
    rows_ref[:, 1 - lx, wide : wide + 8, :] = foreign_tiles[:, 1 - row]
    pair_ref[...] = rows_ref[:, 1 - odd]
    next_ref[...] = rows_ref[:, odd]


def join(scalars, home, foreign, tiles, foreign_tiles, edge, name):
    batch, _, wide, chans = home.shape
    row = (batch, wide + 8, chans)
    return call(
        functools.partial(join_kernel, edge),
        scalars,
        [home, foreign, tiles, foreign_tiles],
        [(batch, 2) + row[1:], row, row],
        [],
        name,
    )


def chunk_rows_kernel(flow, s_ref, own, other, home, tiles, other_tiles, *others):
    lx, nc = s_ref[0], s_ref[1]
    part = others[0].shape[0]
    for row in range(2):
        wide_rows(nc, own[lx, :, row], other[lx, :, row], home.at[:, row])
        for chunk, out in enumerate(others):
            at = slice(chunk * part, (chunk + 1) * part)
            wide_rows(nc, own[1 - lx, at, row], other[1 - lx, at, row], out.at[:, row])
        for side, tile in zip((lx, 1 - lx), (tiles, other_tiles)):
            tile[:, row] = ends(nc, own[side, :, row], other[side, :, row])


def chunk_rows(scalars, own, other, name):
    _, batch, _, cols, chans = own.shape
    tile = (batch, 2, 8, chans)
    row = (2, 2 * cols, chans)
    return call(
        chunk_rows_kernel,
        scalars,
        [own, other],
        [(batch,) + row, tile, tile] + [(batch // CHUNKS,) + row] * CHUNKS,
        [],
        name,
    )


def cell_kernel(first, flow, s_ref, home, foreign, tiles, foreign_tiles, rows_ref, pair_ref, next_ref):
    lx, odd = s_ref[0], s_ref[2]
    part, _, wide, _ = foreign.shape
    at = slice(first, first + part)
    for row in range(2):
        for side, rows, ends_of in ((2 * lx, home[at, row], tiles), (2 - 2 * lx, foreign[:, row], foreign_tiles)):
            rows_ref[:, side + row, 0:wide, :] = rows
            rows_ref[:, side + row, wide : wide + 8, :] = ends_of[at, row]
    pair_ref[...] = rows_ref[:, 3 - 3 * odd]
    next_ref[...] = rows_ref[:, 3 * odd]
    flow.steps(part, lambda here, i: None)


def cell_rows(scalars, home, foreign, tiles, chunk, name):
    part, _, wide, chans = foreign.shape
    row = (part, wide + 8, chans)
    return call(
        functools.partial(cell_kernel, chunk * part),
        scalars,
        [home, foreign, *tiles],
        [Result(part, 4, *row[1:]), row, row],
        [],
        name,
    )


def row_of_parts(parts, row, at):
    edge, inner = parts
    return (edge if row in (0, 3) else inner)[at, 0 if row < 2 else 1]


def ring_row(values, pad, row, high, low):
    step, wide, chans = values.shape
    pad[row, :, 8 : 8 + wide, :] = values
    pad[row, :, 0:8, :] = values[:, wide - 8 : wide]
    pad[row, :, 8 + wide : 16 + wide, :] = values[:, 0:8]
    for tap in range(3):
        shifted = values if tap == 1 else pad[row, :, 7 + tap : 7 + tap + wide, :]
        at = (row * 3 + tap) * chans
        high[:, at : at + chans], low[:, at : at + chans] = split(shifted.reshape(step * wide, chans))


def put_weight(weight, turned, high, low):
    chans = weight.shape[1]
    nothing = jnp.zeros((chans, chans), BF16)
    for row in range(3):
        for tap in range(3):
            block = weight[(2 - row) * 3 + 2 - tap].T if turned else weight[row * 3 + tap]
            parts = split(block)
            for out in range(2):
                at = ((row + out) * 3 + tap) * chans
                for ref, part in zip((high, low), parts):
                    ref[at : at + chans, out * chans : (out + 1) * chans] = part
    for tap in range(3):
        for ref in (high, low):
            ref[(9 + tap) * chans : (10 + tap) * chans, 0:chans] = nothing
            ref[tap * chans : (tap + 1) * chans, chans : 2 * chans] = nothing


def pair_of_rows(pair, high, low, weight_high, weight_low):
    chans = weight_high.shape[1] // 2
    at = slice(pair * 6 * chans, (pair * 6 + 12) * chans)
    total = jnp.dot(high[:, at], weight_high[...], preferred_element_type=F32)
    total += jnp.dot(low[:, at], weight_high[...], preferred_element_type=F32)
    total += jnp.dot(high[:, at], weight_low[...], preferred_element_type=F32)
    return total[:, :chans], total[:, chans:]


def north_south(s_ref, pair, following, at):
    odd = s_ref[2] == 1
    first, second = pair[at], following[at]
    return jnp.where(odd, first, second), jnp.where(odd, second, first)


def put_edges(s_ref, top, bottom, pair_out, next_out, at):
    odd = s_ref[2] == 1
    pair_out[at] = jnp.where(odd, top, bottom)
    next_out[at] = jnp.where(odd, bottom, top)


def lanes(values):
    return jnp.sum(values.reshape(-1, 8, values.shape[-1]), axis=0)


def fold(total):
    return jnp.sum(total, axis=0, keepdims=True)


def add_moments(active, first, shift, sums, others):
    @pl.when(first)
    def _():
        mean = jnp.mean(active[0].reshape(-1, active[0].shape[-1]), axis=0, keepdims=True)
        shift[...] = jnp.broadcast_to(mean, shift.shape)
        sums[...] = jnp.zeros_like(sums)

    base = shift[0:1, :]
    for at, values in enumerate(active):
        distance = values - base
        sums[0] += lanes(distance)
        sums[1] += lanes(distance * distance)
        if others is not None:
            sums[2] += lanes(others[at])
            sums[3] += lanes(others[at] * distance)


def put_moments(out_ref, shift, sums, count, others):
    total, squares = fold(sums[0]), fold(sums[1])
    offset = total / count
    out_ref[...] = jnp.zeros_like(out_ref)
    out_ref[0:1, :] = shift[0:1, :] + offset
    out_ref[1:2, :] = squares - total * offset
    if others:
        weight = fold(sums[2])
        out_ref[2:3, :] = weight
        out_ref[3:4, :] = fold(sums[3]) - weight * offset


def conv_scratch(wide, chans):
    return [
        pltpu.VMEM((6, STEP, wide + 16, chans), F32),
        pltpu.VMEM((STEP * wide, 18 * chans), BF16),
        pltpu.VMEM((STEP * wide, 18 * chans), BF16),
        pltpu.VMEM((12 * chans, 2 * chans), BF16),
        pltpu.VMEM((12 * chans, 2 * chans), BF16),
    ]


def first_kernel(
    flow, s_ref, edge, inner, pair, following, weight, bias, z_ref, stat_ref,
    pad, high, low, weight_high, weight_low, shift, sums,
):
    batch, _, wide, _ = z_ref.shape
    own = wide - 8
    put_weight(weight, False, weight_high, weight_low)

    def step(at, i):
        north, south = north_south(s_ref, pair, following, at)
        for row in range(6):
            values = north if row == 0 else south if row == 5 else row_of_parts((edge, inner), row - 1, at)
            ring_row(values, pad, row, high, low)
        active = []
        for two in range(2):
            for total in pair_of_rows(two, high, low, weight_high, weight_low):
                z = (total + bias[0:1, :]).reshape(-1, wide, total.shape[-1])
                z_ref[at, len(active)] = z
                active.append(z[:, :own] * sigmoid(z[:, :own]))
        add_moments(active, i == 0, shift, sums, None)

    flow.steps(batch, step)
    put_moments(stat_ref, shift, sums, float(batch * 4 * own), False)


def first_conv(scalars, parts, halos, weight, bias):
    batch, _, wide, chans = parts[0].shape
    return call(
        first_kernel,
        scalars,
        parts + halos + (weight, bias),
        [Result(batch, 4, wide, chans), (8, chans)],
        conv_scratch(wide, chans) + [pltpu.VMEM((8, chans), F32), pltpu.VMEM((4, 8, chans), F32)],
        "conv_one",
    )


def first_halo_kernel(
    flow, s_ref, edge, pair, following, pair_inner, following_inner, weight, bias, north_ref, south_ref,
    pad, high, low, weight_high, weight_low,
):
    batch, wide, chans = north_ref.shape
    for tap in range(9):
        taps = slice(tap * chans, (tap + 1) * chans)
        weight_high[taps, :], weight_low[taps, :] = split(weight[tap])

    def step(at, i):
        north, south = north_south(s_ref, pair, following, at)
        far_north, far_south = north_south(s_ref, pair_inner, following_inner, at)
        rows = (far_north, north, edge[at, 0], edge[at, 1], south, far_south)
        for row, values in enumerate(rows):
            ring_row(values, pad, row, high, low)
        for side, ref in enumerate((north_ref, south_ref)):
            taps = slice(side * 9 * chans, (side + 1) * 9 * chans)
            total = jnp.dot(high[:, taps], weight_high[...], preferred_element_type=F32)
            total += jnp.dot(low[:, taps], weight_high[...], preferred_element_type=F32)
            total += jnp.dot(high[:, taps], weight_low[...], preferred_element_type=F32)
            ref[at] = (total + bias[0:1, :]).reshape(-1, wide, chans)

    flow.steps(batch, step)


def first_halo_conv(scalars, edge, halos, far_halos, weight, bias):
    batch, _, wide, chans = edge.shape
    return call(
        first_halo_kernel,
        scalars,
        [Stream(edge), *[Stream(a) for a in halos + far_halos], weight, bias],
        [(batch, wide, chans)] * 2,
        conv_scratch(wide, chans)[:3] + [pltpu.VMEM((9 * chans, chans), BF16)] * 2,
        "conv_one_halo",
    )


def hidden_row(s_ref, z1, north, south, coef, at, there, row):
    center, scale, offset = coef[0:1, :], coef[1:2, :], coef[2:3, :]
    values = north[there] if row == 0 else south[there] if row == 5 else z1[at, row - 1]
    hidden = (values * sigmoid(values) - center) * scale + offset
    if row in (0, 5):
        hidden = jnp.where(s_ref[3 if row == 0 else 4] == 1, 0.0, hidden)
    return hidden


def second_kernel(
    first, flow, s_ref, z1, g_rows, north, south, coef, weight, bias,
    z_ref, pair_out, next_out, stat_ref, pad, high, low, weight_high, weight_low, shift, sums,
):
    part, _, wide, _ = z_ref.shape
    own = wide - 8
    put_weight(weight, False, weight_high, weight_low)

    def step(at, i):
        there = pl.ds(i * STEP + first, STEP)
        for row in range(6):
            ring_row(hidden_row(s_ref, z1, north, south, coef, at, there, row), pad, row, high, low)
        active = []
        rows = []
        for two in range(2):
            for total in pair_of_rows(two, high, low, weight_high, weight_low):
                z = (total + bias[0:1, :]).reshape(-1, wide, total.shape[-1])
                z_ref[at, len(rows)] = z
                rows.append(z)
                active.append(z[:, :own] * sigmoid(z[:, :own]))
        put_edges(s_ref, rows[0], rows[3], pair_out, next_out, at)
        add_moments(active, i == 0, shift, sums, [g_rows[at, row, :own] for row in range(4)])

    flow.steps(part, step)
    put_moments(stat_ref, shift, sums, float(part * 4 * own), True)


def second_conv(scalars, z1, halos, g_rows, coef, weight, bias, chunk):
    part, _, wide, chans = g_rows.shape
    return call(
        functools.partial(second_kernel, chunk * part),
        scalars,
        [Stream(z1, chunk * part, part), Stream(g_rows), *halos, coef, weight, bias],
        [Result(part, 4, wide, chans), (part, wide, chans), (part, wide, chans), (8, chans)],
        conv_scratch(wide, chans) + [pltpu.VMEM((8, chans), F32), pltpu.VMEM((4, 8, chans), F32)],
        "conv_two",
    )


def put_pieces(s_ref, rows, home, other, at):
    lx = s_ref[0]
    for row in range(2):
        home[at, row] = rows[2 * lx + row]
        other[at, row] = rows[2 - 2 * lx + row]


def halves_kernel(flow, s_ref, home, foreign, out):
    cols = out.shape[3]
    there = pl.ds(pl.multiple_of((1 - s_ref[1]) * cols, cols), cols)
    for at, rows in enumerate((home, foreign)):
        for row in range(2):
            out[at, :, row] = rows[:, row, there, :]


def send_side(home, other):
    return home, permute(other, to_side)


def send_core(scalars, home, foreign, name):
    part, _, wide, chans = home.shape
    payload = call(halves_kernel, scalars, [home, foreign], [(2, part, 2, wide // 2, chans)], [], name)[0]
    return home, foreign, permute(payload, to_core)


def place_kernel(chunk, s_ref, home, foreign, core, *refs):
    out, sems = refs[-2:]
    lx, nc = s_ref[0], s_ref[1]
    part, cols = core.shape[1], core.shape[3]
    at = pl.ds(chunk * part, part)
    here = pl.ds(pl.multiple_of(nc * cols, cols), cols)
    copies = [
        pltpu.make_async_copy(home.at[:, :, here, :], out.at[lx, nc, at], sems.at[0]),
        pltpu.make_async_copy(foreign.at[:, :, here, :], out.at[1 - lx, nc, at], sems.at[1]),
        pltpu.make_async_copy(core.at[0], out.at[lx, 1 - nc, at], sems.at[2]),
        pltpu.make_async_copy(core.at[1], out.at[1 - lx, 1 - nc, at], sems.at[3]),
    ]
    for copy in copies:
        copy.start()
    for copy in copies:
        copy.wait()


def place(scalars, pieces, chunk, filled, name):
    _, part, rows_here, cols, chans = pieces[2].shape
    shape = (2, 2, part * CHUNKS, rows_here, cols, chans)
    earlier = [] if filled is None else [filled]
    return pl.pallas_call(
        functools.partial(place_kernel, chunk),
        in_specs=[SMEM] + [VMEM] * 3 + [HBM] * len(earlier),
        out_specs=HBM,
        out_shape=jax.ShapeDtypeStruct(shape, F32),
        scratch_shapes=[pltpu.SemaphoreType.DMA((4,))],
        input_output_aliases={4: 0} if earlier else {},
        compiler_params=pltpu.CompilerParams(vmem_limit_bytes=VMEM_LIMIT),
        name=name,
    )(scalars, *pieces, *earlier)


def silu_and_slope(z):
    sigma = sigmoid(z)
    return z * sigma, sigma * (1.0 + z * (1.0 - sigma))


def third_kernel(
    flow, s_ref, z2, g_rows, z1, x_edge, x_inner, pair, following, g_pair, g_following, coef, weight,
    dh_ref, dz_ref, pair_out, next_out, stat_ref, home, other,
    pad, high, low, weight_high, weight_low, sums, results,
):
    part, _, wide, _ = dh_ref.shape
    own = wide - 8
    center, inverse, scale = coef[0:1, :], coef[1:2, :], coef[2:3, :]
    mean_shift, mean_gain = coef[3:4, :], coef[4:5, :]
    center_one, inverse_one, shift_two = coef[5:6, :], coef[6:7, :], coef[7:8, :]
    put_weight(weight, True, weight_high, weight_low)
    sums[...] = jnp.zeros_like(sums)

    def step(at, i):
        north, south = north_south(s_ref, pair, following, at)
        g_north, g_south = north_south(s_ref, g_pair, g_following, at)
        for row in range(6):
            if row in (0, 5):
                z, g = (north, g_north) if row == 0 else (south, g_south)
            else:
                z, g = z2[at, row - 1], g_rows[at, row - 1]
            active, slope = silu_and_slope(z)
            distance = active - center
            dz = scale * (g - mean_shift - distance * inverse * mean_gain) * slope
            if row in (0, 5):
                dz = jnp.where(s_ref[3 if row == 0 else 4] == 1, 0.0, dz)
            else:
                dz_ref[at, row - 1] = dz[:, :own]
                sums[2] += lanes(dz[:, :own])
                x = row_of_parts((x_edge, x_inner), row - 1, at)
                results[row - 1] = x[:, :own] + (distance[:, :own] * scale + shift_two)
            ring_row(dz, pad, row, high, low)
        rows = []
        for two in range(2):
            for total in pair_of_rows(two, high, low, weight_high, weight_low):
                dh = total.reshape(-1, wide, total.shape[-1])
                row = len(rows)
                dh_ref[at, row] = dh
                rows.append(dh)
                z = z1[at, row, :own]
                sums[0] += lanes(dh[:, :own])
                sums[1] += lanes(dh[:, :own] * ((z * sigmoid(z) - center_one) * inverse_one))
        put_edges(s_ref, rows[0], rows[3], pair_out, next_out, at)
        put_pieces(s_ref, results, home, other, at)

    flow.steps(part, step)
    stat_ref[...] = jnp.zeros_like(stat_ref)
    for row in range(3):
        stat_ref[row : row + 1, :] = fold(sums[row])


def third_conv(scalars, z2, halos, g_rows, g_halos, z1, x_parts, coef, weight, chunk):
    part, _, wide, chans = z2.shape
    own = wide - 8
    first = chunk * part
    return call(
        third_kernel,
        scalars,
        [Stream(z2), Stream(g_rows)]
        + [Stream(a, first, part) for a in (z1,) + x_parts]
        + [*halos, *g_halos, coef, weight],
        [Result(part, 4, wide, chans), Result(part, 4, own, chans)]
        + [(part, wide, chans), (part, wide, chans), (8, chans), (part, 2, own, chans), (part, 2, own, chans)],
        conv_scratch(wide, chans) + [pltpu.VMEM((3, 8, chans), F32), pltpu.VMEM((4, STEP, own, chans), F32)],
        "conv_three",
    )


def slope_one(z, q, coef):
    center, inverse, scale = coef[0:1, :], coef[1:2, :], coef[2:3, :]
    mean_shift, mean_gain = coef[3:4, :], coef[4:5, :]
    active, slope = silu_and_slope(z)
    return scale * (q - mean_shift - (active - center) * inverse * mean_gain) * slope


def fourth_kernel(
    flow, s_ref, dh, z1, z_north, z_south, g_rows, pair, following, coef, weight,
    home, other, pad, high, low, weight_high, weight_low, results,
):
    part, _, wide, _ = dh.shape
    own = wide - 8
    put_weight(weight, True, weight_high, weight_low)

    def step(at, i):
        north, south = north_south(s_ref, pair, following, at)
        for row in range(6):
            if row in (0, 5):
                z, q = (z_north[at], north) if row == 0 else (z_south[at], south)
            else:
                z, q = z1[at, row - 1], dh[at, row - 1]
            dz = slope_one(z, q, coef)
            if row in (0, 5):
                dz = jnp.where(s_ref[3 if row == 0 else 4] == 1, 0.0, dz)
            ring_row(dz, pad, row, high, low)
        row = 0
        for two in range(2):
            for total in pair_of_rows(two, high, low, weight_high, weight_low):
                results[row] = g_rows[at, row, :own] + total.reshape(-1, wide, total.shape[-1])[:, :own]
                row += 1
        put_pieces(s_ref, results, home, other, at)

    flow.steps(part, step)


def fourth_conv(scalars, dh, halos, z1, z_halos, g_rows, coef, weight, chunk):
    part, _, wide, chans = dh.shape
    own = wide - 8
    return call(
        fourth_kernel,
        scalars,
        [Stream(dh)]
        + [Stream(a, chunk * part, part) for a in (z1,) + z_halos]
        + [Stream(g_rows), *halos, coef, weight],
        [(part, 2, own, chans)] * 2,
        conv_scratch(wide, chans) + [pltpu.VMEM((4, STEP, own, chans), F32)],
        "conv_four",
    )


def weight_step(rows, slopes, pad, high, low, total):
    own, chans = slopes[0].shape[1], slopes[0].shape[2]
    wide = own + 8
    for row, values in enumerate(rows):
        pad[row, :, 8 : 8 + wide, :] = values
        pad[row, :, 0:8, :] = values[:, own:wide]
        for tap in range(3):
            shifted = values[:, :own] if tap == 1 else pad[row, :, 7 + tap : 7 + tap + own, :]
            at = (row * 3 + tap) * chans
            high[:, at : at + chans], low[:, at : at + chans] = split(shifted.reshape(-1, chans))

    def product(left, right):
        return lax.dot_general(left, right, (((0,), (0,)), ((), ())), preferred_element_type=F32)

    sums = None
    for two in range(2):
        at = slice(two * 6 * chans, (two * 6 + 12) * chans)
        slope = jnp.concatenate([s.reshape(-1, chans) for s in slopes[2 * two : 2 * two + 2]], axis=1)
        slope_high, slope_low = split(slope)
        part = product(high[:, at], slope_high)
        part += product(low[:, at], slope_high)
        part += product(high[:, at], slope_low)
        sums = part if sums is None else sums + part
    total[...] += sums


SMALL = 32


def weight_end(out_ref, total, small, bias):
    chans = out_ref.shape[1]
    line = 3 * chans
    for row in range(3):
        out_ref[row * line : (row + 1) * line, :] = (
            total[row * line : (row + 1) * line, :chans] + total[(row + 1) * line : (row + 2) * line, chans:]
        )
    out_ref[3 * line :, :] = jnp.zeros((SMALL, chans), F32)
    out_ref[3 * line : 3 * line + 8, :] = small[...]
    if bias is not None:
        out_ref[3 * line : 3 * line + 1, :] = fold(bias[...])


def weight_scratch(own, chans):
    return [
        pltpu.VMEM((6, STEP, own + 16, chans), F32),
        pltpu.VMEM((STEP * own, 18 * chans), BF16),
        pltpu.VMEM((STEP * own, 18 * chans), BF16),
        pltpu.VMEM((12 * chans, 2 * chans), F32),
    ]


def weight_two_kernel(flow, s_ref, *refs):
    chunks = [refs[4 * chunk : 4 * chunk + 4] for chunk in range(CHUNKS)]
    coef, small, out_ref, *scratch = refs[4 * CHUNKS :]
    scratch[-1][...] = jnp.zeros_like(scratch[-1])
    for chunk, (z1, north, south, dz) in enumerate(chunks):

        def step(at, i):
            rows = [hidden_row(s_ref, z1, north, south, coef, at, at, row) for row in range(6)]
            weight_step(rows, [dz[at, row] for row in range(4)], *scratch)

        flow.steps(dz.shape[0], step, chunk)
    weight_end(out_ref, scratch[-1], small, None)


def weight_two_grad(scalars, z1, halos, coef, dz, small):
    part, _, own, chans = dz[0].shape
    streams = []
    for chunk in range(CHUNKS):
        streams += [Stream(a, chunk * part, part, chunk) for a in (z1,) + halos]
        streams += [Stream(dz[chunk], group=chunk)]
    return call(
        weight_two_kernel,
        scalars,
        streams + [coef, small],
        [(9 * chans + SMALL, chans)],
        weight_scratch(own, chans),
        "weight_two",
    )[0]


def weight_one_kernel(flow, s_ref, *refs):
    chunks = [refs[6 * chunk : 6 * chunk + 6] for chunk in range(CHUNKS)]
    coef, small, out_ref, bias, *scratch = refs[6 * CHUNKS :]
    bias[...] = jnp.zeros_like(bias)
    scratch[-1][...] = jnp.zeros_like(scratch[-1])
    for chunk, (edge, inner, pair, following, z1, dh) in enumerate(chunks):
        part, _, wide, _ = dh.shape
        own = wide - 8

        def step(at, i):
            north, south = north_south(s_ref, pair, following, at)
            rows = [north] + [row_of_parts((edge, inner), row, at) for row in range(4)] + [south]
            slopes = [slope_one(z1[at, row, :own], dh[at, row, :own], coef) for row in range(4)]
            for slope in slopes:
                bias[...] += lanes(slope)
            weight_step(rows, slopes, *scratch)

        flow.steps(part, step, chunk)
    weight_end(out_ref, scratch[-1], small, bias)


def weight_one_grad(scalars, parts, halos, dh, z1, coef, small):
    part, _, wide, chans = dh[0].shape
    streams = []
    for chunk in range(CHUNKS):
        streams += [Stream(a, chunk * part, part, chunk) for a in parts + halos + (z1,)]
        streams += [Stream(dh[chunk], group=chunk)]
    return call(
        weight_one_kernel,
        scalars,
        streams + [coef, small],
        [(9 * chans + SMALL, chans)],
        [pltpu.VMEM((8, chans), F32)] + weight_scratch(wide - 8, chans),
        "weight_one",
    )[0]


def rows_of(*vectors):
    filled = [jnp.reshape(v, (1, -1)) for v in vectors]
    if len(filled) < 8:
        filled.append(jnp.zeros((8 - len(filled), filled[0].shape[1]), F32))
    return jnp.concatenate(filled, axis=0)


def merge_moments(one, other, count):
    mean = 0.5 * (one[0] + other[0])
    gap = one[0] - other[0]
    squares = one[1] + other[1] + gap * gap * (0.5 * count)
    weight = one[2] + other[2]
    product = (one[3] + (one[0] - mean) * one[2]) + (other[3] + (other[0] - mean) * other[2])
    return rows_of(mean, squares, weight, product)


def all_moments(stats, here, *others):
    count = here
    partial = []
    for target in group_steps():
        stats = merge_moments(stats, permute(stats, target), count)
        if not partial and others:
            stats = after(stats, *others)
        partial.append(stats)
        count = 2.0 * count
    return partial


def all_sums(stats, *others):
    partial = []
    for target in group_steps():
        stats = stats + permute(stats, target)
        if not partial and others:
            stats = after(stats, *others)
        partial.append(stats)
    return partial


def quarters_kernel(flow, s_ref, value, own, *others):
    size = own.shape[0]
    here = 2 * s_ref[5] + s_ref[2]
    for bits, ref in zip((0, 2, 1, 3), (own,) + others):
        ref[...] = value[pl.ds(pl.multiple_of((here ^ bits) * size, 8), size), :]


def whole_kernel(flow, s_ref, own, *refs):
    others, out = refs[:-1], refs[-1]
    size = own.shape[0]
    here = 2 * s_ref[5] + s_ref[2]
    for bits, ref in zip((0, 2, 1, 3), (own,) + others):
        out[pl.ds(pl.multiple_of((here ^ bits) * size, 8), size), :] = ref[...]


def to_east_pair(row, col):
    return row ^ 2, col ^ 2


def sum_everywhere(scalars, one, two, lon, beside):
    west = lon % 2 == 0
    value = jnp.where(west, one, two) + permute(after(jnp.where(west, two, one), *beside[0]), to_core)
    size, chans = value.shape[0] // 4, value.shape[1]
    targets = (to_east, to_pair, to_east_pair)
    own, *others = call(quarters_kernel, scalars, [value], [(size, chans)] * 4, [], "quarters")
    others = [permute(v, target) for v, target in zip(others, targets)]
    own = after(own, *beside[1])
    own = (own + others[0]) + (others[1] + others[2])
    own = own + permute(own, to_side)
    last = beside[2](own)
    for target in group_steps()[2:]:
        own = own + permute(own, target)
    others = [permute(own, target) for target in targets]
    value = call(whole_kernel, scalars, [after(own, last), *others], [(4 * size, chans)], [], "whole")[0]
    other = permute(value, to_core)
    return jnp.where(west, value, other), jnp.where(west, other, value)


def shards(
    fields, weight_one, bias_one, gain_one, shift_one, weight_two, bias_two, gain_two, shift_two, cotangent
):
    parts_here, batch, rows_here, cols_here, chans = fields.shape
    lat, lon = lax.axis_index("lat"), lax.axis_index("lon")
    lats, lons = lax.axis_size("lat"), lax.axis_size("lon")
    assert (parts_here, rows_here, lons) == (4, 2, 4)
    here = float(batch * 4 * 2 * cols_here)
    members = float(lats * lons // 4)
    count = here * members
    pair = lat // 2
    scalars = jnp.stack([lat % 2, lon % 2, pair % 2, pair == 0, pair == lats // 2 - 1, lon // 2]).astype(jnp.int32)
    cells = fields.reshape((2, 2) + fields.shape[1:])
    slopes = cotangent.reshape((2, 2) + cotangent.shape[1:])
    taps_one = weight_one.reshape((9, chans, chans))
    taps_two = weight_two.reshape((9, chans, chans))

    other = pack(scalars, cells, True, "x_pack_other")
    core = permute(other, to_core)
    own = pack(scalars, after(cells, other), False, "x_pack_own")
    home, edge, inner, tiles, other_tiles = rows(scalars, own, core, "x_rows")
    edge = permute(edge, to_side)
    tiles = permute(tiles, to_east)
    foreign_tiles = permute(other_tiles, to_east_side)
    inner = permute(after(inner, tiles), to_side)
    x_edge, pair_row, next_row = join(scalars, home, edge, tiles, foreign_tiles, True, "x_edge")
    x_halos = exchange_rows(pair_row, next_row)
    slopes = after(slopes, x_edge)
    other = pack(scalars, slopes, True, "g_pack_other")
    core = permute(other, to_core)
    own = pack(scalars, after(slopes, other), False, "g_pack_own")
    g_home, g_tiles, g_other, *g_foreign = chunk_rows(scalars, own, core, "g_rows")
    g_foreign = [permute(part, to_side) for part in g_foreign]
    g_tiles = (permute(g_tiles, to_east), permute(g_other, to_east_side))
    x_inner, pair_row, next_row = join(scalars, after(home, g_home), inner, tiles, foreign_tiles, False, "x_inner")
    x_far = exchange_rows(pair_row, next_row)
    x_parts = (x_edge, x_inner)

    z1, stats = first_conv(scalars, x_parts, x_halos, taps_one, after(rows_of(bias_one), g_home))
    partial = all_moments(after(stats, *x_far, g_foreign[0]), here)
    z1_halos = tuple(
        first_halo_conv(scalars, after(x_edge, partial[-2]), x_halos, x_far, taps_one, rows_of(bias_one))
    )
    g_rows, g_edges = [], []
    for chunk in range(CHUNKS):
        foreign = after(g_foreign[chunk], z1_halos[0])
        four, pair_row, next_row = cell_rows(scalars, g_home, foreign, g_tiles, chunk, "g_cell")
        g_rows.append(four)
        g_edges.append((pair_row, next_row))
    stats = partial[-1]
    center_one, spread_one = stats[0], stats[1] / count
    inv_one = lax.rsqrt(spread_one + EPSILON)

    coef_one = rows_of(center_one, gain_one * inv_one, shift_one)
    g_halos = [exchange_rows(after(top, coef_one), bottom) for top, bottom in g_edges]
    z2, z2_edges, parts, earlier = [], [], [], []
    for chunk in range(CHUNKS):
        z, pair_row, next_row, stats = second_conv(
            scalars, z1, z1_halos, g_rows[chunk], after(coef_one, *earlier), taps_two, rows_of(bias_two), chunk
        )
        earlier = [z, *g_halos[0], *g_halos[1]]
        z2.append(z)
        z2_edges.append((pair_row, next_row))
        parts.append(stats)
    z2_halos = [exchange_rows(*z2_edges[0])]
    partial = all_moments(merge_moments(parts[0], parts[1], here / CHUNKS), here, *z2_halos[0])
    z2_halos.append(exchange_rows(after(z2_edges[1][0], partial[-2]), z2_edges[1][1]))
    stats = partial[-1]
    center_two, spread_two, dshift_two = stats[0], stats[1] / count, stats[2]
    inv_two = lax.rsqrt(spread_two + EPSILON)
    dgain_two = stats[3] * inv_two

    coef = rows_of(
        center_two, inv_two, gain_two * inv_two, dshift_two / count, dgain_two / count, center_one, inv_one,
        shift_two,
    )
    dh1, dz2, dh1_edges, parts, output = [], [], [], [], []
    for chunk in range(CHUNKS):
        dh, dz, pair_row, next_row, stats, *pieces = third_conv(
            scalars, z2[chunk], z2_halos[chunk], g_rows[chunk], g_halos[chunk], z1, x_parts, after(coef, *dh1),
            taps_two, chunk,
        )
        dh1.append(dh)
        dz2.append(dz)
        dh1_edges.append((pair_row, next_row))
        parts.append(stats)
        output.append(send_side(*pieces))
    stats = parts[0] + parts[1]
    dbias_two = stats[2]
    dh1_halos = [exchange_rows(*dh1_edges[0])]
    partial = all_sums(stats, *dh1_halos[0])
    dh1_halos.append(exchange_rows(after(dh1_edges[1][0], partial[-2]), dh1_edges[1][1]))
    small = rows_of(dbias_two, dgain_two / members, dshift_two / members)
    grad_w2 = weight_two_grad(scalars, z1, z1_halos, after(coef_one, partial[-2]), dz2, small)
    dshift_one, dgain_one = partial[-1][0], partial[-1][1]

    coef = rows_of(center_one, inv_one, gain_one * inv_one, dshift_one / count, dgain_one / count)
    small = rows_of(jnp.zeros_like(dgain_one), dgain_one / members, dshift_one / members)

    def input_slope(chunk, coef):
        return fourth_conv(
            scalars, dh1[chunk], dh1_halos[chunk], z1, z1_halos, g_rows[chunk], coef, taps_one, chunk
        )

    pieces = input_slope(0, after(coef, grad_w2, output[0][1], output[1][1]))
    grad_w1 = weight_one_grad(scalars, x_parts, x_halos, dh1, z1, after(coef, pieces[0]), small)
    input_grad = [send_side(*pieces)]
    pieces = input_slope(1, after(coef, grad_w1))
    out_whole = None
    for chunk in range(CHUNKS):
        out_whole = place(scalars, send_core(scalars, *output[chunk], "output_halves"), chunk, out_whole, "output_place")
    def send_last(summed):
        input_grad.append(send_side(pieces[0], after(pieces[1], summed)))
        return input_grad[1][1]

    beside = ([input_grad[0][1]], [pieces[0], out_whole], send_last)
    one, two = sum_everywhere(scalars, grad_w1, grad_w2, lon, beside)
    many = 9 * chans
    sums = (one[:many], one[many], one[many + 1], one[many + 2], two[:many], two[many], two[many + 1], two[many + 2])
    grad_whole = place(scalars, send_core(scalars, *input_grad[0], "grad_halves"), 0, None, "grad_place")
    home, grad_whole = lax.optimization_barrier((input_grad[1][0], grad_whole))
    pieces = send_core(scalars, home, input_grad[1][1], "grad_halves")
    home, *sums = lax.optimization_barrier((home, *sums))
    pieces = (home,) + pieces[1:]
    grad_whole = place(scalars, pieces, 1, grad_whole, "grad_place")
    return (
        out_whole.reshape(fields.shape),
        grad_whole.reshape(fields.shape),
        sums[0].reshape(weight_one.shape),
        *sums[1:4],
        sums[4].reshape(weight_two.shape),
        *sums[5:8],
    )


def solution(mesh):
    field = P(None, None, "lat", "lon", None)
    return jax.shard_map(
        shards,
        mesh=mesh,
        in_specs=(field,) + (P(),) * 8 + (field,),
        out_specs=(field, field) + (P(),) * 8,
        check_vma=False,
    )
```

```python
import functools

import jax
import jax.numpy as jnp
from jax import lax
from jax.experimental import pallas as pl
from jax.experimental.pallas import tpu as pltpu
from jax.sharding import PartitionSpec as P


EPSILON = 1e-05
F32 = jnp.float32
BF16 = jnp.bfloat16
AXES = ("lat", "lon")
STEP = 2
VMEM_LIMIT = 32 << 20
CHUNKS = 2


def permute(value, target):
    rows, cols = lax.axis_size("lat"), lax.axis_size("lon")
    pairs = []
    for row in range(rows):
        for col in range(cols):
            to = target(row, col)
            if 0 <= to[0] < rows and 0 <= to[1] < cols:
                pairs.append((row * cols + col, to[0] * cols + to[1]))
    return lax.ppermute(value, AXES, pairs)


def to_core(row, col):
    return row, col ^ 1


def to_side(row, col):
    return row ^ 1, col


def to_east(row, col):
    return row, col ^ 2


def to_east_side(row, col):
    return row ^ 1, col ^ 2


def to_pair(row, col):
    return row ^ 2, col


def to_next(row, col):
    return (row + 2 if (row // 2) % 2 else row - 2), col


def group_steps():
    steps = []
    bit = 2
    while bit < lax.axis_size("lon"):
        steps.append(functools.partial(lambda bit, row, col: (row, col ^ bit), bit))
        bit *= 2
    bit = 2
    while bit < lax.axis_size("lat"):
        steps.append(functools.partial(lambda bit, row, col: (row ^ bit, col), bit))
        bit *= 2
    return steps


def exchange_rows(pair_row, next_row):
    return permute(pair_row, to_pair), permute(next_row, to_next)


def after(value, *others):
    return lax.optimization_barrier((value,) + others)[0]


def split(value):
    high = value.astype(BF16)
    return high, (value - high.astype(F32)).astype(BF16)


def sigmoid(value):
    return 1.0 / (1.0 + jnp.exp(-value))


VMEM = pl.BlockSpec(memory_space=pltpu.VMEM)
SMEM = pl.BlockSpec(memory_space=pltpu.SMEM)
HBM = pl.BlockSpec(memory_space=pltpu.HBM)


def in_hbm(array):
    return pltpu.with_memory_space_constraint(array, pltpu.HBM)


class Stream:
    def __init__(self, array, first=0, count=None, group=0):
        self.array = array
        self.first = first
        self.count = array.shape[0] if count is None else count
        self.group = group


class Result:
    def __init__(self, *shape):
        self.shape = shape


class Flow:
    def __init__(self, ins, outs, sems):
        self.ins, self.outs, self.sems = ins, outs, sems

    def copy_in(self, k, i):
        _, far, near, first = self.ins[k]
        source = far.at[pl.ds(first + i * STEP, STEP)]
        return pltpu.make_async_copy(source, near.at[pl.ds(i * STEP, STEP)], self.sems.at[k, i])

    def copy_out(self, k, i):
        far, near = self.outs[k]
        at = pl.ds(i * STEP, STEP)
        return pltpu.make_async_copy(near.at[at], far.at[at], self.sems.at[len(self.ins) + k, i])

    def start(self):
        for group in sorted({stream[0] for stream in self.ins}):
            members = [k for k, stream in enumerate(self.ins) if stream[0] == group]
            for i in range(max(self.ins[k][2].shape[0] for k in members) // STEP):
                for k in members:
                    self.copy_in(k, i).start()

    def steps(self, samples, body, group=0):
        def one(i, carry):
            for k, stream in enumerate(self.ins):
                if stream[0] == group:
                    self.copy_in(k, i).wait()
            body(pl.ds(pl.multiple_of(i * STEP, STEP), STEP), i)
            for k in range(len(self.outs)):
                self.copy_out(k, i).start()
            return carry

        lax.fori_loop(0, samples // STEP, one, 0)

    def finish(self):
        for k, (_, near) in enumerate(self.outs):
            for i in range(near.shape[0] // STEP):
                self.copy_out(k, i).wait()


def call(body, scalars, inputs, outputs, scratch, name):
    streams = [a for a in inputs if isinstance(a, Stream)]
    results = [o for o in outputs if isinstance(o, Result)]
    buffers = [pltpu.VMEM((a.count,) + a.array.shape[1:], F32) for a in streams]
    buffers += [pltpu.VMEM(o.shape, F32) for o in results]
    most = max([a.count // STEP for a in streams] + [o.shape[0] // STEP for o in results] + [1])

    def kernel(s_ref, *refs):
        refs = list(refs)
        in_refs, out_refs = refs[: len(inputs)], refs[len(inputs) : len(inputs) + len(outputs)]
        rest = refs[len(inputs) + len(outputs) :]
        near, rest = rest[: len(buffers)], rest[len(buffers) :]
        sems, rest = rest[0], rest[1:]
        ins, outs = [], []
        for at, a in enumerate(inputs):
            if isinstance(a, Stream):
                ins.append((a.group, in_refs[at], near[len(ins)], a.first))
                in_refs[at] = ins[-1][2]
        for at, o in enumerate(outputs):
            if isinstance(o, Result):
                outs.append((out_refs[at], near[len(ins) + len(outs)]))
                out_refs[at] = outs[-1][1]
        flow = Flow(ins, outs, sems)
        flow.start()
        body(flow, s_ref, *in_refs, *out_refs, *rest)
        flow.finish()

    return pl.pallas_call(
        kernel,
        in_specs=[SMEM] + [HBM if isinstance(a, Stream) else VMEM for a in inputs],
        out_specs=[HBM if isinstance(o, Result) else VMEM for o in outputs],
        out_shape=[pltpu.HBM(o.shape, F32) if isinstance(o, Result) else jax.ShapeDtypeStruct(o, F32) for o in outputs],
        scratch_shapes=buffers + [pltpu.SemaphoreType.DMA((max(len(buffers), 1), most))] + list(scratch),
        compiler_params=pltpu.CompilerParams(vmem_limit_bytes=VMEM_LIMIT),
        cost_estimate=pl.CostEstimate(flops=0, bytes_accessed=0, transcendentals=0),
        name=name,
    )(scalars, *[in_hbm(a.array) if isinstance(a, Stream) else a for a in inputs])


def pack_kernel(other_core, s_ref, field, out, sem):
    core = 1 - s_ref[1] if other_core else s_ref[1]
    copy = pltpu.make_async_copy(field.at[:, core], out, sem)
    copy.start()
    copy.wait()


def pack(scalars, field, other_core, name):
    return pl.pallas_call(
        functools.partial(pack_kernel, other_core),
        in_specs=[SMEM, HBM],
        out_specs=VMEM,
        out_shape=jax.ShapeDtypeStruct((2,) + field.shape[2:], F32),
        scratch_shapes=[pltpu.SemaphoreType.DMA],
        compiler_params=pltpu.CompilerParams(vmem_limit_bytes=VMEM_LIMIT),
        name=name,
    )(scalars, in_hbm(field))


def wide_rows(nc, own, other, out):
    half = own.shape[1]
    out[:, pl.ds(pl.multiple_of(nc * half, half), half), :] = own
    out[:, pl.ds(pl.multiple_of((1 - nc) * half, half), half), :] = other


def ends(nc, own, other):
    cols = own.shape[1]
    west, east = jnp.where(nc == 0, own[:, 0:8], other[:, 0:8]), jnp.where(nc == 0, other[:, -8:], own[:, -8:])
    del cols
    return jnp.concatenate([west[:, 0:4], east[:, 4:8]], axis=1)


def rows_kernel(flow, s_ref, own, other, home, edge, inner, *tiles):
    lx, nc = s_ref[0], s_ref[1]
    for row in range(2):
        wide_rows(nc, own[lx, :, row], other[lx, :, row], home.at[:, row])
    wide_rows(nc, own[1 - lx, :, lx], other[1 - lx, :, lx], edge)
    wide_rows(nc, own[1 - lx, :, 1 - lx], other[1 - lx, :, 1 - lx], inner)
    for part, tile in zip((lx, 1 - lx), tiles):
        for row in range(2):
            tile[:, row] = ends(nc, own[part, :, row], other[part, :, row])


def rows(scalars, own, other, name):
    _, batch, _, cols, chans = own.shape
    row = (batch, 2 * cols, chans)
    tile = (batch, 2, 8, chans)
    return call(rows_kernel, scalars, [own, other], [(batch, 2) + row[1:], row, row, tile, tile], [], name)


def join_kernel(edge, flow, s_ref, home, foreign, tiles, foreign_tiles, rows_ref, pair_ref, next_ref):
    lx, odd = s_ref[0], s_ref[2]
    wide = home.shape[2]
    row = lx if edge else 1 - lx
    rows_ref[:, lx, 0:wide, :] = home[:, row]
    rows_ref[:, lx, wide : wide + 8, :] = tiles[:, row]
    rows_ref[:, 1 - lx, 0:wide, :] = foreign[...]
    rows_ref[:, 1 - lx, wide : wide + 8, :] = foreign_tiles[:, 1 - row]
    pair_ref[...] = rows_ref[:, 1 - odd]
    next_ref[...] = rows_ref[:, odd]


def join(scalars, home, foreign, tiles, foreign_tiles, edge, name):
    batch, _, wide, chans = home.shape
    row = (batch, wide + 8, chans)
    return call(
        functools.partial(join_kernel, edge),
        scalars,
        [home, foreign, tiles, foreign_tiles],
        [(batch, 2) + row[1:], row, row],
        [],
        name,
    )


def chunk_rows_kernel(flow, s_ref, own, other, home, tiles, other_tiles, *others):
    lx, nc = s_ref[0], s_ref[1]
    part = others[0].shape[0]
    for row in range(2):
        wide_rows(nc, own[lx, :, row], other[lx, :, row], home.at[:, row])
        for chunk, out in enumerate(others):
            at = slice(chunk * part, (chunk + 1) * part)
            wide_rows(nc, own[1 - lx, at, row], other[1 - lx, at, row], out.at[:, row])
        for side, tile in zip((lx, 1 - lx), (tiles, other_tiles)):
            tile[:, row] = ends(nc, own[side, :, row], other[side, :, row])


def chunk_rows(scalars, own, other, name):
    _, batch, _, cols, chans = own.shape
    tile = (batch, 2, 8, chans)
    row = (2, 2 * cols, chans)
    return call(
        chunk_rows_kernel,
        scalars,
        [own, other],
        [(batch,) + row, tile, tile] + [(batch // CHUNKS,) + row] * CHUNKS,
        [],
        name,
    )


def cell_kernel(first, flow, s_ref, home, foreign, tiles, foreign_tiles, rows_ref, pair_ref, next_ref):
    lx, odd = s_ref[0], s_ref[2]
    part, _, wide, _ = foreign.shape
    at = slice(first, first + part)
    for row in range(2):
        for side, rows, ends_of in ((2 * lx, home[at, row], tiles), (2 - 2 * lx, foreign[:, row], foreign_tiles)):
            rows_ref[:, side + row, 0:wide, :] = rows
            rows_ref[:, side + row, wide : wide + 8, :] = ends_of[at, row]
    pair_ref[...] = rows_ref[:, 3 - 3 * odd]
    next_ref[...] = rows_ref[:, 3 * odd]
    flow.steps(part, lambda here, i: None)


def cell_rows(scalars, home, foreign, tiles, chunk, name):
    part, _, wide, chans = foreign.shape
    row = (part, wide + 8, chans)
    return call(
        functools.partial(cell_kernel, chunk * part),
        scalars,
        [home, foreign, *tiles],
        [Result(part, 4, *row[1:]), row, row],
        [],
        name,
    )


def row_of_parts(parts, row, at):
    edge, inner = parts
    return (edge if row in (0, 3) else inner)[at, 0 if row < 2 else 1]


def ring_row(values, pad, row, high, low):
    step, wide, chans = values.shape
    pad[row, :, 8 : 8 + wide, :] = values
    pad[row, :, 0:8, :] = values[:, wide - 8 : wide]
    pad[row, :, 8 + wide : 16 + wide, :] = values[:, 0:8]
    for tap in range(3):
        shifted = values if tap == 1 else pad[row, :, 7 + tap : 7 + tap + wide, :]
        at = (row * 3 + tap) * chans
        high[:, at : at + chans], low[:, at : at + chans] = split(shifted.reshape(step * wide, chans))


def put_weight(weight, turned, high, low):
    chans = weight.shape[1]
    nothing = jnp.zeros((chans, chans), BF16)
    for row in range(3):
        for tap in range(3):
            block = weight[(2 - row) * 3 + 2 - tap].T if turned else weight[row * 3 + tap]
            parts = split(block)
            for out in range(2):
                at = ((row + out) * 3 + tap) * chans
                for ref, part in zip((high, low), parts):
                    ref[at : at + chans, out * chans : (out + 1) * chans] = part
    for tap in range(3):
        for ref in (high, low):
            ref[(9 + tap) * chans : (10 + tap) * chans, 0:chans] = nothing
            ref[tap * chans : (tap + 1) * chans, chans : 2 * chans] = nothing


def pair_of_rows(pair, high, low, weight_high, weight_low):
    chans = weight_high.shape[1] // 2
    at = slice(pair * 6 * chans, (pair * 6 + 12) * chans)
    total = jnp.dot(high[:, at], weight_high[...], preferred_element_type=F32)
    total += jnp.dot(low[:, at], weight_high[...], preferred_element_type=F32)
    total += jnp.dot(high[:, at], weight_low[...], preferred_element_type=F32)
    return total[:, :chans], total[:, chans:]


def north_south(s_ref, pair, following, at):
    odd = s_ref[2] == 1
    first, second = pair[at], following[at]
    return jnp.where(odd, first, second), jnp.where(odd, second, first)


def put_edges(s_ref, top, bottom, pair_out, next_out, at):
    odd = s_ref[2] == 1
    pair_out[at] = jnp.where(odd, top, bottom)
    next_out[at] = jnp.where(odd, bottom, top)


def lanes(values):
    return jnp.sum(values.reshape(-1, 8, values.shape[-1]), axis=0)


def fold(total):
    return jnp.sum(total, axis=0, keepdims=True)


def add_moments(active, first, shift, sums, others):
    @pl.when(first)
    def _():
        mean = jnp.mean(active[0].reshape(-1, active[0].shape[-1]), axis=0, keepdims=True)
        shift[...] = jnp.broadcast_to(mean, shift.shape)
        sums[...] = jnp.zeros_like(sums)

    base = shift[0:1, :]
    for at, values in enumerate(active):
        distance = values - base
        sums[0] += lanes(distance)
        sums[1] += lanes(distance * distance)
        if others is not None:
            sums[2] += lanes(others[at])
            sums[3] += lanes(others[at] * distance)


def put_moments(out_ref, shift, sums, count, others):
    total, squares = fold(sums[0]), fold(sums[1])
    offset = total / count
    out_ref[...] = jnp.zeros_like(out_ref)
    out_ref[0:1, :] = shift[0:1, :] + offset
    out_ref[1:2, :] = squares - total * offset
    if others:
        weight = fold(sums[2])
        out_ref[2:3, :] = weight
        out_ref[3:4, :] = fold(sums[3]) - weight * offset


def conv_scratch(wide, chans):
    return [
        pltpu.VMEM((6, STEP, wide + 16, chans), F32),
        pltpu.VMEM((STEP * wide, 18 * chans), BF16),
        pltpu.VMEM((STEP * wide, 18 * chans), BF16),
        pltpu.VMEM((12 * chans, 2 * chans), BF16),
        pltpu.VMEM((12 * chans, 2 * chans), BF16),
    ]


def first_kernel(
    flow, s_ref, edge, inner, pair, following, weight, bias, z_ref, stat_ref,
    pad, high, low, weight_high, weight_low, shift, sums,
):
    batch, _, wide, _ = z_ref.shape
    own = wide - 8
    put_weight(weight, False, weight_high, weight_low)

    def step(at, i):
        north, south = north_south(s_ref, pair, following, at)
        for row in range(6):
            values = north if row == 0 else south if row == 5 else row_of_parts((edge, inner), row - 1, at)
            ring_row(values, pad, row, high, low)
        active = []
        for two in range(2):
            for total in pair_of_rows(two, high, low, weight_high, weight_low):
                z = (total + bias[0:1, :]).reshape(-1, wide, total.shape[-1])
                z_ref[at, len(active)] = z
                active.append(z[:, :own] * sigmoid(z[:, :own]))
        add_moments(active, i == 0, shift, sums, None)

    flow.steps(batch, step)
    put_moments(stat_ref, shift, sums, float(batch * 4 * own), False)


def first_conv(scalars, parts, halos, weight, bias):
    batch, _, wide, chans = parts[0].shape
    return call(
        first_kernel,
        scalars,
        parts + halos + (weight, bias),
        [Result(batch, 4, wide, chans), (8, chans)],
        conv_scratch(wide, chans) + [pltpu.VMEM((8, chans), F32), pltpu.VMEM((4, 8, chans), F32)],
        "conv_one",
    )


def first_halo_kernel(
    flow, s_ref, edge, pair, following, pair_inner, following_inner, weight, bias, north_ref, south_ref,
    pad, high, low, weight_high, weight_low,
):
    batch, wide, chans = north_ref.shape
    for tap in range(9):
        taps = slice(tap * chans, (tap + 1) * chans)
        weight_high[taps, :], weight_low[taps, :] = split(weight[tap])

    def step(at, i):
        north, south = north_south(s_ref, pair, following, at)
        far_north, far_south = north_south(s_ref, pair_inner, following_inner, at)
        rows = (far_north, north, edge[at, 0], edge[at, 1], south, far_south)
        for row, values in enumerate(rows):
            ring_row(values, pad, row, high, low)
        for side, ref in enumerate((north_ref, south_ref)):
            taps = slice(side * 9 * chans, (side + 1) * 9 * chans)
            total = jnp.dot(high[:, taps], weight_high[...], preferred_element_type=F32)
            total += jnp.dot(low[:, taps], weight_high[...], preferred_element_type=F32)
            total += jnp.dot(high[:, taps], weight_low[...], preferred_element_type=F32)
            ref[at] = (total + bias[0:1, :]).reshape(-1, wide, chans)

    flow.steps(batch, step)


def first_halo_conv(scalars, edge, halos, far_halos, weight, bias):
    batch, _, wide, chans = edge.shape
    return call(
        first_halo_kernel,
        scalars,
        [Stream(edge), *[Stream(a) for a in halos + far_halos], weight, bias],
        [(batch, wide, chans)] * 2,
        conv_scratch(wide, chans)[:3] + [pltpu.VMEM((9 * chans, chans), BF16)] * 2,
        "conv_one_halo",
    )


def hidden_row(s_ref, z1, north, south, coef, at, there, row):
    center, scale, offset = coef[0:1, :], coef[1:2, :], coef[2:3, :]
    values = north[there] if row == 0 else south[there] if row == 5 else z1[at, row - 1]
    hidden = (values * sigmoid(values) - center) * scale + offset
    if row in (0, 5):
        hidden = jnp.where(s_ref[3 if row == 0 else 4] == 1, 0.0, hidden)
    return hidden


def second_kernel(
    first, flow, s_ref, z1, g_rows, north, south, coef, weight, bias,
    z_ref, pair_out, next_out, stat_ref, pad, high, low, weight_high, weight_low, shift, sums,
):
    part, _, wide, _ = z_ref.shape
    own = wide - 8
    put_weight(weight, False, weight_high, weight_low)

    def step(at, i):
        there = pl.ds(i * STEP + first, STEP)
        for row in range(6):
            ring_row(hidden_row(s_ref, z1, north, south, coef, at, there, row), pad, row, high, low)
        active = []
        rows = []
        for two in range(2):
            for total in pair_of_rows(two, high, low, weight_high, weight_low):
                z = (total + bias[0:1, :]).reshape(-1, wide, total.shape[-1])
                z_ref[at, len(rows)] = z
                rows.append(z)
                active.append(z[:, :own] * sigmoid(z[:, :own]))
        put_edges(s_ref, rows[0], rows[3], pair_out, next_out, at)
        add_moments(active, i == 0, shift, sums, [g_rows[at, row, :own] for row in range(4)])

    flow.steps(part, step)
    put_moments(stat_ref, shift, sums, float(part * 4 * own), True)


def second_conv(scalars, z1, halos, g_rows, coef, weight, bias, chunk):
    part, _, wide, chans = g_rows.shape
    return call(
        functools.partial(second_kernel, chunk * part),
        scalars,
        [Stream(z1, chunk * part, part), Stream(g_rows), *halos, coef, weight, bias],
        [Result(part, 4, wide, chans), (part, wide, chans), (part, wide, chans), (8, chans)],
        conv_scratch(wide, chans) + [pltpu.VMEM((8, chans), F32), pltpu.VMEM((4, 8, chans), F32)],
        "conv_two",
    )


def put_pieces(s_ref, rows, home, other, at):
    lx = s_ref[0]
    for row in range(2):
        home[at, row] = rows[2 * lx + row]
        other[at, row] = rows[2 - 2 * lx + row]


def halves_kernel(flow, s_ref, home, foreign, out):
    cols = out.shape[3]
    there = pl.ds(pl.multiple_of((1 - s_ref[1]) * cols, cols), cols)
    for at, rows in enumerate((home, foreign)):
        for row in range(2):
            out[at, :, row] = rows[:, row, there, :]


def send_side(home, other):
    return home, permute(other, to_side)


def send_core(scalars, home, foreign, name):
    part, _, wide, chans = home.shape
    payload = call(halves_kernel, scalars, [home, foreign], [(2, part, 2, wide // 2, chans)], [], name)[0]
    return home, foreign, permute(payload, to_core)


def place_kernel(chunk, s_ref, home, foreign, core, *refs):
    out, sems = refs[-2:]
    lx, nc = s_ref[0], s_ref[1]
    part, cols = core.shape[1], core.shape[3]
    at = pl.ds(chunk * part, part)
    here = pl.ds(pl.multiple_of(nc * cols, cols), cols)
    copies = [
        pltpu.make_async_copy(home.at[:, :, here, :], out.at[lx, nc, at], sems.at[0]),
        pltpu.make_async_copy(foreign.at[:, :, here, :], out.at[1 - lx, nc, at], sems.at[1]),
        pltpu.make_async_copy(core.at[0], out.at[lx, 1 - nc, at], sems.at[2]),
        pltpu.make_async_copy(core.at[1], out.at[1 - lx, 1 - nc, at], sems.at[3]),
    ]
    for copy in copies:
        copy.start()
    for copy in copies:
        copy.wait()


def place(scalars, pieces, chunk, filled, name):
    _, part, rows_here, cols, chans = pieces[2].shape
    shape = (2, 2, part * CHUNKS, rows_here, cols, chans)
    earlier = [] if filled is None else [filled]
    return pl.pallas_call(
        functools.partial(place_kernel, chunk),
        in_specs=[SMEM] + [VMEM] * 3 + [HBM] * len(earlier),
        out_specs=HBM,
        out_shape=jax.ShapeDtypeStruct(shape, F32),
        scratch_shapes=[pltpu.SemaphoreType.DMA((4,))],
        input_output_aliases={4: 0} if earlier else {},
        compiler_params=pltpu.CompilerParams(vmem_limit_bytes=VMEM_LIMIT),
        name=name,
    )(scalars, *pieces, *earlier)


def silu_and_slope(z):
    sigma = sigmoid(z)
    return z * sigma, sigma * (1.0 + z * (1.0 - sigma))


def third_kernel(
    flow, s_ref, z2, g_rows, z1, x_edge, x_inner, pair, following, g_pair, g_following, coef, weight,
    dh_ref, dz_ref, pair_out, next_out, stat_ref, home, other,
    pad, high, low, weight_high, weight_low, sums, results,
):
    part, _, wide, _ = dh_ref.shape
    own = wide - 8
    center, inverse, scale = coef[0:1, :], coef[1:2, :], coef[2:3, :]
    mean_shift, mean_gain = coef[3:4, :], coef[4:5, :]
    center_one, inverse_one, shift_two = coef[5:6, :], coef[6:7, :], coef[7:8, :]
    put_weight(weight, True, weight_high, weight_low)
    sums[...] = jnp.zeros_like(sums)

    def step(at, i):
        north, south = north_south(s_ref, pair, following, at)
        g_north, g_south = north_south(s_ref, g_pair, g_following, at)
        for row in range(6):
            if row in (0, 5):
                z, g = (north, g_north) if row == 0 else (south, g_south)
            else:
                z, g = z2[at, row - 1], g_rows[at, row - 1]
            active, slope = silu_and_slope(z)
            distance = active - center
            dz = scale * (g - mean_shift - distance * inverse * mean_gain) * slope
            if row in (0, 5):
                dz = jnp.where(s_ref[3 if row == 0 else 4] == 1, 0.0, dz)
            else:
                dz_ref[at, row - 1] = dz[:, :own]
                sums[2] += lanes(dz[:, :own])
                x = row_of_parts((x_edge, x_inner), row - 1, at)
                results[row - 1] = x[:, :own] + (distance[:, :own] * scale + shift_two)
            ring_row(dz, pad, row, high, low)
        rows = []
        for two in range(2):
            for total in pair_of_rows(two, high, low, weight_high, weight_low):
                dh = total.reshape(-1, wide, total.shape[-1])
                row = len(rows)
                dh_ref[at, row] = dh
                rows.append(dh)
                z = z1[at, row, :own]
                sums[0] += lanes(dh[:, :own])
                sums[1] += lanes(dh[:, :own] * ((z * sigmoid(z) - center_one) * inverse_one))
        put_edges(s_ref, rows[0], rows[3], pair_out, next_out, at)
        put_pieces(s_ref, results, home, other, at)

    flow.steps(part, step)
    stat_ref[...] = jnp.zeros_like(stat_ref)
    for row in range(3):
        stat_ref[row : row + 1, :] = fold(sums[row])


def third_conv(scalars, z2, halos, g_rows, g_halos, z1, x_parts, coef, weight, chunk):
    part, _, wide, chans = z2.shape
    own = wide - 8
    first = chunk * part
    return call(
        third_kernel,
        scalars,
        [Stream(z2), Stream(g_rows)]
        + [Stream(a, first, part) for a in (z1,) + x_parts]
        + [*halos, *g_halos, coef, weight],
        [Result(part, 4, wide, chans), Result(part, 4, own, chans)]
        + [(part, wide, chans), (part, wide, chans), (8, chans), (part, 2, own, chans), (part, 2, own, chans)],
        conv_scratch(wide, chans) + [pltpu.VMEM((3, 8, chans), F32), pltpu.VMEM((4, STEP, own, chans), F32)],
        "conv_three",
    )


def slope_one(z, q, coef):
    center, inverse, scale = coef[0:1, :], coef[1:2, :], coef[2:3, :]
    mean_shift, mean_gain = coef[3:4, :], coef[4:5, :]
    active, slope = silu_and_slope(z)
    return scale * (q - mean_shift - (active - center) * inverse * mean_gain) * slope


def fourth_kernel(
    flow, s_ref, dh, z1, z_north, z_south, g_rows, pair, following, coef, weight,
    home, other, pad, high, low, weight_high, weight_low, results,
):
    part, _, wide, _ = dh.shape
    own = wide - 8
    put_weight(weight, True, weight_high, weight_low)

    def step(at, i):
        north, south = north_south(s_ref, pair, following, at)
        for row in range(6):
            if row in (0, 5):
                z, q = (z_north[at], north) if row == 0 else (z_south[at], south)
            else:
                z, q = z1[at, row - 1], dh[at, row - 1]
            dz = slope_one(z, q, coef)
            if row in (0, 5):
                dz = jnp.where(s_ref[3 if row == 0 else 4] == 1, 0.0, dz)
            ring_row(dz, pad, row, high, low)
        row = 0
        for two in range(2):
            for total in pair_of_rows(two, high, low, weight_high, weight_low):
                results[row] = g_rows[at, row, :own] + total.reshape(-1, wide, total.shape[-1])[:, :own]
                row += 1
        put_pieces(s_ref, results, home, other, at)

    flow.steps(part, step)


def fourth_conv(scalars, dh, halos, z1, z_halos, g_rows, coef, weight, chunk):
    part, _, wide, chans = dh.shape
    own = wide - 8
    return call(
        fourth_kernel,
        scalars,
        [Stream(dh)]
        + [Stream(a, chunk * part, part) for a in (z1,) + z_halos]
        + [Stream(g_rows), *halos, coef, weight],
        [(part, 2, own, chans)] * 2,
        conv_scratch(wide, chans) + [pltpu.VMEM((4, STEP, own, chans), F32)],
        "conv_four",
    )


def weight_step(rows, slopes, pad, high, low, total):
    own, chans = slopes[0].shape[1], slopes[0].shape[2]
    wide = own + 8
    for row, values in enumerate(rows):
        pad[row, :, 8 : 8 + wide, :] = values
        pad[row, :, 0:8, :] = values[:, own:wide]
        for tap in range(3):
            shifted = values[:, :own] if tap == 1 else pad[row, :, 7 + tap : 7 + tap + own, :]
            at = (row * 3 + tap) * chans
            high[:, at : at + chans], low[:, at : at + chans] = split(shifted.reshape(-1, chans))

    def product(left, right):
        return lax.dot_general(left, right, (((0,), (0,)), ((), ())), preferred_element_type=F32)

    sums = None
    for two in range(2):
        at = slice(two * 6 * chans, (two * 6 + 12) * chans)
        slope = jnp.concatenate([s.reshape(-1, chans) for s in slopes[2 * two : 2 * two + 2]], axis=1)
        slope_high, slope_low = split(slope)
        part = product(high[:, at], slope_high)
        part += product(low[:, at], slope_high)
        part += product(high[:, at], slope_low)
        sums = part if sums is None else sums + part
    total[...] += sums


SMALL = 32


def weight_end(out_ref, total, small, bias):
    chans = out_ref.shape[1]
    line = 3 * chans
    for row in range(3):
        out_ref[row * line : (row + 1) * line, :] = (
            total[row * line : (row + 1) * line, :chans] + total[(row + 1) * line : (row + 2) * line, chans:]
        )
    out_ref[3 * line :, :] = jnp.zeros((SMALL, chans), F32)
    out_ref[3 * line : 3 * line + 8, :] = small[...]
    if bias is not None:
        out_ref[3 * line : 3 * line + 1, :] = fold(bias[...])


def weight_scratch(own, chans):
    return [
        pltpu.VMEM((6, STEP, own + 16, chans), F32),
        pltpu.VMEM((STEP * own, 18 * chans), BF16),
        pltpu.VMEM((STEP * own, 18 * chans), BF16),
        pltpu.VMEM((12 * chans, 2 * chans), F32),
    ]


def weight_two_kernel(flow, s_ref, *refs):
    chunks = [refs[4 * chunk : 4 * chunk + 4] for chunk in range(CHUNKS)]
    coef, small, out_ref, *scratch = refs[4 * CHUNKS :]
    scratch[-1][...] = jnp.zeros_like(scratch[-1])
    for chunk, (z1, north, south, dz) in enumerate(chunks):

        def step(at, i):
            rows = [hidden_row(s_ref, z1, north, south, coef, at, at, row) for row in range(6)]
            weight_step(rows, [dz[at, row] for row in range(4)], *scratch)

        flow.steps(dz.shape[0], step, chunk)
    weight_end(out_ref, scratch[-1], small, None)


def weight_two_grad(scalars, z1, halos, coef, dz, small):
    part, _, own, chans = dz[0].shape
    streams = []
    for chunk in range(CHUNKS):
        streams += [Stream(a, chunk * part, part, chunk) for a in (z1,) + halos]
        streams += [Stream(dz[chunk], group=chunk)]
    return call(
        weight_two_kernel,
        scalars,
        streams + [coef, small],
        [(9 * chans + SMALL, chans)],
        weight_scratch(own, chans),
        "weight_two",
    )[0]


def weight_one_kernel(flow, s_ref, *refs):
    chunks = [refs[6 * chunk : 6 * chunk + 6] for chunk in range(CHUNKS)]
    coef, small, out_ref, bias, *scratch = refs[6 * CHUNKS :]
    bias[...] = jnp.zeros_like(bias)
    scratch[-1][...] = jnp.zeros_like(scratch[-1])
    for chunk, (edge, inner, pair, following, z1, dh) in enumerate(chunks):
        part, _, wide, _ = dh.shape
        own = wide - 8

        def step(at, i):
            north, south = north_south(s_ref, pair, following, at)
            rows = [north] + [row_of_parts((edge, inner), row, at) for row in range(4)] + [south]
            slopes = [slope_one(z1[at, row, :own], dh[at, row, :own], coef) for row in range(4)]
            for slope in slopes:
                bias[...] += lanes(slope)
            weight_step(rows, slopes, *scratch)

        flow.steps(part, step, chunk)
    weight_end(out_ref, scratch[-1], small, bias)


def weight_one_grad(scalars, parts, halos, dh, z1, coef, small):
    part, _, wide, chans = dh[0].shape
    streams = []
    for chunk in range(CHUNKS):
        streams += [Stream(a, chunk * part, part, chunk) for a in parts + halos + (z1,)]
        streams += [Stream(dh[chunk], group=chunk)]
    return call(
        weight_one_kernel,
        scalars,
        streams + [coef, small],
        [(9 * chans + SMALL, chans)],
        [pltpu.VMEM((8, chans), F32)] + weight_scratch(wide - 8, chans),
        "weight_one",
    )[0]


def rows_of(*vectors):
    filled = [jnp.reshape(v, (1, -1)) for v in vectors]
    if len(filled) < 8:
        filled.append(jnp.zeros((8 - len(filled), filled[0].shape[1]), F32))
    return jnp.concatenate(filled, axis=0)


def merge_moments(one, other, count):
    mean = 0.5 * (one[0] + other[0])
    gap = one[0] - other[0]
    squares = one[1] + other[1] + gap * gap * (0.5 * count)
    weight = one[2] + other[2]
    product = (one[3] + (one[0] - mean) * one[2]) + (other[3] + (other[0] - mean) * other[2])
    return rows_of(mean, squares, weight, product)


def all_moments(stats, here, *others):
    count = here
    partial = []
    for target in group_steps():
        stats = merge_moments(stats, permute(stats, target), count)
        if not partial and others:
            stats = after(stats, *others)
        partial.append(stats)
        count = 2.0 * count
    return partial


def all_sums(stats, *others):
    partial = []
    for target in group_steps():
        stats = stats + permute(stats, target)
        if not partial and others:
            stats = after(stats, *others)
        partial.append(stats)
    return partial


def quarters_kernel(flow, s_ref, value, own, *others):
    size = own.shape[0]
    here = 2 * s_ref[5] + s_ref[2]
    for bits, ref in zip((0, 2, 1, 3), (own,) + others):
        ref[...] = value[pl.ds(pl.multiple_of((here ^ bits) * size, 8), size), :]


def whole_kernel(flow, s_ref, own, *refs):
    others, out = refs[:-1], refs[-1]
    size = own.shape[0]
    here = 2 * s_ref[5] + s_ref[2]
    for bits, ref in zip((0, 2, 1, 3), (own,) + others):
        out[pl.ds(pl.multiple_of((here ^ bits) * size, 8), size), :] = ref[...]


def to_east_pair(row, col):
    return row ^ 2, col ^ 2


def sum_everywhere(scalars, one, two, lon, beside):
    west = lon % 2 == 0
    value = jnp.where(west, one, two) + permute(after(jnp.where(west, two, one), *beside[0]), to_core)
    size, chans = value.shape[0] // 4, value.shape[1]
    targets = (to_east, to_pair, to_east_pair)
    own, *others = call(quarters_kernel, scalars, [value], [(size, chans)] * 4, [], "quarters")
    others = [permute(v, target) for v, target in zip(others, targets)]
    own = after(own, *beside[1])
    own = (own + others[0]) + (others[1] + others[2])
    own = own + permute(own, to_side)
    last = beside[2](own)
    for target in group_steps()[2:]:
        own = own + permute(own, target)
    others = [permute(own, target) for target in targets]
    value = call(whole_kernel, scalars, [after(own, last, *beside[3]), *others], [(4 * size, chans)], [], "whole")[0]
    other = permute(value, to_core)
    return value, other


def shards(
    fields, weight_one, bias_one, gain_one, shift_one, weight_two, bias_two, gain_two, shift_two, cotangent
):
    parts_here, batch, rows_here, cols_here, chans = fields.shape
    lat, lon = lax.axis_index("lat"), lax.axis_index("lon")
    lats, lons = lax.axis_size("lat"), lax.axis_size("lon")
    assert (parts_here, rows_here, lons) == (4, 2, 4)
    here = float(batch * 4 * 2 * cols_here)
    members = float(lats * lons // 4)
    count = here * members
    pair = lat // 2
    scalars = jnp.stack([lat % 2, lon % 2, pair % 2, pair == 0, pair == lats // 2 - 1, lon // 2]).astype(jnp.int32)
    cells = fields.reshape((2, 2) + fields.shape[1:])
    slopes = cotangent.reshape((2, 2) + cotangent.shape[1:])
    taps_one = weight_one.reshape((9, chans, chans))
    taps_two = weight_two.reshape((9, chans, chans))

    other = pack(scalars, cells, True, "x_pack_other")
    core = permute(other, to_core)
    own = pack(scalars, after(cells, other), False, "x_pack_own")
    home, edge, inner, tiles, other_tiles = rows(scalars, own, core, "x_rows")
    edge = permute(edge, to_side)
    tiles = permute(tiles, to_east)
    foreign_tiles = permute(other_tiles, to_east_side)
    inner = permute(after(inner, tiles), to_side)
    x_edge, pair_row, next_row = join(scalars, home, edge, tiles, foreign_tiles, True, "x_edge")
    x_halos = exchange_rows(pair_row, next_row)
    slopes = after(slopes, x_edge)
    other = pack(scalars, slopes, True, "g_pack_other")
    core = permute(other, to_core)
    own = pack(scalars, after(slopes, other), False, "g_pack_own")
    g_home, g_tiles, g_other, *g_foreign = chunk_rows(scalars, own, core, "g_rows")
    g_foreign = [permute(part, to_side) for part in g_foreign]
    g_tiles = (permute(g_tiles, to_east), permute(g_other, to_east_side))
    x_inner, pair_row, next_row = join(scalars, after(home, g_home), inner, tiles, foreign_tiles, False, "x_inner")
    x_far = exchange_rows(pair_row, next_row)
    x_parts = (x_edge, x_inner)

    z1, stats = first_conv(scalars, x_parts, x_halos, taps_one, after(rows_of(bias_one), g_home))
    partial = all_moments(stats, here, *x_far, g_foreign[0])
    z1_halos = tuple(
        first_halo_conv(scalars, after(x_edge, partial[-2]), x_halos, x_far, taps_one, rows_of(bias_one))
    )
    g_rows, g_edges = [], []
    for chunk in range(CHUNKS):
        foreign = after(g_foreign[chunk], z1_halos[0])
        four, pair_row, next_row = cell_rows(scalars, g_home, foreign, g_tiles, chunk, "g_cell")
        g_rows.append(four)
        g_edges.append((pair_row, next_row))
    stats = partial[-1]
    center_one, spread_one = stats[0], stats[1] / count
    inv_one = lax.rsqrt(spread_one + EPSILON)

    coef_one = rows_of(center_one, gain_one * inv_one, shift_one)
    g_halos = [exchange_rows(after(top, coef_one), bottom) for top, bottom in g_edges]
    z2, z2_edges, parts, earlier = [], [], [], []
    for chunk in range(CHUNKS):
        z, pair_row, next_row, stats = second_conv(
            scalars, z1, z1_halos, g_rows[chunk], after(coef_one, *earlier), taps_two, rows_of(bias_two), chunk
        )
        earlier = [z, *g_halos[0]]
        z2.append(z)
        z2_edges.append((pair_row, next_row))
        parts.append(stats)
    z2_halos = [exchange_rows(*z2_edges[0])]
    stats = after(merge_moments(parts[0], parts[1], here / CHUNKS), *g_halos[1])
    partial = all_moments(stats, here, *z2_halos[0])
    z2_halos.append(exchange_rows(after(z2_edges[1][0], partial[-2]), z2_edges[1][1]))
    stats = partial[-1]
    center_two, spread_two, dshift_two = stats[0], stats[1] / count, stats[2]
    inv_two = lax.rsqrt(spread_two + EPSILON)
    dgain_two = stats[3] * inv_two

    coef = rows_of(
        center_two, inv_two, gain_two * inv_two, dshift_two / count, dgain_two / count, center_one, inv_one,
        shift_two,
    )
    dh1, dz2, dh1_edges, parts, output = [], [], [], [], []
    for chunk in range(CHUNKS):
        dh, dz, pair_row, next_row, stats, *pieces = third_conv(
            scalars, z2[chunk], z2_halos[chunk], g_rows[chunk], g_halos[chunk], z1, x_parts, after(coef, *dh1),
            taps_two, chunk,
        )
        dh1.append(dh)
        dz2.append(dz)
        dh1_edges.append((pair_row, next_row))
        parts.append(stats)
        output.append(send_side(*pieces))
    stats = parts[0] + parts[1]
    dbias_two = stats[2]
    dh1_halos = [exchange_rows(*dh1_edges[0])]
    partial = all_sums(stats, *dh1_halos[0])
    dh1_halos.append(exchange_rows(after(dh1_edges[1][0], partial[-2]), dh1_edges[1][1]))
    small = rows_of(dbias_two, dgain_two / members, dshift_two / members)
    grad_w2 = weight_two_grad(scalars, z1, z1_halos, after(coef_one, partial[-2]), dz2, small)
    dshift_one, dgain_one = partial[-1][0], partial[-1][1]

    coef = rows_of(center_one, inv_one, gain_one * inv_one, dshift_one / count, dgain_one / count)
    small = rows_of(jnp.zeros_like(dgain_one), dgain_one / members, dshift_one / members)

    def input_slope(chunk, coef):
        return fourth_conv(
            scalars, dh1[chunk], dh1_halos[chunk], z1, z1_halos, g_rows[chunk], coef, taps_one, chunk
        )

    pieces = input_slope(0, after(coef, grad_w2, output[0][1], output[1][1], *dh1_halos[1]))
    grad_w1 = weight_one_grad(scalars, x_parts, x_halos, dh1, z1, after(coef, pieces[0]), small)
    input_grad = [send_side(*pieces)]
    pieces = input_slope(1, after(coef, grad_w1))
    out_whole = None
    for chunk in range(CHUNKS):
        out_whole = place(scalars, send_core(scalars, *output[chunk], "output_halves"), chunk, out_whole, "output_place")
    def send_last(summed):
        input_grad.append(send_side(pieces[0], after(pieces[1], summed)))
        return input_grad[1][1]

    grad_whole = place(scalars, send_core(scalars, *input_grad[0], "grad_halves"), 0, None, "grad_place")
    beside = ([input_grad[0][1]], pieces[:1], send_last, [out_whole, grad_whole])
    one, two = sum_everywhere(scalars, grad_w1, grad_w2, lon, beside)
    many, west = 9 * chans, lon % 2 == 0
    sums = []
    for mine, its in ((one, two), (two, one)):
        sums.append(jnp.where(west, mine[:many], its[:many]))
        sums += [jnp.where(west, mine[many + row], its[many + row]) for row in range(3)]
    home, grad_whole = lax.optimization_barrier((input_grad[1][0], grad_whole))
    pieces = send_core(scalars, home, input_grad[1][1], "grad_halves")
    home, *sums = lax.optimization_barrier((home, *sums))
    pieces = (home,) + pieces[1:]
    grad_whole = place(scalars, pieces, 1, grad_whole, "grad_place")
    return (
        out_whole.reshape(fields.shape),
        grad_whole.reshape(fields.shape),
        sums[0].reshape(weight_one.shape),
        *sums[1:4],
        sums[4].reshape(weight_two.shape),
        *sums[5:8],
    )


def solution(mesh):
    field = P(None, None, "lat", "lon", None)
    return jax.shard_map(
        shards,
        mesh=mesh,
        in_specs=(field,) + (P(),) * 8 + (field,),
        out_specs=(field, field) + (P(),) * 8,
        check_vma=False,
    )
```

```python
import functools

import jax
import jax.numpy as jnp
from jax import lax
from jax.experimental import pallas as pl
from jax.experimental.pallas import tpu as pltpu
from jax.sharding import PartitionSpec as P


EPSILON = 1e-05
F32 = jnp.float32
BF16 = jnp.bfloat16
AXES = ("lat", "lon")
STEP = 2
VMEM_LIMIT = 32 << 20
CHUNKS = 2


def permute(value, target):
    rows, cols = lax.axis_size("lat"), lax.axis_size("lon")
    pairs = []
    for row in range(rows):
        for col in range(cols):
            to = target(row, col)
            if 0 <= to[0] < rows and 0 <= to[1] < cols:
                pairs.append((row * cols + col, to[0] * cols + to[1]))
    return lax.ppermute(value, AXES, pairs)


def to_core(row, col):
    return row, col ^ 1


def to_side(row, col):
    return row ^ 1, col


def to_east(row, col):
    return row, col ^ 2


def to_east_side(row, col):
    return row ^ 1, col ^ 2


def to_pair(row, col):
    return row ^ 2, col


def to_next(row, col):
    return (row + 2 if (row // 2) % 2 else row - 2), col


def group_steps():
    steps = []
    bit = 2
    while bit < lax.axis_size("lon"):
        steps.append(functools.partial(lambda bit, row, col: (row, col ^ bit), bit))
        bit *= 2
    bit = 2
    while bit < lax.axis_size("lat"):
        steps.append(functools.partial(lambda bit, row, col: (row ^ bit, col), bit))
        bit *= 2
    return steps


def exchange_rows(pair_row, next_row):
    return permute(pair_row, to_pair), permute(next_row, to_next)


def after(value, *others):
    return lax.optimization_barrier((value,) + others)[0]


def split(value):
    high = value.astype(BF16)
    return high, (value - high.astype(F32)).astype(BF16)


def sigmoid(value):
    return 1.0 / (1.0 + jnp.exp(-value))


VMEM = pl.BlockSpec(memory_space=pltpu.VMEM)
SMEM = pl.BlockSpec(memory_space=pltpu.SMEM)
HBM = pl.BlockSpec(memory_space=pltpu.HBM)


def in_hbm(array):
    return pltpu.with_memory_space_constraint(array, pltpu.HBM)


class Stream:
    def __init__(self, array, first=0, count=None, group=0):
        self.array = array
        self.first = first
        self.count = array.shape[0] if count is None else count
        self.group = group


class Result:
    def __init__(self, *shape):
        self.shape = shape


class Flow:
    def __init__(self, ins, outs, sems):
        self.ins, self.outs, self.sems = ins, outs, sems

    def copy_in(self, k, i):
        _, far, near, first = self.ins[k]
        source = far.at[pl.ds(first + i * STEP, STEP)]
        return pltpu.make_async_copy(source, near.at[pl.ds(i * STEP, STEP)], self.sems.at[k, i])

    def copy_out(self, k, i):
        far, near = self.outs[k]
        at = pl.ds(i * STEP, STEP)
        return pltpu.make_async_copy(near.at[at], far.at[at], self.sems.at[len(self.ins) + k, i])

    def start(self):
        for group in sorted({stream[0] for stream in self.ins}):
            members = [k for k, stream in enumerate(self.ins) if stream[0] == group]
            for i in range(max(self.ins[k][2].shape[0] for k in members) // STEP):
                for k in members:
                    self.copy_in(k, i).start()

    def steps(self, samples, body, group=0):
        def one(i, carry):
            for k, stream in enumerate(self.ins):
                if stream[0] == group:
                    self.copy_in(k, i).wait()
            body(pl.ds(pl.multiple_of(i * STEP, STEP), STEP), i)
            for k in range(len(self.outs)):
                self.copy_out(k, i).start()
            return carry

        lax.fori_loop(0, samples // STEP, one, 0)

    def finish(self):
        for k, (_, near) in enumerate(self.outs):
            for i in range(near.shape[0] // STEP):
                self.copy_out(k, i).wait()


def call(body, scalars, inputs, outputs, scratch, name):
    streams = [a for a in inputs if isinstance(a, Stream)]
    results = [o for o in outputs if isinstance(o, Result)]
    buffers = [pltpu.VMEM((a.count,) + a.array.shape[1:], F32) for a in streams]
    buffers += [pltpu.VMEM(o.shape, F32) for o in results]
    most = max([a.count // STEP for a in streams] + [o.shape[0] // STEP for o in results] + [1])

    def kernel(s_ref, *refs):
        refs = list(refs)
        in_refs, out_refs = refs[: len(inputs)], refs[len(inputs) : len(inputs) + len(outputs)]
        rest = refs[len(inputs) + len(outputs) :]
        near, rest = rest[: len(buffers)], rest[len(buffers) :]
        sems, rest = rest[0], rest[1:]
        ins, outs = [], []
        for at, a in enumerate(inputs):
            if isinstance(a, Stream):
                ins.append((a.group, in_refs[at], near[len(ins)], a.first))
                in_refs[at] = ins[-1][2]
        for at, o in enumerate(outputs):
            if isinstance(o, Result):
                outs.append((out_refs[at], near[len(ins) + len(outs)]))
                out_refs[at] = outs[-1][1]
        flow = Flow(ins, outs, sems)
        flow.start()
        body(flow, s_ref, *in_refs, *out_refs, *rest)
        flow.finish()

    return pl.pallas_call(
        kernel,
        in_specs=[SMEM] + [HBM if isinstance(a, Stream) else VMEM for a in inputs],
        out_specs=[HBM if isinstance(o, Result) else VMEM for o in outputs],
        out_shape=[pltpu.HBM(o.shape, F32) if isinstance(o, Result) else jax.ShapeDtypeStruct(o, F32) for o in outputs],
        scratch_shapes=buffers + [pltpu.SemaphoreType.DMA((max(len(buffers), 1), most))] + list(scratch),
        compiler_params=pltpu.CompilerParams(vmem_limit_bytes=VMEM_LIMIT),
        cost_estimate=pl.CostEstimate(flops=0, bytes_accessed=0, transcendentals=0),
        name=name,
    )(scalars, *[in_hbm(a.array) if isinstance(a, Stream) else a for a in inputs])


def pack_kernel(other_core, s_ref, field, out, sem):
    core = 1 - s_ref[1] if other_core else s_ref[1]
    copy = pltpu.make_async_copy(field.at[:, core], out, sem)
    copy.start()
    copy.wait()


def pack(scalars, field, other_core, name):
    return pl.pallas_call(
        functools.partial(pack_kernel, other_core),
        in_specs=[SMEM, HBM],
        out_specs=VMEM,
        out_shape=jax.ShapeDtypeStruct((2,) + field.shape[2:], F32),
        scratch_shapes=[pltpu.SemaphoreType.DMA],
        compiler_params=pltpu.CompilerParams(vmem_limit_bytes=VMEM_LIMIT),
        name=name,
    )(scalars, in_hbm(field))


def wide_rows(nc, own, other, out):
    half = own.shape[1]
    out[:, pl.ds(pl.multiple_of(nc * half, half), half), :] = own
    out[:, pl.ds(pl.multiple_of((1 - nc) * half, half), half), :] = other


def ends(nc, own, other):
    cols = own.shape[1]
    west, east = jnp.where(nc == 0, own[:, 0:8], other[:, 0:8]), jnp.where(nc == 0, other[:, -8:], own[:, -8:])
    del cols
    return jnp.concatenate([west[:, 0:4], east[:, 4:8]], axis=1)


def rows_kernel(flow, s_ref, own, other, home, edge, inner, *tiles):
    lx, nc = s_ref[0], s_ref[1]
    for row in range(2):
        wide_rows(nc, own[lx, :, row], other[lx, :, row], home.at[:, row])
    wide_rows(nc, own[1 - lx, :, lx], other[1 - lx, :, lx], edge)
    wide_rows(nc, own[1 - lx, :, 1 - lx], other[1 - lx, :, 1 - lx], inner)
    for part, tile in zip((lx, 1 - lx), tiles):
        for row in range(2):
            tile[:, row] = ends(nc, own[part, :, row], other[part, :, row])


def rows(scalars, own, other, name):
    _, batch, _, cols, chans = own.shape
    row = (batch, 2 * cols, chans)
    tile = (batch, 2, 8, chans)
    return call(rows_kernel, scalars, [own, other], [(batch, 2) + row[1:], row, row, tile, tile], [], name)


def join_kernel(edge, flow, s_ref, home, foreign, tiles, foreign_tiles, rows_ref, pair_ref, next_ref):
    lx, odd = s_ref[0], s_ref[2]
    wide = home.shape[2]
    row = lx if edge else 1 - lx
    rows_ref[:, lx, 0:wide, :] = home[:, row]
    rows_ref[:, lx, wide : wide + 8, :] = tiles[:, row]
    rows_ref[:, 1 - lx, 0:wide, :] = foreign[...]
    rows_ref[:, 1 - lx, wide : wide + 8, :] = foreign_tiles[:, 1 - row]
    pair_ref[...] = rows_ref[:, 1 - odd]
    next_ref[...] = rows_ref[:, odd]


def join(scalars, home, foreign, tiles, foreign_tiles, edge, name):
    batch, _, wide, chans = home.shape
    row = (batch, wide + 8, chans)
    return call(
        functools.partial(join_kernel, edge),
        scalars,
        [home, foreign, tiles, foreign_tiles],
        [(batch, 2) + row[1:], row, row],
        [],
        name,
    )


def chunk_rows_kernel(flow, s_ref, own, other, home, tiles, other_tiles, *others):
    lx, nc = s_ref[0], s_ref[1]
    part = others[0].shape[0]
    for row in range(2):
        wide_rows(nc, own[lx, :, row], other[lx, :, row], home.at[:, row])
        for chunk, out in enumerate(others):
            at = slice(chunk * part, (chunk + 1) * part)
            wide_rows(nc, own[1 - lx, at, row], other[1 - lx, at, row], out.at[:, row])
        for side, tile in zip((lx, 1 - lx), (tiles, other_tiles)):
            tile[:, row] = ends(nc, own[side, :, row], other[side, :, row])


def chunk_rows(scalars, own, other, name):
    _, batch, _, cols, chans = own.shape
    tile = (batch, 2, 8, chans)
    row = (2, 2 * cols, chans)
    return call(
        chunk_rows_kernel,
        scalars,
        [own, other],
        [(batch,) + row, tile, tile] + [(batch // CHUNKS,) + row] * CHUNKS,
        [],
        name,
    )


def cell_kernel(first, flow, s_ref, home, foreign, tiles, foreign_tiles, rows_ref, pair_ref, next_ref):
    lx, odd = s_ref[0], s_ref[2]
    part, _, wide, _ = foreign.shape
    at = slice(first, first + part)
    for row in range(2):
        for side, rows, ends_of in ((2 * lx, home[at, row], tiles), (2 - 2 * lx, foreign[:, row], foreign_tiles)):
            rows_ref[:, side + row, 0:wide, :] = rows
            rows_ref[:, side + row, wide : wide + 8, :] = ends_of[at, row]
    pair_ref[...] = rows_ref[:, 3 - 3 * odd]
    next_ref[...] = rows_ref[:, 3 * odd]
    flow.steps(part, lambda here, i: None)


def cell_rows(scalars, home, foreign, tiles, chunk, name):
    part, _, wide, chans = foreign.shape
    row = (part, wide + 8, chans)
    return call(
        functools.partial(cell_kernel, chunk * part),
        scalars,
        [home, foreign, *tiles],
        [Result(part, 4, *row[1:]), row, row],
        [],
        name,
    )


def row_of_parts(parts, row, at):
    edge, inner = parts
    return (edge if row in (0, 3) else inner)[at, 0 if row < 2 else 1]


def ring_row(values, pad, row, high, low):
    step, wide, chans = values.shape
    pad[row, :, 8 : 8 + wide, :] = values
    pad[row, :, 0:8, :] = values[:, wide - 8 : wide]
    pad[row, :, 8 + wide : 16 + wide, :] = values[:, 0:8]
    for tap in range(3):
        shifted = values if tap == 1 else pad[row, :, 7 + tap : 7 + tap + wide, :]
        at = (row * 3 + tap) * chans
        high[:, at : at + chans], low[:, at : at + chans] = split(shifted.reshape(step * wide, chans))


def put_weight(weight, turned, high, low):
    chans = weight.shape[1]
    nothing = jnp.zeros((chans, chans), BF16)
    for row in range(3):
        for tap in range(3):
            block = weight[(2 - row) * 3 + 2 - tap].T if turned else weight[row * 3 + tap]
            parts = split(block)
            for out in range(2):
                at = ((row + out) * 3 + tap) * chans
                for ref, part in zip((high, low), parts):
                    ref[at : at + chans, out * chans : (out + 1) * chans] = part
    for tap in range(3):
        for ref in (high, low):
            ref[(9 + tap) * chans : (10 + tap) * chans, 0:chans] = nothing
            ref[tap * chans : (tap + 1) * chans, chans : 2 * chans] = nothing


def pair_of_rows(pair, high, low, weight_high, weight_low):
    chans = weight_high.shape[1] // 2
    at = slice(pair * 6 * chans, (pair * 6 + 12) * chans)
    total = jnp.dot(high[:, at], weight_high[...], preferred_element_type=F32)
    total += jnp.dot(low[:, at], weight_high[...], preferred_element_type=F32)
    total += jnp.dot(high[:, at], weight_low[...], preferred_element_type=F32)
    return total[:, :chans], total[:, chans:]


def north_south(s_ref, pair, following, at):
    odd = s_ref[2] == 1
    first, second = pair[at], following[at]
    return jnp.where(odd, first, second), jnp.where(odd, second, first)


def put_edges(s_ref, top, bottom, pair_out, next_out, at):
    odd = s_ref[2] == 1
    pair_out[at] = jnp.where(odd, top, bottom)
    next_out[at] = jnp.where(odd, bottom, top)


def lanes(values):
    return jnp.sum(values.reshape(-1, 8, values.shape[-1]), axis=0)


def fold(total):
    return jnp.sum(total, axis=0, keepdims=True)


def add_moments(active, first, shift, sums, others):
    @pl.when(first)
    def _():
        mean = jnp.mean(active[0].reshape(-1, active[0].shape[-1]), axis=0, keepdims=True)
        shift[...] = jnp.broadcast_to(mean, shift.shape)
        sums[...] = jnp.zeros_like(sums)

    base = shift[0:1, :]
    for at, values in enumerate(active):
        distance = values - base
        sums[0] += lanes(distance)
        sums[1] += lanes(distance * distance)
        if others is not None:
            sums[2] += lanes(others[at])
            sums[3] += lanes(others[at] * distance)


def put_moments(out_ref, shift, sums, count, others):
    total, squares = fold(sums[0]), fold(sums[1])
    offset = total / count
    out_ref[...] = jnp.zeros_like(out_ref)
    out_ref[0:1, :] = shift[0:1, :] + offset
    out_ref[1:2, :] = squares - total * offset
    if others:
        weight = fold(sums[2])
        out_ref[2:3, :] = weight
        out_ref[3:4, :] = fold(sums[3]) - weight * offset


def conv_scratch(wide, chans):
    return [
        pltpu.VMEM((6, STEP, wide + 16, chans), F32),
        pltpu.VMEM((STEP * wide, 18 * chans), BF16),
        pltpu.VMEM((STEP * wide, 18 * chans), BF16),
        pltpu.VMEM((12 * chans, 2 * chans), BF16),
        pltpu.VMEM((12 * chans, 2 * chans), BF16),
    ]


def first_kernel(
    flow, s_ref, edge, inner, pair, following, weight, bias, z_ref, stat_ref,
    pad, high, low, weight_high, weight_low, shift, sums,
):
    batch, _, wide, _ = z_ref.shape
    own = wide - 8
    put_weight(weight, False, weight_high, weight_low)

    def step(at, i):
        north, south = north_south(s_ref, pair, following, at)
        for row in range(6):
            values = north if row == 0 else south if row == 5 else row_of_parts((edge, inner), row - 1, at)
            ring_row(values, pad, row, high, low)
        active = []
        for two in range(2):
            for total in pair_of_rows(two, high, low, weight_high, weight_low):
                z = (total + bias[0:1, :]).reshape(-1, wide, total.shape[-1])
                z_ref[at, len(active)] = z
                active.append(z[:, :own] * sigmoid(z[:, :own]))
        add_moments(active, i == 0, shift, sums, None)

    flow.steps(batch, step)
    put_moments(stat_ref, shift, sums, float(batch * 4 * own), False)


def first_conv(scalars, parts, halos, weight, bias):
    batch, _, wide, chans = parts[0].shape
    return call(
        first_kernel,
        scalars,
        parts + halos + (weight, bias),
        [Result(batch, 4, wide, chans), (8, chans)],
        conv_scratch(wide, chans) + [pltpu.VMEM((8, chans), F32), pltpu.VMEM((4, 8, chans), F32)],
        "conv_one",
    )


def first_halo_kernel(
    flow, s_ref, edge, pair, following, pair_inner, following_inner, weight, bias, north_ref, south_ref,
    pad, high, low, weight_high, weight_low,
):
    batch, wide, chans = north_ref.shape
    for tap in range(9):
        taps = slice(tap * chans, (tap + 1) * chans)
        weight_high[taps, :], weight_low[taps, :] = split(weight[tap])

    def step(at, i):
        north, south = north_south(s_ref, pair, following, at)
        far_north, far_south = north_south(s_ref, pair_inner, following_inner, at)
        rows = (far_north, north, edge[at, 0], edge[at, 1], south, far_south)
        for row, values in enumerate(rows):
            ring_row(values, pad, row, high, low)
        for side, ref in enumerate((north_ref, south_ref)):
            taps = slice(side * 9 * chans, (side + 1) * 9 * chans)
            total = jnp.dot(high[:, taps], weight_high[...], preferred_element_type=F32)
            total += jnp.dot(low[:, taps], weight_high[...], preferred_element_type=F32)
            total += jnp.dot(high[:, taps], weight_low[...], preferred_element_type=F32)
            ref[at] = (total + bias[0:1, :]).reshape(-1, wide, chans)

    flow.steps(batch, step)


def first_halo_conv(scalars, edge, halos, far_halos, weight, bias):
    batch, _, wide, chans = edge.shape
    return call(
        first_halo_kernel,
        scalars,
        [Stream(edge), *[Stream(a) for a in halos + far_halos], weight, bias],
        [(batch, wide, chans)] * 2,
        conv_scratch(wide, chans)[:3] + [pltpu.VMEM((9 * chans, chans), BF16)] * 2,
        "conv_one_halo",
    )


def hidden_row(s_ref, z1, north, south, coef, at, there, row):
    center, scale, offset = coef[0:1, :], coef[1:2, :], coef[2:3, :]
    values = north[there] if row == 0 else south[there] if row == 5 else z1[at, row - 1]
    hidden = (values * sigmoid(values) - center) * scale + offset
    if row in (0, 5):
        hidden = jnp.where(s_ref[3 if row == 0 else 4] == 1, 0.0, hidden)
    return hidden


def second_kernel(
    first, flow, s_ref, z1, g_rows, north, south, coef, weight, bias,
    z_ref, pair_out, next_out, stat_ref, pad, high, low, weight_high, weight_low, shift, sums,
):
    part, _, wide, _ = z_ref.shape
    own = wide - 8
    put_weight(weight, False, weight_high, weight_low)

    def step(at, i):
        there = pl.ds(i * STEP + first, STEP)
        for row in range(6):
            ring_row(hidden_row(s_ref, z1, north, south, coef, at, there, row), pad, row, high, low)
        active = []
        rows = []
        for two in range(2):
            for total in pair_of_rows(two, high, low, weight_high, weight_low):
                z = (total + bias[0:1, :]).reshape(-1, wide, total.shape[-1])
                z_ref[at, len(rows)] = z
                rows.append(z)
                active.append(z[:, :own] * sigmoid(z[:, :own]))
        put_edges(s_ref, rows[0], rows[3], pair_out, next_out, at)
        add_moments(active, i == 0, shift, sums, [g_rows[at, row, :own] for row in range(4)])

    flow.steps(part, step)
    put_moments(stat_ref, shift, sums, float(part * 4 * own), True)


def second_conv(scalars, z1, halos, g_rows, coef, weight, bias, chunk):
    part, _, wide, chans = g_rows.shape
    return call(
        functools.partial(second_kernel, chunk * part),
        scalars,
        [Stream(z1, chunk * part, part), Stream(g_rows), *halos, coef, weight, bias],
        [Result(part, 4, wide, chans), (part, wide, chans), (part, wide, chans), (8, chans)],
        conv_scratch(wide, chans) + [pltpu.VMEM((8, chans), F32), pltpu.VMEM((4, 8, chans), F32)],
        "conv_two",
    )


def put_pieces(s_ref, rows, home, other, at):
    lx = s_ref[0]
    for row in range(2):
        home[at, row] = rows[2 * lx + row]
        other[at, row] = rows[2 - 2 * lx + row]


def halves_kernel(flow, s_ref, home, foreign, out):
    cols = out.shape[3]
    there = pl.ds(pl.multiple_of((1 - s_ref[1]) * cols, cols), cols)
    for at, rows in enumerate((home, foreign)):
        for row in range(2):
            out[at, :, row] = rows[:, row, there, :]


def send_side(home, other):
    return home, permute(other, to_side)


def send_core(scalars, home, foreign, name):
    part, _, wide, chans = home.shape
    payload = call(halves_kernel, scalars, [home, foreign], [(2, part, 2, wide // 2, chans)], [], name)[0]
    return home, foreign, permute(payload, to_core)


def place_kernel(chunk, s_ref, home, foreign, core, *refs):
    out, sems = refs[-2:]
    lx, nc = s_ref[0], s_ref[1]
    part, cols = core.shape[1], core.shape[3]
    at = pl.ds(chunk * part, part)
    here = pl.ds(pl.multiple_of(nc * cols, cols), cols)
    copies = [
        pltpu.make_async_copy(home.at[:, :, here, :], out.at[lx, nc, at], sems.at[0]),
        pltpu.make_async_copy(foreign.at[:, :, here, :], out.at[1 - lx, nc, at], sems.at[1]),
        pltpu.make_async_copy(core.at[0], out.at[lx, 1 - nc, at], sems.at[2]),
        pltpu.make_async_copy(core.at[1], out.at[1 - lx, 1 - nc, at], sems.at[3]),
    ]
    for copy in copies:
        copy.start()
    for copy in copies:
        copy.wait()


def place(scalars, pieces, chunk, filled, name):
    _, part, rows_here, cols, chans = pieces[2].shape
    shape = (2, 2, part * CHUNKS, rows_here, cols, chans)
    earlier = [] if filled is None else [filled]
    return pl.pallas_call(
        functools.partial(place_kernel, chunk),
        in_specs=[SMEM] + [VMEM] * 3 + [HBM] * len(earlier),
        out_specs=HBM,
        out_shape=jax.ShapeDtypeStruct(shape, F32),
        scratch_shapes=[pltpu.SemaphoreType.DMA((4,))],
        input_output_aliases={4: 0} if earlier else {},
        compiler_params=pltpu.CompilerParams(vmem_limit_bytes=VMEM_LIMIT),
        name=name,
    )(scalars, *pieces, *earlier)


def silu_and_slope(z):
    sigma = sigmoid(z)
    return z * sigma, sigma * (1.0 + z * (1.0 - sigma))


def third_kernel(
    flow, s_ref, z2, g_rows, z1, x_edge, x_inner, pair, following, g_pair, g_following, coef, weight,
    dh_ref, dz_ref, pair_out, next_out, stat_ref, home, other,
    pad, high, low, weight_high, weight_low, sums, results,
):
    part, _, wide, _ = dh_ref.shape
    own = wide - 8
    center, inverse, scale = coef[0:1, :], coef[1:2, :], coef[2:3, :]
    mean_shift, mean_gain = coef[3:4, :], coef[4:5, :]
    center_one, inverse_one, shift_two = coef[5:6, :], coef[6:7, :], coef[7:8, :]
    put_weight(weight, True, weight_high, weight_low)
    sums[...] = jnp.zeros_like(sums)

    def step(at, i):
        north, south = north_south(s_ref, pair, following, at)
        g_north, g_south = north_south(s_ref, g_pair, g_following, at)
        for row in range(6):
            if row in (0, 5):
                z, g = (north, g_north) if row == 0 else (south, g_south)
            else:
                z, g = z2[at, row - 1], g_rows[at, row - 1]
            active, slope = silu_and_slope(z)
            distance = active - center
            dz = scale * (g - mean_shift - distance * inverse * mean_gain) * slope
            if row in (0, 5):
                dz = jnp.where(s_ref[3 if row == 0 else 4] == 1, 0.0, dz)
            else:
                dz_ref[at, row - 1] = dz[:, :own]
                sums[2] += lanes(dz[:, :own])
                x = row_of_parts((x_edge, x_inner), row - 1, at)
                results[row - 1] = x[:, :own] + (distance[:, :own] * scale + shift_two)
            ring_row(dz, pad, row, high, low)
        rows = []
        for two in range(2):
            for total in pair_of_rows(two, high, low, weight_high, weight_low):
                dh = total.reshape(-1, wide, total.shape[-1])
                row = len(rows)
                dh_ref[at, row] = dh
                rows.append(dh)
                z = z1[at, row, :own]
                sums[0] += lanes(dh[:, :own])
                sums[1] += lanes(dh[:, :own] * ((z * sigmoid(z) - center_one) * inverse_one))
        put_edges(s_ref, rows[0], rows[3], pair_out, next_out, at)
        put_pieces(s_ref, results, home, other, at)

    flow.steps(part, step)
    stat_ref[...] = jnp.zeros_like(stat_ref)
    for row in range(3):
        stat_ref[row : row + 1, :] = fold(sums[row])


def third_conv(scalars, z2, halos, g_rows, g_halos, z1, x_parts, coef, weight, chunk):
    part, _, wide, chans = z2.shape
    own = wide - 8
    first = chunk * part
    return call(
        third_kernel,
        scalars,
        [Stream(z2), Stream(g_rows)]
        + [Stream(a, first, part) for a in (z1,) + x_parts]
        + [*halos, *[Stream(a) for a in g_halos], coef, weight],
        [Result(part, 4, wide, chans), Result(part, 4, own, chans)]
        + [(part, wide, chans), (part, wide, chans), (8, chans), (part, 2, own, chans), (part, 2, own, chans)],
        conv_scratch(wide, chans) + [pltpu.VMEM((3, 8, chans), F32), pltpu.VMEM((4, STEP, own, chans), F32)],
        "conv_three",
    )


def slope_one(z, q, coef):
    center, inverse, scale = coef[0:1, :], coef[1:2, :], coef[2:3, :]
    mean_shift, mean_gain = coef[3:4, :], coef[4:5, :]
    active, slope = silu_and_slope(z)
    return scale * (q - mean_shift - (active - center) * inverse * mean_gain) * slope


def fourth_kernel(
    flow, s_ref, dh, z1, z_north, z_south, g_rows, pair, following, coef, weight,
    home, other, pad, high, low, weight_high, weight_low, results,
):
    part, _, wide, _ = dh.shape
    own = wide - 8
    put_weight(weight, True, weight_high, weight_low)

    def step(at, i):
        north, south = north_south(s_ref, pair, following, at)
        for row in range(6):
            if row in (0, 5):
                z, q = (z_north[at], north) if row == 0 else (z_south[at], south)
            else:
                z, q = z1[at, row - 1], dh[at, row - 1]
            dz = slope_one(z, q, coef)
            if row in (0, 5):
                dz = jnp.where(s_ref[3 if row == 0 else 4] == 1, 0.0, dz)
            ring_row(dz, pad, row, high, low)
        row = 0
        for two in range(2):
            for total in pair_of_rows(two, high, low, weight_high, weight_low):
                results[row] = g_rows[at, row, :own] + total.reshape(-1, wide, total.shape[-1])[:, :own]
                row += 1
        put_pieces(s_ref, results, home, other, at)

    flow.steps(part, step)


def fourth_conv(scalars, dh, halos, z1, z_halos, g_rows, coef, weight, chunk):
    part, _, wide, chans = dh.shape
    own = wide - 8
    return call(
        fourth_kernel,
        scalars,
        [Stream(dh)]
        + [Stream(a, chunk * part, part) for a in (z1,) + z_halos]
        + [Stream(g_rows), *[Stream(a) for a in halos], coef, weight],
        [(part, 2, own, chans)] * 2,
        conv_scratch(wide, chans) + [pltpu.VMEM((4, STEP, own, chans), F32)],
        "conv_four",
    )


def weight_step(rows, slopes, pad, high, low, total):
    own, chans = slopes[0].shape[1], slopes[0].shape[2]
    wide = own + 8
    for row, values in enumerate(rows):
        pad[row, :, 8 : 8 + wide, :] = values
        pad[row, :, 0:8, :] = values[:, own:wide]
        for tap in range(3):
            shifted = values[:, :own] if tap == 1 else pad[row, :, 7 + tap : 7 + tap + own, :]
            at = (row * 3 + tap) * chans
            high[:, at : at + chans], low[:, at : at + chans] = split(shifted.reshape(-1, chans))

    def product(left, right):
        return lax.dot_general(left, right, (((0,), (0,)), ((), ())), preferred_element_type=F32)

    sums = None
    for two in range(2):
        at = slice(two * 6 * chans, (two * 6 + 12) * chans)
        slope = jnp.concatenate([s.reshape(-1, chans) for s in slopes[2 * two : 2 * two + 2]], axis=1)
        slope_high, slope_low = split(slope)
        part = product(high[:, at], slope_high)
        part += product(low[:, at], slope_high)
        part += product(high[:, at], slope_low)
        sums = part if sums is None else sums + part
    total[...] += sums


SMALL = 32


def weight_end(out_ref, total, small, bias):
    chans = out_ref.shape[1]
    line = 3 * chans
    for row in range(3):
        out_ref[row * line : (row + 1) * line, :] = (
            total[row * line : (row + 1) * line, :chans] + total[(row + 1) * line : (row + 2) * line, chans:]
        )
    out_ref[3 * line :, :] = jnp.zeros((SMALL, chans), F32)
    out_ref[3 * line : 3 * line + 8, :] = small[...]
    if bias is not None:
        out_ref[3 * line : 3 * line + 1, :] = fold(bias[...])


def weight_scratch(own, chans):
    return [
        pltpu.VMEM((6, STEP, own + 16, chans), F32),
        pltpu.VMEM((STEP * own, 18 * chans), BF16),
        pltpu.VMEM((STEP * own, 18 * chans), BF16),
        pltpu.VMEM((12 * chans, 2 * chans), F32),
    ]


def weight_two_kernel(flow, s_ref, *refs):
    chunks = [refs[4 * chunk : 4 * chunk + 4] for chunk in range(CHUNKS)]
    coef, small, out_ref, *scratch = refs[4 * CHUNKS :]
    scratch[-1][...] = jnp.zeros_like(scratch[-1])
    for chunk, (z1, north, south, dz) in enumerate(chunks):

        def step(at, i):
            rows = [hidden_row(s_ref, z1, north, south, coef, at, at, row) for row in range(6)]
            weight_step(rows, [dz[at, row] for row in range(4)], *scratch)

        flow.steps(dz.shape[0], step, chunk)
    weight_end(out_ref, scratch[-1], small, None)


def weight_two_grad(scalars, z1, halos, coef, dz, small):
    part, _, own, chans = dz[0].shape
    streams = []
    for chunk in range(CHUNKS):
        streams += [Stream(a, chunk * part, part, chunk) for a in (z1,) + halos]
        streams += [Stream(dz[chunk], group=chunk)]
    return call(
        weight_two_kernel,
        scalars,
        streams + [coef, small],
        [(9 * chans + SMALL, chans)],
        weight_scratch(own, chans),
        "weight_two",
    )[0]


def weight_one_kernel(flow, s_ref, *refs):
    chunks = [refs[6 * chunk : 6 * chunk + 6] for chunk in range(CHUNKS)]
    coef, small, out_ref, bias, *scratch = refs[6 * CHUNKS :]
    bias[...] = jnp.zeros_like(bias)
    scratch[-1][...] = jnp.zeros_like(scratch[-1])
    for chunk, (edge, inner, pair, following, z1, dh) in enumerate(chunks):
        part, _, wide, _ = dh.shape
        own = wide - 8

        def step(at, i):
            north, south = north_south(s_ref, pair, following, at)
            rows = [north] + [row_of_parts((edge, inner), row, at) for row in range(4)] + [south]
            slopes = [slope_one(z1[at, row, :own], dh[at, row, :own], coef) for row in range(4)]
            for slope in slopes:
                bias[...] += lanes(slope)
            weight_step(rows, slopes, *scratch)

        flow.steps(part, step, chunk)
    weight_end(out_ref, scratch[-1], small, bias)


def weight_one_grad(scalars, parts, halos, dh, z1, coef, small):
    part, _, wide, chans = dh[0].shape
    streams = []
    for chunk in range(CHUNKS):
        streams += [Stream(a, chunk * part, part, chunk) for a in parts + halos + (z1,)]
        streams += [Stream(dh[chunk], group=chunk)]
    return call(
        weight_one_kernel,
        scalars,
        streams + [coef, small],
        [(9 * chans + SMALL, chans)],
        [pltpu.VMEM((8, chans), F32)] + weight_scratch(wide - 8, chans),
        "weight_one",
    )[0]


def rows_of(*vectors):
    filled = [jnp.reshape(v, (1, -1)) for v in vectors]
    if len(filled) < 8:
        filled.append(jnp.zeros((8 - len(filled), filled[0].shape[1]), F32))
    return jnp.concatenate(filled, axis=0)


def merge_moments(one, other, count):
    mean = 0.5 * (one[0] + other[0])
    gap = one[0] - other[0]
    squares = one[1] + other[1] + gap * gap * (0.5 * count)
    weight = one[2] + other[2]
    product = (one[3] + (one[0] - mean) * one[2]) + (other[3] + (other[0] - mean) * other[2])
    return rows_of(mean, squares, weight, product)


def all_moments(stats, here, *others):
    count = here
    partial = []
    for target in group_steps():
        stats = merge_moments(stats, permute(stats, target), count)
        if not partial and others:
            stats = after(stats, *others)
        partial.append(stats)
        count = 2.0 * count
    return partial


def all_sums(stats, *others):
    partial = []
    for target in group_steps():
        stats = stats + permute(stats, target)
        if not partial and others:
            stats = after(stats, *others)
        partial.append(stats)
    return partial


def quarters_kernel(flow, s_ref, value, own, *others):
    size = own.shape[0]
    here = 2 * s_ref[5] + s_ref[2]
    for bits, ref in zip((0, 2, 1, 3), (own,) + others):
        ref[...] = value[pl.ds(pl.multiple_of((here ^ bits) * size, 8), size), :]


def whole_kernel(flow, s_ref, own, *refs):
    others, out = refs[:-1], refs[-1]
    size = own.shape[0]
    here = 2 * s_ref[5] + s_ref[2]
    for bits, ref in zip((0, 2, 1, 3), (own,) + others):
        out[pl.ds(pl.multiple_of((here ^ bits) * size, 8), size), :] = ref[...]


def to_east_pair(row, col):
    return row ^ 2, col ^ 2


def sum_everywhere(scalars, one, two, lon, beside):
    west = lon % 2 == 0
    value = jnp.where(west, one, two) + permute(after(jnp.where(west, two, one), *beside[0]), to_core)
    size, chans = value.shape[0] // 4, value.shape[1]
    targets = (to_east, to_pair, to_east_pair)
    own, *others = call(quarters_kernel, scalars, [value], [(size, chans)] * 4, [], "quarters")
    others = [permute(v, target) for v, target in zip(others, targets)]
    own = after(own, *beside[1])
    own = (own + others[0]) + (others[1] + others[2])
    own = own + permute(own, to_side)
    last = beside[2](own)
    for target in group_steps()[2:]:
        own = own + permute(own, target)
    others = [permute(own, target) for target in targets]
    value = call(whole_kernel, scalars, [after(own, last, *beside[3]), *others], [(4 * size, chans)], [], "whole")[0]
    other = permute(value, to_core)
    return value, other


def shards(
    fields, weight_one, bias_one, gain_one, shift_one, weight_two, bias_two, gain_two, shift_two, cotangent
):
    parts_here, batch, rows_here, cols_here, chans = fields.shape
    lat, lon = lax.axis_index("lat"), lax.axis_index("lon")
    lats, lons = lax.axis_size("lat"), lax.axis_size("lon")
    assert (parts_here, rows_here, lons) == (4, 2, 4)
    here = float(batch * 4 * 2 * cols_here)
    members = float(lats * lons // 4)
    count = here * members
    pair = lat // 2
    scalars = jnp.stack([lat % 2, lon % 2, pair % 2, pair == 0, pair == lats // 2 - 1, lon // 2]).astype(jnp.int32)
    cells = fields.reshape((2, 2) + fields.shape[1:])
    slopes = cotangent.reshape((2, 2) + cotangent.shape[1:])
    taps_one = weight_one.reshape((9, chans, chans))
    taps_two = weight_two.reshape((9, chans, chans))

    other = pack(scalars, cells, True, "x_pack_other")
    core = permute(other, to_core)
    own = pack(scalars, after(cells, other), False, "x_pack_own")
    home, edge, inner, tiles, other_tiles = rows(scalars, own, core, "x_rows")
    edge = permute(edge, to_side)
    tiles = permute(tiles, to_east)
    foreign_tiles = permute(other_tiles, to_east_side)
    inner = permute(after(inner, foreign_tiles), to_side)
    x_edge, pair_row, next_row = join(scalars, home, edge, tiles, foreign_tiles, True, "x_edge")
    x_halos = exchange_rows(pair_row, next_row)
    slopes = after(slopes, x_edge)
    other = pack(scalars, slopes, True, "g_pack_other")
    core = permute(other, to_core)
    own = pack(scalars, after(slopes, other), False, "g_pack_own")
    g_home, g_tiles, g_other, *g_foreign = chunk_rows(scalars, own, core, "g_rows")
    g_foreign = [permute(part, to_side) for part in g_foreign]
    g_tiles = (permute(g_tiles, to_east), permute(g_other, to_east_side))
    x_inner, pair_row, next_row = join(scalars, after(home, g_home), inner, tiles, foreign_tiles, False, "x_inner")
    x_far = exchange_rows(pair_row, next_row)
    x_parts = (x_edge, x_inner)

    z1, stats = first_conv(scalars, x_parts, x_halos, taps_one, after(rows_of(bias_one), g_home))
    partial = all_moments(stats, here, *x_far, g_foreign[0])
    z1_halos = tuple(
        first_halo_conv(scalars, after(x_edge, partial[-2]), x_halos, x_far, taps_one, rows_of(bias_one))
    )
    g_rows, g_edges = [], []
    for chunk in range(CHUNKS):
        foreign = after(g_foreign[chunk], z1_halos[0])
        four, pair_row, next_row = cell_rows(scalars, g_home, foreign, g_tiles, chunk, "g_cell")
        g_rows.append(four)
        g_edges.append((pair_row, next_row))
    stats = partial[-1]
    center_one, spread_one = stats[0], stats[1] / count
    inv_one = lax.rsqrt(spread_one + EPSILON)

    coef_one = rows_of(center_one, gain_one * inv_one, shift_one)
    g_halos = [exchange_rows(after(top, coef_one), bottom) for top, bottom in g_edges]
    z2, z2_edges, parts, earlier = [], [], [], []
    for chunk in range(CHUNKS):
        z, pair_row, next_row, stats = second_conv(
            scalars, z1, z1_halos, g_rows[chunk], after(coef_one, *earlier), taps_two, rows_of(bias_two), chunk
        )
        earlier = [z, *g_halos[0]]
        z2.append(z)
        z2_edges.append((pair_row, next_row))
        parts.append(stats)
    z2_halos = [exchange_rows(*z2_edges[0])]
    stats = after(merge_moments(parts[0], parts[1], here / CHUNKS), *g_halos[1])
    partial = all_moments(stats, here, *z2_halos[0])
    z2_halos.append(exchange_rows(after(z2_edges[1][0], partial[-2]), z2_edges[1][1]))
    stats = partial[-1]
    center_two, spread_two, dshift_two = stats[0], stats[1] / count, stats[2]
    inv_two = lax.rsqrt(spread_two + EPSILON)
    dgain_two = stats[3] * inv_two

    coef = rows_of(
        center_two, inv_two, gain_two * inv_two, dshift_two / count, dgain_two / count, center_one, inv_one,
        shift_two,
    )
    dh1, dz2, dh1_edges, parts, output = [], [], [], [], []
    for chunk in range(CHUNKS):
        dh, dz, pair_row, next_row, stats, *pieces = third_conv(
            scalars, z2[chunk], z2_halos[chunk], g_rows[chunk], g_halos[chunk], z1, x_parts, after(coef, *dh1),
            taps_two, chunk,
        )
        dh1.append(dh)
        dz2.append(dz)
        dh1_edges.append((pair_row, next_row))
        parts.append(stats)
        output.append(send_side(*pieces))
    stats = parts[0] + parts[1]
    dbias_two = stats[2]
    dh1_halos = [exchange_rows(*dh1_edges[0])]
    partial = all_sums(stats, *dh1_halos[0])
    dh1_halos.append(exchange_rows(after(dh1_edges[1][0], partial[-2]), dh1_edges[1][1]))
    small = rows_of(dbias_two, dgain_two / members, dshift_two / members)
    grad_w2 = weight_two_grad(scalars, z1, z1_halos, after(coef_one, partial[-2]), dz2, small)
    dshift_one, dgain_one = partial[-1][0], partial[-1][1]

    coef = rows_of(center_one, inv_one, gain_one * inv_one, dshift_one / count, dgain_one / count)
    small = rows_of(jnp.zeros_like(dgain_one), dgain_one / members, dshift_one / members)

    def input_slope(chunk, coef):
        return fourth_conv(
            scalars, dh1[chunk], dh1_halos[chunk], z1, z1_halos, g_rows[chunk], coef, taps_one, chunk
        )

    pieces = input_slope(0, after(coef, grad_w2, output[0][1], output[1][1], *dh1_halos[1]))
    grad_w1 = weight_one_grad(scalars, x_parts, x_halos, dh1, z1, after(coef, pieces[0]), small)
    input_grad = [send_side(*pieces)]
    pieces = input_slope(1, after(coef, grad_w1))
    out_whole = None
    for chunk in range(CHUNKS):
        out_whole = place(scalars, send_core(scalars, *output[chunk], "output_halves"), chunk, out_whole, "output_place")
    def send_last(summed):
        input_grad.append(send_side(pieces[0], after(pieces[1], summed)))
        return input_grad[1][1]

    grad_whole = place(scalars, send_core(scalars, *input_grad[0], "grad_halves"), 0, None, "grad_place")
    beside = ([input_grad[0][1]], pieces[:1], send_last, [out_whole, grad_whole])
    one, two = sum_everywhere(scalars, grad_w1, grad_w2, lon, beside)
    many, west = 9 * chans, lon % 2 == 0
    sums = []
    for mine, its in ((one, two), (two, one)):
        sums.append(jnp.where(west, mine[:many], its[:many]))
        sums += [jnp.where(west, mine[many + row], its[many + row]) for row in range(3)]
    home, grad_whole = lax.optimization_barrier((input_grad[1][0], grad_whole))
    pieces = send_core(scalars, home, input_grad[1][1], "grad_halves")
    home, *sums = lax.optimization_barrier((home, *sums))
    pieces = (home,) + pieces[1:]
    grad_whole = place(scalars, pieces, 1, grad_whole, "grad_place")
    return (
        out_whole.reshape(fields.shape),
        grad_whole.reshape(fields.shape),
        sums[0].reshape(weight_one.shape),
        *sums[1:4],
        sums[4].reshape(weight_two.shape),
        *sums[5:8],
    )


def solution(mesh):
    field = P(None, None, "lat", "lon", None)
    return jax.shard_map(
        shards,
        mesh=mesh,
        in_specs=(field,) + (P(),) * 8 + (field,),
        out_specs=(field, field) + (P(),) * 8,
        check_vma=False,
    )
```

```python
import functools

import jax
import jax.numpy as jnp
from jax import lax
from jax.experimental import pallas as pl
from jax.experimental.pallas import tpu as pltpu
from jax.sharding import PartitionSpec as P


EPSILON = 1e-05
F32 = jnp.float32
BF16 = jnp.bfloat16
AXES = ("lat", "lon")
STEP = 2
VMEM_LIMIT = 32 << 20
CHUNKS = 2


def permute(value, target):
    rows, cols = lax.axis_size("lat"), lax.axis_size("lon")
    pairs = []
    for row in range(rows):
        for col in range(cols):
            to = target(row, col)
            if 0 <= to[0] < rows and 0 <= to[1] < cols:
                pairs.append((row * cols + col, to[0] * cols + to[1]))
    return lax.ppermute(value, AXES, pairs)


def to_core(row, col):
    return row, col ^ 1


def to_side(row, col):
    return row ^ 1, col


def to_east(row, col):
    return row, col ^ 2


def to_east_side(row, col):
    return row ^ 1, col ^ 2


def to_pair(row, col):
    return row ^ 2, col


def to_next(row, col):
    return (row + 2 if (row // 2) % 2 else row - 2), col


def group_steps():
    steps = []
    bit = 2
    while bit < lax.axis_size("lon"):
        steps.append(functools.partial(lambda bit, row, col: (row, col ^ bit), bit))
        bit *= 2
    bit = 2
    while bit < lax.axis_size("lat"):
        steps.append(functools.partial(lambda bit, row, col: (row ^ bit, col), bit))
        bit *= 2
    return steps


def exchange_rows(pair_row, next_row):
    return permute(pair_row, to_pair), permute(next_row, to_next)


def after(value, *others):
    return lax.optimization_barrier((value,) + others)[0]


def split(value):
    high = value.astype(BF16)
    return high, (value - high.astype(F32)).astype(BF16)


def sigmoid(value):
    return 1.0 / (1.0 + jnp.exp(-value))


VMEM = pl.BlockSpec(memory_space=pltpu.VMEM)
SMEM = pl.BlockSpec(memory_space=pltpu.SMEM)
HBM = pl.BlockSpec(memory_space=pltpu.HBM)


def in_hbm(array):
    return pltpu.with_memory_space_constraint(array, pltpu.HBM)


class Stream:
    def __init__(self, array, first=0, count=None, group=0):
        self.array = array
        self.first = first
        self.count = array.shape[0] if count is None else count
        self.group = group


class Result:
    def __init__(self, *shape):
        self.shape = shape


class Flow:
    def __init__(self, ins, outs, sems):
        self.ins, self.outs, self.sems = ins, outs, sems

    def copy_in(self, k, i):
        _, far, near, first = self.ins[k]
        source = far.at[pl.ds(first + i * STEP, STEP)]
        return pltpu.make_async_copy(source, near.at[pl.ds(i * STEP, STEP)], self.sems.at[k, i])

    def copy_out(self, k, i):
        far, near = self.outs[k]
        at = pl.ds(i * STEP, STEP)
        return pltpu.make_async_copy(near.at[at], far.at[at], self.sems.at[len(self.ins) + k, i])

    def start(self):
        for group in sorted({stream[0] for stream in self.ins}):
            members = [k for k, stream in enumerate(self.ins) if stream[0] == group]
            for i in range(max(self.ins[k][2].shape[0] for k in members) // STEP):
                for k in members:
                    self.copy_in(k, i).start()

    def steps(self, samples, body, group=0):
        def one(i, carry):
            for k, stream in enumerate(self.ins):
                if stream[0] == group:
                    self.copy_in(k, i).wait()
            body(pl.ds(pl.multiple_of(i * STEP, STEP), STEP), i)
            for k in range(len(self.outs)):
                self.copy_out(k, i).start()
            return carry

        lax.fori_loop(0, samples // STEP, one, 0)

    def finish(self):
        for k, (_, near) in enumerate(self.outs):
            for i in range(near.shape[0] // STEP):
                self.copy_out(k, i).wait()


def call(body, scalars, inputs, outputs, scratch, name):
    streams = [a for a in inputs if isinstance(a, Stream)]
    results = [o for o in outputs if isinstance(o, Result)]
    buffers = [pltpu.VMEM((a.count,) + a.array.shape[1:], F32) for a in streams]
    buffers += [pltpu.VMEM(o.shape, F32) for o in results]
    most = max([a.count // STEP for a in streams] + [o.shape[0] // STEP for o in results] + [1])

    def kernel(s_ref, *refs):
        refs = list(refs)
        in_refs, out_refs = refs[: len(inputs)], refs[len(inputs) : len(inputs) + len(outputs)]
        rest = refs[len(inputs) + len(outputs) :]
        near, rest = rest[: len(buffers)], rest[len(buffers) :]
        sems, rest = rest[0], rest[1:]
        ins, outs = [], []
        for at, a in enumerate(inputs):
            if isinstance(a, Stream):
                ins.append((a.group, in_refs[at], near[len(ins)], a.first))
                in_refs[at] = ins[-1][2]
        for at, o in enumerate(outputs):
            if isinstance(o, Result):
                outs.append((out_refs[at], near[len(ins) + len(outs)]))
                out_refs[at] = outs[-1][1]
        flow = Flow(ins, outs, sems)
        flow.start()
        body(flow, s_ref, *in_refs, *out_refs, *rest)
        flow.finish()

    return pl.pallas_call(
        kernel,
        in_specs=[SMEM] + [HBM if isinstance(a, Stream) else VMEM for a in inputs],
        out_specs=[HBM if isinstance(o, Result) else VMEM for o in outputs],
        out_shape=[pltpu.HBM(o.shape, F32) if isinstance(o, Result) else jax.ShapeDtypeStruct(o, F32) for o in outputs],
        scratch_shapes=buffers + [pltpu.SemaphoreType.DMA((max(len(buffers), 1), most))] + list(scratch),
        compiler_params=pltpu.CompilerParams(vmem_limit_bytes=VMEM_LIMIT),
        cost_estimate=pl.CostEstimate(flops=0, bytes_accessed=0, transcendentals=0),
        name=name,
    )(scalars, *[in_hbm(a.array) if isinstance(a, Stream) else a for a in inputs])


def pack_kernel(other_core, s_ref, field, out, sem):
    core = 1 - s_ref[1] if other_core else s_ref[1]
    copy = pltpu.make_async_copy(field.at[:, core], out, sem)
    copy.start()
    copy.wait()


def pack(scalars, field, other_core, name):
    return pl.pallas_call(
        functools.partial(pack_kernel, other_core),
        in_specs=[SMEM, HBM],
        out_specs=VMEM,
        out_shape=jax.ShapeDtypeStruct((2,) + field.shape[2:], F32),
        scratch_shapes=[pltpu.SemaphoreType.DMA],
        compiler_params=pltpu.CompilerParams(vmem_limit_bytes=VMEM_LIMIT),
        name=name,
    )(scalars, in_hbm(field))


def wide_rows(nc, own, other, out):
    half = own.shape[1]
    out[:, pl.ds(pl.multiple_of(nc * half, half), half), :] = own
    out[:, pl.ds(pl.multiple_of((1 - nc) * half, half), half), :] = other


def ends(nc, own, other):
    cols = own.shape[1]
    west, east = jnp.where(nc == 0, own[:, 0:8], other[:, 0:8]), jnp.where(nc == 0, other[:, -8:], own[:, -8:])
    del cols
    return jnp.concatenate([west[:, 0:4], east[:, 4:8]], axis=1)


def rows_kernel(flow, s_ref, own, other, home, edge, inner, *tiles):
    lx, nc = s_ref[0], s_ref[1]
    for row in range(2):
        wide_rows(nc, own[lx, :, row], other[lx, :, row], home.at[:, row])
    wide_rows(nc, own[1 - lx, :, lx], other[1 - lx, :, lx], edge)
    wide_rows(nc, own[1 - lx, :, 1 - lx], other[1 - lx, :, 1 - lx], inner)
    for part, tile in zip((lx, 1 - lx), tiles):
        for row in range(2):
            tile[:, row] = ends(nc, own[part, :, row], other[part, :, row])


def rows(scalars, own, other, name):
    _, batch, _, cols, chans = own.shape
    row = (batch, 2 * cols, chans)
    tile = (batch, 2, 8, chans)
    return call(rows_kernel, scalars, [own, other], [(batch, 2) + row[1:], row, row, tile, tile], [], name)


def join_kernel(edge, flow, s_ref, home, foreign, tiles, foreign_tiles, rows_ref, pair_ref, next_ref):
    lx, odd = s_ref[0], s_ref[2]
    wide = home.shape[2]
    row = lx if edge else 1 - lx
    rows_ref[:, lx, 0:wide, :] = home[:, row]
    rows_ref[:, lx, wide : wide + 8, :] = tiles[:, row]
    rows_ref[:, 1 - lx, 0:wide, :] = foreign[...]
    rows_ref[:, 1 - lx, wide : wide + 8, :] = foreign_tiles[:, 1 - row]
    pair_ref[...] = rows_ref[:, 1 - odd]
    next_ref[...] = rows_ref[:, odd]


def join(scalars, home, foreign, tiles, foreign_tiles, edge, name):
    batch, _, wide, chans = home.shape
    row = (batch, wide + 8, chans)
    return call(
        functools.partial(join_kernel, edge),
        scalars,
        [home, foreign, tiles, foreign_tiles],
        [(batch, 2) + row[1:], row, row],
        [],
        name,
    )


def chunk_rows_kernel(flow, s_ref, own, other, home, tiles, other_tiles, *others):
    lx, nc = s_ref[0], s_ref[1]
    part = others[0].shape[0]
    for row in range(2):
        wide_rows(nc, own[lx, :, row], other[lx, :, row], home.at[:, row])
        for chunk, out in enumerate(others):
            at = slice(chunk * part, (chunk + 1) * part)
            wide_rows(nc, own[1 - lx, at, row], other[1 - lx, at, row], out.at[:, row])
        for side, tile in zip((lx, 1 - lx), (tiles, other_tiles)):
            tile[:, row] = ends(nc, own[side, :, row], other[side, :, row])


def chunk_rows(scalars, own, other, name):
    _, batch, _, cols, chans = own.shape
    tile = (batch, 2, 8, chans)
    row = (2, 2 * cols, chans)
    return call(
        chunk_rows_kernel,
        scalars,
        [own, other],
        [(batch,) + row, tile, tile] + [(batch // CHUNKS,) + row] * CHUNKS,
        [],
        name,
    )


def cell_kernel(first, flow, s_ref, home, foreign, tiles, foreign_tiles, rows_ref, pair_ref, next_ref):
    lx, odd = s_ref[0], s_ref[2]
    part, _, wide, _ = foreign.shape
    at = slice(first, first + part)
    for row in range(2):
        for side, rows, ends_of in ((2 * lx, home[at, row], tiles), (2 - 2 * lx, foreign[:, row], foreign_tiles)):
            rows_ref[:, side + row, 0:wide, :] = rows
            rows_ref[:, side + row, wide : wide + 8, :] = ends_of[at, row]
    pair_ref[...] = rows_ref[:, 3 - 3 * odd]
    next_ref[...] = rows_ref[:, 3 * odd]
    flow.steps(part, lambda here, i: None)


def cell_rows(scalars, home, foreign, tiles, chunk, name):
    part, _, wide, chans = foreign.shape
    row = (part, wide + 8, chans)
    return call(
        functools.partial(cell_kernel, chunk * part),
        scalars,
        [home, foreign, *tiles],
        [Result(part, 4, *row[1:]), row, row],
        [],
        name,
    )


def row_of_parts(parts, row, at):
    edge, inner = parts
    return (edge if row in (0, 3) else inner)[at, 0 if row < 2 else 1]


def ring_row(values, pad, row, high, low):
    step, wide, chans = values.shape
    pad[row, :, 8 : 8 + wide, :] = values
    pad[row, :, 0:8, :] = values[:, wide - 8 : wide]
    pad[row, :, 8 + wide : 16 + wide, :] = values[:, 0:8]
    for tap in range(3):
        shifted = values if tap == 1 else pad[row, :, 7 + tap : 7 + tap + wide, :]
        at = (row * 3 + tap) * chans
        high[:, at : at + chans], low[:, at : at + chans] = split(shifted.reshape(step * wide, chans))


def put_weight(weight, turned, high, low):
    chans = weight.shape[1]
    nothing = jnp.zeros((chans, chans), BF16)
    for row in range(3):
        for tap in range(3):
            block = weight[(2 - row) * 3 + 2 - tap].T if turned else weight[row * 3 + tap]
            parts = split(block)
            for out in range(2):
                at = ((row + out) * 3 + tap) * chans
                for ref, part in zip((high, low), parts):
                    ref[at : at + chans, out * chans : (out + 1) * chans] = part
    for tap in range(3):
        for ref in (high, low):
            ref[(9 + tap) * chans : (10 + tap) * chans, 0:chans] = nothing
            ref[tap * chans : (tap + 1) * chans, chans : 2 * chans] = nothing


def pair_of_rows(pair, high, low, weight_high, weight_low):
    chans = weight_high.shape[1] // 2
    at = slice(pair * 6 * chans, (pair * 6 + 12) * chans)
    total = jnp.dot(high[:, at], weight_high[...], preferred_element_type=F32)
    total += jnp.dot(low[:, at], weight_high[...], preferred_element_type=F32)
    total += jnp.dot(high[:, at], weight_low[...], preferred_element_type=F32)
    return total[:, :chans], total[:, chans:]


def north_south(s_ref, pair, following, at):
    odd = s_ref[2] == 1
    first, second = pair[at], following[at]
    return jnp.where(odd, first, second), jnp.where(odd, second, first)


def put_edges(s_ref, top, bottom, pair_out, next_out, at):
    odd = s_ref[2] == 1
    pair_out[at] = jnp.where(odd, top, bottom)
    next_out[at] = jnp.where(odd, bottom, top)


def lanes(values):
    return jnp.sum(values.reshape(-1, 8, values.shape[-1]), axis=0)


def fold(total):
    return jnp.sum(total, axis=0, keepdims=True)


def add_moments(active, first, shift, sums, others):
    @pl.when(first)
    def _():
        mean = jnp.mean(active[0].reshape(-1, active[0].shape[-1]), axis=0, keepdims=True)
        shift[...] = jnp.broadcast_to(mean, shift.shape)
        sums[...] = jnp.zeros_like(sums)

    base = shift[0:1, :]
    for at, values in enumerate(active):
        distance = values - base
        sums[0] += lanes(distance)
        sums[1] += lanes(distance * distance)
        if others is not None:
            sums[2] += lanes(others[at])
            sums[3] += lanes(others[at] * distance)


def put_moments(out_ref, shift, sums, count, others):
    total, squares = fold(sums[0]), fold(sums[1])
    offset = total / count
    out_ref[...] = jnp.zeros_like(out_ref)
    out_ref[0:1, :] = shift[0:1, :] + offset
    out_ref[1:2, :] = squares - total * offset
    if others:
        weight = fold(sums[2])
        out_ref[2:3, :] = weight
        out_ref[3:4, :] = fold(sums[3]) - weight * offset


def conv_scratch(wide, chans):
    return [
        pltpu.VMEM((6, STEP, wide + 16, chans), F32),
        pltpu.VMEM((STEP * wide, 18 * chans), BF16),
        pltpu.VMEM((STEP * wide, 18 * chans), BF16),
        pltpu.VMEM((12 * chans, 2 * chans), BF16),
        pltpu.VMEM((12 * chans, 2 * chans), BF16),
    ]


def first_kernel(
    flow, s_ref, edge, inner, pair, following, weight, bias, z_ref, stat_ref,
    pad, high, low, weight_high, weight_low, shift, sums,
):
    batch, _, wide, _ = z_ref.shape
    own = wide - 8
    put_weight(weight, False, weight_high, weight_low)

    def step(at, i):
        north, south = north_south(s_ref, pair, following, at)
        for row in range(6):
            values = north if row == 0 else south if row == 5 else row_of_parts((edge, inner), row - 1, at)
            ring_row(values, pad, row, high, low)
        active = []
        for two in range(2):
            for total in pair_of_rows(two, high, low, weight_high, weight_low):
                z = (total + bias[0:1, :]).reshape(-1, wide, total.shape[-1])
                z_ref[at, len(active)] = z
                active.append(z[:, :own] * sigmoid(z[:, :own]))
        add_moments(active, i == 0, shift, sums, None)

    flow.steps(batch, step)
    put_moments(stat_ref, shift, sums, float(batch * 4 * own), False)


def first_conv(scalars, parts, halos, weight, bias):
    batch, _, wide, chans = parts[0].shape
    return call(
        first_kernel,
        scalars,
        parts + halos + (weight, bias),
        [Result(batch, 4, wide, chans), (8, chans)],
        conv_scratch(wide, chans) + [pltpu.VMEM((8, chans), F32), pltpu.VMEM((4, 8, chans), F32)],
        "conv_one",
    )


def first_halo_kernel(
    flow, s_ref, edge, pair, following, pair_inner, following_inner, weight, bias, north_ref, south_ref,
    pad, high, low, weight_high, weight_low,
):
    batch, wide, chans = north_ref.shape
    for tap in range(9):
        taps = slice(tap * chans, (tap + 1) * chans)
        weight_high[taps, :], weight_low[taps, :] = split(weight[tap])

    def step(at, i):
        north, south = north_south(s_ref, pair, following, at)
        far_north, far_south = north_south(s_ref, pair_inner, following_inner, at)
        rows = (far_north, north, edge[at, 0], edge[at, 1], south, far_south)
        for row, values in enumerate(rows):
            ring_row(values, pad, row, high, low)
        for side, ref in enumerate((north_ref, south_ref)):
            taps = slice(side * 9 * chans, (side + 1) * 9 * chans)
            total = jnp.dot(high[:, taps], weight_high[...], preferred_element_type=F32)
            total += jnp.dot(low[:, taps], weight_high[...], preferred_element_type=F32)
            total += jnp.dot(high[:, taps], weight_low[...], preferred_element_type=F32)
            ref[at] = (total + bias[0:1, :]).reshape(-1, wide, chans)

    flow.steps(batch, step)


def first_halo_conv(scalars, edge, halos, far_halos, weight, bias):
    batch, _, wide, chans = edge.shape
    return call(
        first_halo_kernel,
        scalars,
        [Stream(edge), *[Stream(a) for a in halos + far_halos], weight, bias],
        [(batch, wide, chans)] * 2,
        conv_scratch(wide, chans)[:3] + [pltpu.VMEM((9 * chans, chans), BF16)] * 2,
        "conv_one_halo",
    )


def hidden_row(s_ref, z1, north, south, coef, at, there, row):
    center, scale, offset = coef[0:1, :], coef[1:2, :], coef[2:3, :]
    values = north[there] if row == 0 else south[there] if row == 5 else z1[at, row - 1]
    hidden = (values * sigmoid(values) - center) * scale + offset
    if row in (0, 5):
        hidden = jnp.where(s_ref[3 if row == 0 else 4] == 1, 0.0, hidden)
    return hidden


def second_kernel(
    first, flow, s_ref, z1, g_rows, north, south, coef, weight, bias,
    z_ref, pair_out, next_out, stat_ref, pad, high, low, weight_high, weight_low, shift, sums,
):
    part, _, wide, _ = z_ref.shape
    own = wide - 8
    put_weight(weight, False, weight_high, weight_low)

    def step(at, i):
        there = pl.ds(i * STEP + first, STEP)
        for row in range(6):
            ring_row(hidden_row(s_ref, z1, north, south, coef, at, there, row), pad, row, high, low)
        active = []
        rows = []
        for two in range(2):
            for total in pair_of_rows(two, high, low, weight_high, weight_low):
                z = (total + bias[0:1, :]).reshape(-1, wide, total.shape[-1])
                z_ref[at, len(rows)] = z
                rows.append(z)
                active.append(z[:, :own] * sigmoid(z[:, :own]))
        put_edges(s_ref, rows[0], rows[3], pair_out, next_out, at)
        add_moments(active, i == 0, shift, sums, [g_rows[at, row, :own] for row in range(4)])

    flow.steps(part, step)
    put_moments(stat_ref, shift, sums, float(part * 4 * own), True)


def second_conv(scalars, z1, halos, g_rows, coef, weight, bias, chunk):
    part, _, wide, chans = g_rows.shape
    return call(
        functools.partial(second_kernel, chunk * part),
        scalars,
        [Stream(z1, chunk * part, part), Stream(g_rows), *halos, coef, weight, bias],
        [Result(part, 4, wide, chans), (part, wide, chans), (part, wide, chans), (8, chans)],
        conv_scratch(wide, chans) + [pltpu.VMEM((8, chans), F32), pltpu.VMEM((4, 8, chans), F32)],
        "conv_two",
    )


def put_pieces(s_ref, rows, home, other, at):
    lx = s_ref[0]
    for row in range(2):
        home[at, row] = rows[2 * lx + row]
        other[at, row] = rows[2 - 2 * lx + row]


def halves_kernel(flow, s_ref, home, foreign, out):
    cols = out.shape[3]
    there = pl.ds(pl.multiple_of((1 - s_ref[1]) * cols, cols), cols)
    for at, rows in enumerate((home, foreign)):
        for row in range(2):
            out[at, :, row] = rows[:, row, there, :]


def send_side(home, other):
    return home, permute(other, to_side)


def send_core(scalars, home, foreign, name):
    part, _, wide, chans = home.shape
    payload = call(halves_kernel, scalars, [home, foreign], [(2, part, 2, wide // 2, chans)], [], name)[0]
    return home, foreign, permute(payload, to_core)


def place_kernel(chunk, s_ref, home, foreign, core, *refs):
    out, sems = refs[-2:]
    lx, nc = s_ref[0], s_ref[1]
    part, cols = core.shape[1], core.shape[3]
    at = pl.ds(chunk * part, part)
    here = pl.ds(pl.multiple_of(nc * cols, cols), cols)
    copies = [
        pltpu.make_async_copy(home.at[:, :, here, :], out.at[lx, nc, at], sems.at[0]),
        pltpu.make_async_copy(foreign.at[:, :, here, :], out.at[1 - lx, nc, at], sems.at[1]),
        pltpu.make_async_copy(core.at[0], out.at[lx, 1 - nc, at], sems.at[2]),
        pltpu.make_async_copy(core.at[1], out.at[1 - lx, 1 - nc, at], sems.at[3]),
    ]
    for copy in copies:
        copy.start()
    for copy in copies:
        copy.wait()


def place(scalars, pieces, chunk, filled, name):
    _, part, rows_here, cols, chans = pieces[2].shape
    shape = (2, 2, part * CHUNKS, rows_here, cols, chans)
    earlier = [] if filled is None else [filled]
    return pl.pallas_call(
        functools.partial(place_kernel, chunk),
        in_specs=[SMEM] + [VMEM] * 3 + [HBM] * len(earlier),
        out_specs=HBM,
        out_shape=jax.ShapeDtypeStruct(shape, F32),
        scratch_shapes=[pltpu.SemaphoreType.DMA((4,))],
        input_output_aliases={4: 0} if earlier else {},
        compiler_params=pltpu.CompilerParams(vmem_limit_bytes=VMEM_LIMIT),
        name=name,
    )(scalars, *pieces, *earlier)


def silu_and_slope(z):
    sigma = sigmoid(z)
    return z * sigma, sigma * (1.0 + z * (1.0 - sigma))


def third_kernel(
    flow, s_ref, z2, g_rows, z1, x_edge, x_inner, pair, following, g_pair, g_following, coef, weight,
    dh_ref, dz_ref, pair_out, next_out, stat_ref, home, other,
    pad, high, low, weight_high, weight_low, sums, results,
):
    part, _, wide, _ = dh_ref.shape
    own = wide - 8
    center, inverse, scale = coef[0:1, :], coef[1:2, :], coef[2:3, :]
    mean_shift, mean_gain = coef[3:4, :], coef[4:5, :]
    center_one, inverse_one, shift_two = coef[5:6, :], coef[6:7, :], coef[7:8, :]
    put_weight(weight, True, weight_high, weight_low)
    sums[...] = jnp.zeros_like(sums)

    def step(at, i):
        north, south = north_south(s_ref, pair, following, at)
        g_north, g_south = north_south(s_ref, g_pair, g_following, at)
        for row in range(6):
            if row in (0, 5):
                z, g = (north, g_north) if row == 0 else (south, g_south)
            else:
                z, g = z2[at, row - 1], g_rows[at, row - 1]
            active, slope = silu_and_slope(z)
            distance = active - center
            dz = scale * (g - mean_shift - distance * inverse * mean_gain) * slope
            if row in (0, 5):
                dz = jnp.where(s_ref[3 if row == 0 else 4] == 1, 0.0, dz)
            else:
                dz_ref[at, row - 1] = dz[:, :own]
                sums[2] += lanes(dz[:, :own])
                x = row_of_parts((x_edge, x_inner), row - 1, at)
                results[row - 1] = x[:, :own] + (distance[:, :own] * scale + shift_two)
            ring_row(dz, pad, row, high, low)
        rows = []
        for two in range(2):
            for total in pair_of_rows(two, high, low, weight_high, weight_low):
                dh = total.reshape(-1, wide, total.shape[-1])
                row = len(rows)
                dh_ref[at, row] = dh
                rows.append(dh)
                z = z1[at, row, :own]
                sums[0] += lanes(dh[:, :own])
                sums[1] += lanes(dh[:, :own] * ((z * sigmoid(z) - center_one) * inverse_one))
        put_edges(s_ref, rows[0], rows[3], pair_out, next_out, at)
        put_pieces(s_ref, results, home, other, at)

    flow.steps(part, step)
    stat_ref[...] = jnp.zeros_like(stat_ref)
    for row in range(3):
        stat_ref[row : row + 1, :] = fold(sums[row])


def third_conv(scalars, z2, halos, g_rows, g_halos, z1, x_parts, coef, weight, chunk):
    part, _, wide, chans = z2.shape
    own = wide - 8
    first = chunk * part
    return call(
        third_kernel,
        scalars,
        [Stream(z2), Stream(g_rows)]
        + [Stream(a, first, part) for a in (z1,) + x_parts]
        + [*halos, *[Stream(a) for a in g_halos], coef, weight],
        [Result(part, 4, wide, chans), Result(part, 4, own, chans)]
        + [(part, wide, chans), (part, wide, chans), (8, chans), (part, 2, own, chans), (part, 2, own, chans)],
        conv_scratch(wide, chans) + [pltpu.VMEM((3, 8, chans), F32), pltpu.VMEM((4, STEP, own, chans), F32)],
        "conv_three",
    )


def slope_one(z, q, coef):
    center, inverse, scale = coef[0:1, :], coef[1:2, :], coef[2:3, :]
    mean_shift, mean_gain = coef[3:4, :], coef[4:5, :]
    active, slope = silu_and_slope(z)
    return scale * (q - mean_shift - (active - center) * inverse * mean_gain) * slope


def fourth_kernel(
    flow, s_ref, dh, z1, z_north, z_south, g_rows, pair, following, coef, weight,
    home, other, pad, high, low, weight_high, weight_low, results,
):
    part, _, wide, _ = dh.shape
    own = wide - 8
    put_weight(weight, True, weight_high, weight_low)

    def step(at, i):
        north, south = north_south(s_ref, pair, following, at)
        for row in range(6):
            if row in (0, 5):
                z, q = (z_north[at], north) if row == 0 else (z_south[at], south)
            else:
                z, q = z1[at, row - 1], dh[at, row - 1]
            dz = slope_one(z, q, coef)
            if row in (0, 5):
                dz = jnp.where(s_ref[3 if row == 0 else 4] == 1, 0.0, dz)
            ring_row(dz, pad, row, high, low)
        row = 0
        for two in range(2):
            for total in pair_of_rows(two, high, low, weight_high, weight_low):
                results[row] = g_rows[at, row, :own] + total.reshape(-1, wide, total.shape[-1])[:, :own]
                row += 1
        put_pieces(s_ref, results, home, other, at)

    flow.steps(part, step)


def fourth_conv(scalars, dh, halos, z1, z_halos, g_rows, coef, weight, chunk):
    part, _, wide, chans = dh.shape
    own = wide - 8
    return call(
        fourth_kernel,
        scalars,
        [Stream(dh)]
        + [Stream(a, chunk * part, part) for a in (z1,) + z_halos]
        + [Stream(g_rows), *[Stream(a) for a in halos], coef, weight],
        [(part, 2, own, chans)] * 2,
        conv_scratch(wide, chans) + [pltpu.VMEM((4, STEP, own, chans), F32)],
        "conv_four",
    )


def weight_step(rows, slopes, pad, high, low, total):
    own, chans = slopes[0].shape[1], slopes[0].shape[2]
    wide = own + 8
    for row, values in enumerate(rows):
        pad[row, :, 8 : 8 + wide, :] = values
        pad[row, :, 0:8, :] = values[:, own:wide]
        for tap in range(3):
            shifted = values[:, :own] if tap == 1 else pad[row, :, 7 + tap : 7 + tap + own, :]
            at = (row * 3 + tap) * chans
            high[:, at : at + chans], low[:, at : at + chans] = split(shifted.reshape(-1, chans))

    def product(left, right):
        return lax.dot_general(left, right, (((0,), (0,)), ((), ())), preferred_element_type=F32)

    sums = None
    for two in range(2):
        at = slice(two * 6 * chans, (two * 6 + 12) * chans)
        slope = jnp.concatenate([s.reshape(-1, chans) for s in slopes[2 * two : 2 * two + 2]], axis=1)
        slope_high, slope_low = split(slope)
        both = product(high[:, at], jnp.concatenate([slope_high, slope_low], axis=1))
        part = both[:, : 2 * chans] + both[:, 2 * chans :]
        part += product(low[:, at], slope_high)
        sums = part if sums is None else sums + part
    total[...] += sums


SMALL = 32


def weight_end(out_ref, total, small, bias):
    chans = out_ref.shape[1]
    line = 3 * chans
    for row in range(3):
        out_ref[row * line : (row + 1) * line, :] = (
            total[row * line : (row + 1) * line, :chans] + total[(row + 1) * line : (row + 2) * line, chans:]
        )
    out_ref[3 * line :, :] = jnp.zeros((SMALL, chans), F32)
    out_ref[3 * line : 3 * line + 8, :] = small[...]
    if bias is not None:
        out_ref[3 * line : 3 * line + 1, :] = fold(bias[...])


def weight_scratch(own, chans):
    return [
        pltpu.VMEM((6, STEP, own + 16, chans), F32),
        pltpu.VMEM((STEP * own, 18 * chans), BF16),
        pltpu.VMEM((STEP * own, 18 * chans), BF16),
        pltpu.VMEM((12 * chans, 2 * chans), F32),
    ]


def weight_two_kernel(flow, s_ref, *refs):
    chunks = [refs[4 * chunk : 4 * chunk + 4] for chunk in range(CHUNKS)]
    coef, small, out_ref, *scratch = refs[4 * CHUNKS :]
    scratch[-1][...] = jnp.zeros_like(scratch[-1])
    for chunk, (z1, north, south, dz) in enumerate(chunks):

        def step(at, i):
            rows = [hidden_row(s_ref, z1, north, south, coef, at, at, row) for row in range(6)]
            weight_step(rows, [dz[at, row] for row in range(4)], *scratch)

        flow.steps(dz.shape[0], step, chunk)
    weight_end(out_ref, scratch[-1], small, None)


def weight_two_grad(scalars, z1, halos, coef, dz, small):
    part, _, own, chans = dz[0].shape
    streams = []
    for chunk in range(CHUNKS):
        streams += [Stream(a, chunk * part, part, chunk) for a in (z1,) + halos]
        streams += [Stream(dz[chunk], group=chunk)]
    return call(
        weight_two_kernel,
        scalars,
        streams + [coef, small],
        [(9 * chans + SMALL, chans)],
        weight_scratch(own, chans),
        "weight_two",
    )[0]


def weight_one_kernel(flow, s_ref, *refs):
    chunks = [refs[6 * chunk : 6 * chunk + 6] for chunk in range(CHUNKS)]
    coef, small, out_ref, bias, *scratch = refs[6 * CHUNKS :]
    bias[...] = jnp.zeros_like(bias)
    scratch[-1][...] = jnp.zeros_like(scratch[-1])
    for chunk, (edge, inner, pair, following, z1, dh) in enumerate(chunks):
        part, _, wide, _ = dh.shape
        own = wide - 8

        def step(at, i):
            north, south = north_south(s_ref, pair, following, at)
            rows = [north] + [row_of_parts((edge, inner), row, at) for row in range(4)] + [south]
            slopes = [slope_one(z1[at, row, :own], dh[at, row, :own], coef) for row in range(4)]
            for slope in slopes:
                bias[...] += lanes(slope)
            weight_step(rows, slopes, *scratch)

        flow.steps(part, step, chunk)
    weight_end(out_ref, scratch[-1], small, bias)


def weight_one_grad(scalars, parts, halos, dh, z1, coef, small):
    part, _, wide, chans = dh[0].shape
    streams = []
    for chunk in range(CHUNKS):
        streams += [Stream(a, chunk * part, part, chunk) for a in parts + halos + (z1,)]
        streams += [Stream(dh[chunk], group=chunk)]
    return call(
        weight_one_kernel,
        scalars,
        streams + [coef, small],
        [(9 * chans + SMALL, chans)],
        [pltpu.VMEM((8, chans), F32)] + weight_scratch(wide - 8, chans),
        "weight_one",
    )[0]


def rows_of(*vectors):
    filled = [jnp.reshape(v, (1, -1)) for v in vectors]
    if len(filled) < 8:
        filled.append(jnp.zeros((8 - len(filled), filled[0].shape[1]), F32))
    return jnp.concatenate(filled, axis=0)


def merge_moments(one, other, count):
    mean = 0.5 * (one[0] + other[0])
    gap = one[0] - other[0]
    squares = one[1] + other[1] + gap * gap * (0.5 * count)
    weight = one[2] + other[2]
    product = (one[3] + (one[0] - mean) * one[2]) + (other[3] + (other[0] - mean) * other[2])
    return rows_of(mean, squares, weight, product)


def all_moments(stats, here, *others):
    count = here
    partial = []
    for target in group_steps():
        stats = merge_moments(stats, permute(stats, target), count)
        if not partial and others:
            stats = after(stats, *others)
        partial.append(stats)
        count = 2.0 * count
    return partial


def all_sums(stats, *others):
    partial = []
    for target in group_steps():
        stats = stats + permute(stats, target)
        if not partial and others:
            stats = after(stats, *others)
        partial.append(stats)
    return partial


def quarters_kernel(flow, s_ref, value, own, *others):
    size = own.shape[0]
    here = 2 * s_ref[5] + s_ref[2]
    for bits, ref in zip((0, 2, 1, 3), (own,) + others):
        ref[...] = value[pl.ds(pl.multiple_of((here ^ bits) * size, 8), size), :]


def whole_kernel(flow, s_ref, own, *refs):
    others, out = refs[:-1], refs[-1]
    size = own.shape[0]
    here = 2 * s_ref[5] + s_ref[2]
    for bits, ref in zip((0, 2, 1, 3), (own,) + others):
        out[pl.ds(pl.multiple_of((here ^ bits) * size, 8), size), :] = ref[...]


def to_east_pair(row, col):
    return row ^ 2, col ^ 2


def sum_everywhere(scalars, one, two, lon, beside):
    west = lon % 2 == 0
    value = jnp.where(west, one, two) + permute(after(jnp.where(west, two, one), *beside[0]), to_core)
    size, chans = value.shape[0] // 4, value.shape[1]
    targets = (to_east, to_pair, to_east_pair)
    own, *others = call(quarters_kernel, scalars, [value], [(size, chans)] * 4, [], "quarters")
    others = [permute(v, target) for v, target in zip(others, targets)]
    own = after(own, *beside[1])
    own = (own + others[0]) + (others[1] + others[2])
    own = own + permute(own, to_side)
    last = beside[2](own)
    for target in group_steps()[2:]:
        own = own + permute(own, target)
    others = [permute(own, target) for target in targets]
    value = call(whole_kernel, scalars, [after(own, last, *beside[3]), *others], [(4 * size, chans)], [], "whole")[0]
    other = permute(value, to_core)
    return value, other


def shards(
    fields, weight_one, bias_one, gain_one, shift_one, weight_two, bias_two, gain_two, shift_two, cotangent
):
    parts_here, batch, rows_here, cols_here, chans = fields.shape
    lat, lon = lax.axis_index("lat"), lax.axis_index("lon")
    lats, lons = lax.axis_size("lat"), lax.axis_size("lon")
    assert (parts_here, rows_here, lons) == (4, 2, 4)
    here = float(batch * 4 * 2 * cols_here)
    members = float(lats * lons // 4)
    count = here * members
    pair = lat // 2
    scalars = jnp.stack([lat % 2, lon % 2, pair % 2, pair == 0, pair == lats // 2 - 1, lon // 2]).astype(jnp.int32)
    cells = fields.reshape((2, 2) + fields.shape[1:])
    slopes = cotangent.reshape((2, 2) + cotangent.shape[1:])
    taps_one = weight_one.reshape((9, chans, chans))
    taps_two = weight_two.reshape((9, chans, chans))

    other = pack(scalars, cells, True, "x_pack_other")
    core = permute(other, to_core)
    own = pack(scalars, after(cells, other), False, "x_pack_own")
    home, edge, inner, tiles, other_tiles = rows(scalars, own, core, "x_rows")
    edge = permute(edge, to_side)
    tiles = permute(tiles, to_east)
    foreign_tiles = permute(other_tiles, to_east_side)
    inner = permute(after(inner, foreign_tiles), to_side)
    x_edge, pair_row, next_row = join(scalars, home, edge, tiles, foreign_tiles, True, "x_edge")
    x_halos = exchange_rows(pair_row, next_row)
    slopes = after(slopes, x_edge)
    other = pack(scalars, slopes, True, "g_pack_other")
    core = permute(other, to_core)
    own = pack(scalars, after(slopes, other), False, "g_pack_own")
    g_home, g_tiles, g_other, *g_foreign = chunk_rows(scalars, own, core, "g_rows")
    g_foreign = [permute(part, to_side) for part in g_foreign]
    g_tiles = (permute(g_tiles, to_east), permute(g_other, to_east_side))
    x_inner, pair_row, next_row = join(scalars, after(home, g_home), inner, tiles, foreign_tiles, False, "x_inner")
    x_far = exchange_rows(pair_row, next_row)
    x_parts = (x_edge, x_inner)

    z1, stats = first_conv(scalars, x_parts, x_halos, taps_one, after(rows_of(bias_one), g_home))
    partial = all_moments(stats, here, *x_far, g_foreign[0])
    z1_halos = tuple(
        first_halo_conv(scalars, after(x_edge, partial[-2]), x_halos, x_far, taps_one, rows_of(bias_one))
    )
    g_rows, g_edges = [], []
    for chunk in range(CHUNKS):
        foreign = after(g_foreign[chunk], z1_halos[0])
        four, pair_row, next_row = cell_rows(scalars, g_home, foreign, g_tiles, chunk, "g_cell")
        g_rows.append(four)
        g_edges.append((pair_row, next_row))
    stats = partial[-1]
    center_one, spread_one = stats[0], stats[1] / count
    inv_one = lax.rsqrt(spread_one + EPSILON)

    coef_one = rows_of(center_one, gain_one * inv_one, shift_one)
    g_halos = [exchange_rows(after(top, coef_one), bottom) for top, bottom in g_edges]
    z2, z2_edges, parts, earlier = [], [], [], []
    for chunk in range(CHUNKS):
        z, pair_row, next_row, stats = second_conv(
            scalars, z1, z1_halos, g_rows[chunk], after(coef_one, *earlier), taps_two, rows_of(bias_two), chunk
        )
        earlier = [z, *g_halos[0]]
        z2.append(z)
        z2_edges.append((pair_row, next_row))
        parts.append(stats)
    z2_halos = [exchange_rows(*z2_edges[0])]
    stats = after(merge_moments(parts[0], parts[1], here / CHUNKS), *g_halos[1])
    partial = all_moments(stats, here, *z2_halos[0])
    z2_halos.append(exchange_rows(after(z2_edges[1][0], partial[-2]), z2_edges[1][1]))
    stats = partial[-1]
    center_two, spread_two, dshift_two = stats[0], stats[1] / count, stats[2]
    inv_two = lax.rsqrt(spread_two + EPSILON)
    dgain_two = stats[3] * inv_two

    coef = rows_of(
        center_two, inv_two, gain_two * inv_two, dshift_two / count, dgain_two / count, center_one, inv_one,
        shift_two,
    )
    dh1, dz2, dh1_edges, parts, output = [], [], [], [], []
    for chunk in range(CHUNKS):
        dh, dz, pair_row, next_row, stats, *pieces = third_conv(
            scalars, z2[chunk], z2_halos[chunk], g_rows[chunk], g_halos[chunk], z1, x_parts, after(coef, *dh1),
            taps_two, chunk,
        )
        dh1.append(dh)
        dz2.append(dz)
        dh1_edges.append((pair_row, next_row))
        parts.append(stats)
        output.append(send_side(*pieces))
    stats = parts[0] + parts[1]
    dbias_two = stats[2]
    dh1_halos = [exchange_rows(*dh1_edges[0])]
    partial = all_sums(stats, *dh1_halos[0])
    dh1_halos.append(exchange_rows(after(dh1_edges[1][0], partial[-2]), dh1_edges[1][1]))
    small = rows_of(dbias_two, dgain_two / members, dshift_two / members)
    grad_w2 = weight_two_grad(scalars, z1, z1_halos, after(coef_one, partial[-2]), dz2, small)
    dshift_one, dgain_one = partial[-1][0], partial[-1][1]

    coef = rows_of(center_one, inv_one, gain_one * inv_one, dshift_one / count, dgain_one / count)
    small = rows_of(jnp.zeros_like(dgain_one), dgain_one / members, dshift_one / members)

    def input_slope(chunk, coef):
        return fourth_conv(
            scalars, dh1[chunk], dh1_halos[chunk], z1, z1_halos, g_rows[chunk], coef, taps_one, chunk
        )

    pieces = input_slope(0, after(coef, grad_w2, output[0][1], output[1][1], *dh1_halos[1]))
    grad_w1 = weight_one_grad(scalars, x_parts, x_halos, dh1, z1, after(coef, pieces[0]), small)
    input_grad = [send_side(*pieces)]
    pieces = input_slope(1, after(coef, grad_w1))
    out_whole = None
    for chunk in range(CHUNKS):
        out_whole = place(scalars, send_core(scalars, *output[chunk], "output_halves"), chunk, out_whole, "output_place")
    def send_last(summed):
        input_grad.append(send_side(pieces[0], after(pieces[1], summed)))
        return input_grad[1][1]

    grad_whole = place(scalars, send_core(scalars, *input_grad[0], "grad_halves"), 0, None, "grad_place")
    beside = ([input_grad[0][1]], pieces[:1], send_last, [out_whole, grad_whole])
    one, two = sum_everywhere(scalars, grad_w1, grad_w2, lon, beside)
    many, west = 9 * chans, lon % 2 == 0
    sums = []
    for mine, its in ((one, two), (two, one)):
        sums.append(jnp.where(west, mine[:many], its[:many]))
        sums += [jnp.where(west, mine[many + row], its[many + row]) for row in range(3)]
    home, grad_whole = lax.optimization_barrier((input_grad[1][0], grad_whole))
    pieces = send_core(scalars, home, input_grad[1][1], "grad_halves")
    home, *sums = lax.optimization_barrier((home, *sums))
    pieces = (home,) + pieces[1:]
    grad_whole = place(scalars, pieces, 1, grad_whole, "grad_place")
    return (
        out_whole.reshape(fields.shape),
        grad_whole.reshape(fields.shape),
        sums[0].reshape(weight_one.shape),
        *sums[1:4],
        sums[4].reshape(weight_two.shape),
        *sums[5:8],
    )


def solution(mesh):
    field = P(None, None, "lat", "lon", None)
    return jax.shard_map(
        shards,
        mesh=mesh,
        in_specs=(field,) + (P(),) * 8 + (field,),
        out_specs=(field, field) + (P(),) * 8,
        check_vma=False,
    )
```
